256 devices in a mesh: row: 32 (over z, x), col: 8 (over y, core).
Axes of the slice: x: 4, y: 4, z: 8, core: 2. Of those that a mesh axis runs over, the one named last changes fastest.
Arguments:
- noise: bfloat16 [8192, 4096], P('row', 'col'), may hold values from -6 to 6
- data: bfloat16 [8192, 4096], P('col', 'row'), may hold values from -6 to 6
Outputs:
- potential_noise: float32 [8192], P('row')
- potential_data: float32 [8192], P('col')
- velocity: bfloat16 [8192, 4096], P('row', 'col')
The draws below stay inside these ranges and needn't reach their ends.
All inputs are finite; a program needn't handle non-finite values.
Results may differ from the reference program's by a relative error of at most 0.0075.
Values may be sent and summed in bfloat16 or wider, within the bound.
No kernel may reach another device: no remote copies, remote signals or barrier semaphores. Data moves between devices by JAX's collectives and lax.ppermute only.
A program may use at most 64 MiB of HBM per device.

```python
import jax
import jax.numpy as jnp

D = 4096
ITERS = 3
NOISE = 8192
SAMPLES = 8192


def shared_latents(key):
    return jnp.clip(jax.random.normal(key, (NOISE, D), jnp.float32), -6.0, 6.0)


def draw_noise(key, part):
    return shared_latents(key).astype(jnp.bfloat16)


def draw_data(key, part):
    key = jax.random.fold_in(key, 11)
    fresh = jnp.clip(jax.random.normal(key, (SAMPLES, D), jnp.float32), -6.0, 6.0)
    return fresh.astype(jnp.bfloat16)


def setup_inputs(seed: int = 0) -> dict:
    streams_of = jax.random.split(jax.random.key(seed), 3)
    noise = draw_noise(jax.random.fold_in(streams_of[2], 71), 0)
    data = draw_data(jax.random.fold_in(streams_of[2], 71), 0)
    return dict(noise=noise, data=data)


eps_scale = 0.01


def reference(noise, data):
    first = noise.astype(jnp.float32)
    second = data.astype(jnp.float32)
    gram = jnp.dot(noise, data.T, preferred_element_type=jnp.float32)
    cost = (jnp.sum(first * first, axis=1)[:, None] + jnp.sum(second * second, axis=1)[None, :] - 2.0 * gram) / D
    pot_f = jnp.zeros((NOISE,), jnp.float32)
    pot_g = jnp.zeros((SAMPLES,), jnp.float32)
    for step in range(ITERS):
        pot_f = -eps_scale * jnp.log(jnp.float32(NOISE)) - eps_scale * jax.nn.logsumexp((pot_g[None, :] - cost) / eps_scale, axis=1)
        pot_g = -eps_scale * jnp.log(jnp.float32(SAMPLES)) - eps_scale * jax.nn.logsumexp((pot_f[:, None] - cost) / eps_scale, axis=0)
    weights = (NOISE * jnp.exp((pot_f[:, None] + pot_g[None, :] - cost) / eps_scale)).astype(jnp.bfloat16)
    target = jnp.dot(weights, data, preferred_element_type=jnp.float32)
    velocity = (target - first).astype(jnp.bfloat16)
    return pot_f, pot_g, velocity
```

```python
import jax
import jax.numpy as jnp
from jax import lax
from jax.sharding import Mesh, PartitionSpec as P

ITERS = 3
EPS = 0.01


def shift(x, axis, by):
    n = lax.axis_size(axis)
    return lax.ppermute(x, axis, [(j, (j + by) % n) for j in range(n)])


def merge(parts):
    top = parts[0]
    for part in parts[1:]:
        top = jnp.maximum(top, part)
    total = sum(jnp.exp(part - top) for part in parts)
    return top + jnp.log(total)


def merge_along(lse, axis):
    return merge([lse] + [shift(lse, axis, by) for by in range(1, lax.axis_size(axis))])


def local_lse(scores, axis):
    peak = jnp.max(scores, axis=axis, keepdims=True)
    total = jnp.sum(jnp.exp(scores - peak), axis=axis)
    return jnp.squeeze(peak, axis) + jnp.log(total)


def noise_lse(scores):
    return merge_along(merge_along(local_lse(scores, 1), "core"), "y")


def data_lse(scores):
    mine = local_lse(scores, 0)
    n = lax.axis_size("z") * lax.axis_size("x")
    parts = lax.all_to_all(jnp.broadcast_to(mine[None], (n, mine.shape[0])), ("z", "x"), 0, 0)
    top = jnp.max(parts, axis=0)
    return top + jnp.log(jnp.sum(jnp.exp(parts - top[None]), axis=0))


def body(noise, data):
    width = noise.shape[1] * 8
    data_full = lax.all_gather(data, ("z", "x"), axis=1, tiled=True)
    noise_full = lax.all_gather(noise, ("y", "core"), axis=1, tiled=True)
    wide = data_full.astype(jnp.float32)
    flat = noise_full.astype(jnp.float32)
    sq_data = jnp.sum(wide * wide, axis=1)
    sq_noise = jnp.sum(flat * flat, axis=1)
    gram = lax.dot_general(
        noise_full, data_full, (((1,), (1,)), ((), ())), preferred_element_type=jnp.float32
    )
    cost = (sq_noise[:, None] + sq_data[None, :] - 2.0 * gram) / width
    noise_total = noise.shape[0] * 32
    data_total = data.shape[0] * 8
    pot_g = jnp.zeros((data.shape[0],), jnp.float32)
    for _ in range(ITERS):
        pot_f = -EPS * jnp.log(jnp.float32(noise_total)) - EPS * noise_lse((pot_g[None, :] - cost) / EPS)
        pot_g = -EPS * jnp.log(jnp.float32(data_total)) - EPS * data_lse((pot_f[:, None] - cost) / EPS)
    weights = (noise_total * jnp.exp((pot_f[:, None] + pot_g[None, :] - cost) / EPS)).astype(jnp.bfloat16)
    partial = jnp.dot(weights, data_full, preferred_element_type=jnp.float32)
    rows, share = noise.shape
    partial = partial.reshape(rows, 4, 2, share)
    core = lax.axis_index("core")
    keep = lax.dynamic_index_in_dim(partial, core, 2, keepdims=False)
    give = lax.dynamic_index_in_dim(partial, 1 - core, 2, keepdims=False).astype(jnp.bfloat16)
    pair = keep + shift(give, "core", 1).astype(jnp.float32)
    y = lax.axis_index("y")
    target = lax.dynamic_index_in_dim(pair, y, 1, keepdims=False)
    for by in range(1, 4):
        part = lax.dynamic_index_in_dim(pair, lax.rem(y + by, 4), 1, keepdims=False)
        target = target + shift(part.astype(jnp.bfloat16), "y", by).astype(jnp.float32)
    velocity = (target - noise.astype(jnp.float32)).astype(jnp.bfloat16)
    return pot_f, pot_g, velocity


def solution(mesh):
    fine = Mesh(mesh.devices.reshape(8, 4, 4, 2), ("z", "x", "y", "core"))
    row, col = ("z", "x"), ("y", "core")
    return jax.shard_map(
        body,
        mesh=fine,
        in_specs=(P(row, col), P(col, row)),
        out_specs=(P(row), P(col), P(row, col)),
        check_vma=False,
    )
```

```python
import functools
import math

import jax
import jax.numpy as jnp
from jax import lax
from jax.experimental import pallas as pl
from jax.experimental.pallas import tpu as pltpu
from jax.sharding import Mesh, PartitionSpec as P

ITERS = 3
EPS = 0.01
LOG2E = math.log2(math.e)
Z, X, Y, C = 8, 4, 4, 2
ROWS, SHARE = 256, 512
COUNT, SLICE = 1024, 128
WIDTH = 4096
PAIR = 2 * ROWS
HALF = COUNT // 2
TOTAL = 8192
UNIT = LOG2E / (WIDTH * EPS)
LOG2N = math.log2(TOTAL)
F32, BF16 = jnp.float32, jnp.bfloat16
VMEM = pl.BlockSpec(memory_space=pltpu.VMEM)
SMEM = pl.BlockSpec(memory_space=pltpu.SMEM)
ANY = pl.BlockSpec(memory_space=pl.ANY)


def shift(x, axis, by):
    n = {"z": Z, "x": X, "y": Y, "core": C}[axis]
    return lax.ppermute(x, axis, [(j, (j + by) % n) for j in range(n)])


def params(mib):
    return pltpu.CompilerParams(vmem_limit_bytes=mib * 2**20)


def ring(x, axis, steps):
    forward = backward = x
    got = [(0, x)]
    for s in range(1, steps):
        forward, backward = shift(forward, axis, 1), shift(backward, axis, -1)
        got += [(-s, forward), (s, backward)]
    cut = x.shape[0] // 2
    top = shift(forward[:cut], axis, 1)
    low = shift(backward[cut:], axis, -1)
    return got, top, low


def gather_noise(noise, z):
    other = lax.ppermute(noise, "z", [(j, j ^ 1) for j in range(Z)])
    odd = lax.rem(z, 2) == 1
    block = jnp.concatenate([jnp.where(odd, other, noise), jnp.where(odd, noise, other)], 0)
    got, top, low = ring(block, "y", 2)
    out = []
    for rel, part in got:
        out += [(rel, 0, 0, part), (rel, 1, 0, shift(part, "core", 1))]
    for row, part in ((0, top), (PAIR // 2, low)):
        out += [(2, 0, row, part), (2, 1, row, shift(part, "core", 1))]
    return out


def gather_data(data):
    out = []
    first, second = data[:HALF], data[HALF:]
    across = [(0, first), (-1, shift(first, "x", 1)), (1, shift(first, "x", -1)), (2, shift(first, "x", 2))]
    wide = jnp.concatenate([part for _, part in across], 1)
    got, top, low = ring(wide, "z", Z // 2)
    for lane, (rx, _) in enumerate(across):
        for rz, part in got:
            out.append((rz, rx, 0, 0, HALF, lane * SLICE, part))
        out.append((4, rx, 0, 0, HALF // 2, lane * SLICE, top))
        out.append((4, rx, HALF // 2, 0, HALF // 2, lane * SLICE, low))
    got, top, low = ring(second, "z", Z // 2)
    rows = COUNT - HALF
    for group in (got[:3], got[3:] + [(4, jnp.concatenate([top, low], 0))]):
        tall = jnp.concatenate([part for _, part in group], 0)
        right, left = shift(tall, "x", 1), shift(tall, "x", -1)
        cut = tall.shape[0] // 2
        far = ((0, shift(right[:cut], "x", 1)), (cut, shift(left[cut:], "x", -1)))
        for n, (rz, part) in enumerate(group):
            out.append((rz, 0, HALF, 0, rows, 0, part))
            out.append((rz, -1, HALF, n * rows, rows, 0, right))
            out.append((rz, 1, HALF, n * rows, rows, 0, left))
            for start, part2 in far:
                lo, hi = max(n * rows, start), min((n + 1) * rows, start + part2.shape[0])
                if lo < hi:
                    out.append((rz, 2, HALF + lo - n * rows, lo - start, hi - lo, 0, part2))
    return out


def prepare(data_parts, noise_parts, place):
    arrays, index = [], {}

    def number(a):
        if id(a) not in index:
            index[id(a)] = len(arrays)
            arrays.append(a)
        return index[id(a)]

    data_plan = [(number(p[-1]),) + tuple(p[:-1]) for p in data_parts]
    noise_plan = [(number(p[-1]),) + tuple(p[:-1]) + (p[-1].shape[0],) for p in noise_parts]
    n_in = len(arrays)
    n_copies = len(data_plan) + len(noise_plan) + 2

    def kernel(place_ref, *refs):
        ins = refs[:n_in]
        q_ref, sqn_ref, g0_ref, full_ref = refs[n_in : n_in + 4]
        data_ref, noise_ref, sems = refs[n_in + 4 :]
        z, x, y, c = place_ref[0], place_ref[1], place_ref[2], place_ref[3]
        early, late, k = [], [], 0
        for which, ry, rc, row, rows in noise_plan:
            piece = lax.rem(y + ry + Y, Y) * C + lax.rem(c + rc, C)
            lanes = pl.ds(pl.multiple_of(piece * SHARE, SHARE), SHARE)
            early.append(pltpu.make_async_copy(ins[which], noise_ref.at[pl.ds(row, rows), lanes], sems.at[k]))
            k += 1
        for which, rz, rx, sample, row, rows, lane in data_plan:
            piece = lax.rem(z + rz + Z, Z) * X + lax.rem(x + rx + X, X)
            lanes = pl.ds(pl.multiple_of(piece * SLICE, SLICE), SLICE)
            copy = pltpu.make_async_copy(
                ins[which].at[pl.ds(row, rows), pl.ds(lane, SLICE)],
                data_ref.at[pl.ds(sample, rows), lanes],
                sems.at[k],
            )
            (early if sample < HALF else late).append(copy)
            k += 1
        for copy in early + late:
            copy.start()
        for copy in early:
            copy.wait()
        out_copies = []
        step = 256
        for half in range(2):
            if half:
                for copy in late:
                    copy.wait()
            out = pltpu.make_async_copy(
                data_ref.at[pl.ds(half * HALF, HALF)], full_ref.at[pl.ds(half * HALF, HALF)], sems.at[k + half]
            )
            out.start()
            out_copies.append(out)
            for start in range(half * HALF, (half + 1) * HALF, step):
                block = data_ref[pl.ds(start, step), :]
                gram = lax.dot_general(noise_ref[...], block, (((1,), (1,)), ((), ())), preferred_element_type=F32)
                q_ref[:, pl.ds(start, step)] = gram * (2.0 * UNIT)
                total = jnp.zeros((step, 128), F32)
                for lane in range(0, WIDTH, 128):
                    part = data_ref[pl.ds(start, step), pl.ds(lane, 128)].astype(F32)
                    total = total + part * part
                sums = jnp.sum(jnp.transpose(total), axis=0, keepdims=True)
                g0_ref[:, pl.ds(start, step)] = sums
        for start in range(0, PAIR, step):
            total = jnp.zeros((step, 128), F32)
            for lane in range(0, WIDTH, 128):
                part = noise_ref[pl.ds(start, step), pl.ds(lane, 128)].astype(F32)
                total = total + part * part
            sqn_ref[:, pl.ds(start, step)] = jnp.sum(jnp.transpose(total), axis=0, keepdims=True)
        for copy in out_copies:
            copy.wait()

    return pl.pallas_call(
        kernel,
        out_shape=(
            jax.ShapeDtypeStruct((PAIR, COUNT), F32),
            jax.ShapeDtypeStruct((1, PAIR), F32),
            jax.ShapeDtypeStruct((1, COUNT), F32),
            jax.ShapeDtypeStruct((COUNT, WIDTH), BF16),
        ),
        in_specs=[SMEM] + [ANY] * n_in,
        out_specs=(VMEM, VMEM, VMEM, ANY),
        scratch_shapes=[
            pltpu.VMEM((COUNT, WIDTH), BF16),
            pltpu.VMEM((PAIR, WIDTH), BF16),
            pltpu.SemaphoreType.DMA((n_copies,)),
        ],
        compiler_params=params(40),
        name="prepare",
    )(place, *arrays)


def merged(parts):
    if len(parts) == 1:
        return parts[0]
    top = functools.reduce(jnp.maximum, parts)
    e = [jnp.exp2(part - top) for part in parts]
    total = e[0] + e[1] if len(parts) == 2 else (e[0] + e[1]) + (e[2] + e[3])
    return top + jnp.log2(total)


def rows_kernel(first, *refs):
    q_ref, part_refs, (out_ref, wide_ref) = refs[0], refs[1:-2], refs[-2:]
    if first:
        g = part_refs[0][...] * -UNIT
    else:
        g = -LOG2N - merged([ref[...] for ref in part_refs])
    step = 32

    @pl.loop(0, PAIR // step)
    def _(n):
        rows = pl.ds(pl.multiple_of(n * step, step), step)
        t = q_ref[rows, :] + g
        top = jnp.max(t, axis=1, keepdims=True)
        total = jnp.sum(jnp.exp2(t - top), axis=1, keepdims=True)
        wide_ref[rows, :] = jnp.broadcast_to(top + jnp.log2(total), (step, 128))

    out_ref[...] = jnp.transpose(wide_ref[...])[0:1, :]


def rows_lse(q, parts, first):
    return pl.pallas_call(
        functools.partial(rows_kernel, first),
        out_shape=jax.ShapeDtypeStruct((1, PAIR), F32),
        in_specs=[VMEM] * (1 + len(parts)),
        out_specs=VMEM,
        scratch_shapes=[pltpu.VMEM((PAIR, 128), F32)],
        compiler_params=params(16),
        name="rows",
    )(q, *parts)


def columns_kernel(*refs):
    q_ref, part_refs, (out_ref, f_ref, wide_ref) = refs[0], refs[1:-3], refs[-3:]
    f = -LOG2N - merged([ref[...] for ref in part_refs])
    f_ref[...] = f
    wide_ref[...] = jnp.transpose(jnp.broadcast_to(f, (128, PAIR)))

    @pl.loop(0, COUNT // 128)
    def _(n):
        lanes = pl.ds(pl.multiple_of(n * 128, 128), 128)
        t = q_ref[:, lanes] + wide_ref[...]
        top = jnp.max(t, axis=0, keepdims=True)
        total = jnp.sum(jnp.exp2(t - top), axis=0, keepdims=True)
        out_ref[:, lanes] = top + jnp.log2(total)


def columns_lse(q, parts):
    return pl.pallas_call(
        columns_kernel,
        out_shape=(jax.ShapeDtypeStruct((1, COUNT), F32), jax.ShapeDtypeStruct((1, PAIR), F32)),
        in_specs=[VMEM] * (1 + len(parts)),
        out_specs=(VMEM, VMEM),
        scratch_shapes=[pltpu.VMEM((PAIR, 128), F32)],
        compiler_params=params(16),
        name="columns",
    )(q, *parts)


def piece_of(place, s, mine):
    core = place[3] if mine else 1 - place[3]
    return lax.rem(place[2] + s, Y) * C + core


def give_kernel(place, q_ref, f_ref, p0, p1, p2, p3, data_ref, out_ref, w_ref, g_ref):
    @pl.when(pl.program_id(0) == 0)
    def _():
        g = -LOG2N - merged([p0[...], p1[...], p2[...], p3[...]])
        g_ref[...] = g
        f = jnp.transpose(jnp.broadcast_to(f_ref[...], (128, ROWS)))[:, 0:1]
        w_ref[...] = jnp.exp2(q_ref[...] + f + (g + LOG2N)).astype(BF16)

    out_ref[0] = jnp.dot(w_ref[...], data_ref[...], preferred_element_type=F32).astype(BF16)


def give(q, f, parts, data, place):
    whole = lambda s, place: (0, 0)
    own = lambda s, place: (lax.rem(place[0], 2), 0)
    own_f = lambda s, place: (0, lax.rem(place[0], 2))
    return pl.pallas_call(
        give_kernel,
        grid_spec=pltpu.PrefetchScalarGridSpec(
            num_scalar_prefetch=1,
            grid=(Y,),
            in_specs=[pl.BlockSpec((ROWS, COUNT), own), pl.BlockSpec((1, ROWS), own_f)]
            + [pl.BlockSpec((1, COUNT), whole)] * 4
            + [pl.BlockSpec((COUNT, SHARE), lambda s, place: (0, piece_of(place, s, False)))],
            out_specs=(
                pl.BlockSpec((1, ROWS, SHARE), lambda s, place: (s, 0, 0)),
                pl.BlockSpec((ROWS, COUNT), whole),
                pl.BlockSpec((1, COUNT), whole),
            ),
        ),
        out_shape=(
            jax.ShapeDtypeStruct((Y, ROWS, SHARE), BF16),
            jax.ShapeDtypeStruct((ROWS, COUNT), BF16),
            jax.ShapeDtypeStruct((1, COUNT), F32),
        ),
        compiler_params=params(24),
        name="give",
    )(place, q, f, *parts, data)


def keep_kernel(place, w_ref, data_ref, out_ref):
    out_ref[0] = jnp.dot(w_ref[...], data_ref[...], preferred_element_type=F32)


def keep(w, data, place):
    return pl.pallas_call(
        keep_kernel,
        grid_spec=pltpu.PrefetchScalarGridSpec(
            num_scalar_prefetch=1,
            grid=(Y,),
            in_specs=[
                pl.BlockSpec((ROWS, COUNT), lambda s, place: (0, 0)),
                pl.BlockSpec((COUNT, SHARE), lambda s, place: (0, piece_of(place, s, True))),
            ],
            out_specs=pl.BlockSpec((1, ROWS, SHARE), lambda s, place: (s, 0, 0)),
        ),
        out_shape=jax.ShapeDtypeStruct((Y, ROWS, SHARE), F32),
        compiler_params=params(24),
        cost_estimate=pl.CostEstimate(flops=2 * ROWS * COUNT * WIDTH // 2, bytes_accessed=8 * 2**20, transcendentals=0),
        name="keep",
    )(place, w, data)


def four(v, axis):
    return [v, shift(v, axis, 2), shift(v, axis, 1), shift(v, axis, -1)]


def z_pairs(v):
    near = [(j, (j + (1 if j % 2 else -1)) % Z) for j in range(Z)]
    two = [(j, (j + (2 if j % 2 else -2)) % Z) for j in range(Z)]
    far = [(j, (j + (3 if j % 2 else -3)) % Z) for j in range(Z)]
    return [v, lax.ppermute(v, "z", far), lax.ppermute(v, "z", two), lax.ppermute(v, "z", near)]


def body(noise, data):
    z, x, y, c = (lax.axis_index(a) for a in ("z", "x", "y", "core"))
    place = jnp.stack([z, x, y, c]).astype(jnp.int32)
    data_parts = gather_data(data)
    noise_parts = gather_noise(noise, z)
    q, sq_noise, sq_data, data_full = prepare(data_parts, noise_parts, place)
    parts, first = [sq_data], True
    for _ in range(ITERS):
        rows = rows_lse(q, parts, first)
        rows = merged([rows, shift(rows, "core", 1)])
        columns, f = columns_lse(q, four(rows, "y"))
        parts, first = z_pairs(merged(four(columns, "x"))), False
    give_parts, w, g = give(q, f, parts, data_full, place)
    got = shift(give_parts, "core", 1)
    mine = keep(w, data_full, place)
    both = mine + got.astype(F32)
    target = both[0]
    for by in (2, 1, 3):
        target = target + shift(both[by].astype(BF16), "y", by).astype(F32)
    velocity = (target - noise.astype(F32)).astype(BF16)
    own = lax.rem(z, 2) * ROWS
    f = lax.dynamic_slice_in_dim(f[0], own, ROWS, 0)
    sq_noise = lax.dynamic_slice_in_dim(sq_noise[0], own, ROWS, 0)
    pot_f = f * (EPS / LOG2E) + sq_noise / WIDTH
    pot_g = g[0] * (EPS / LOG2E) + sq_data[0] / WIDTH
    return pot_f, pot_g, velocity


def solution(mesh):
    fine = Mesh(mesh.devices.reshape(Z, X, Y, C), ("z", "x", "y", "core"))
    row, col = ("z", "x"), ("y", "core")
    return jax.shard_map(
        body,
        mesh=fine,
        in_specs=(P(row, col), P(col, row)),
        out_specs=(P(row), P(col), P(row, col)),
        check_vma=False,
    )
```

```python
import functools
import math

import jax
import jax.numpy as jnp
from jax import lax
from jax.experimental import pallas as pl
from jax.experimental.pallas import tpu as pltpu
from jax.sharding import Mesh, PartitionSpec as P

ITERS = 3
EPS = 0.01
LOG2E = math.log2(math.e)
Z, X, Y, C = 8, 4, 4, 2
ROWS, SHARE = 256, 512
COUNT, SLICE = 1024, 128
WIDTH = 4096
QUARTER = COUNT // X
TALL = ROWS * X
CHUNKS = TALL // 128
GROUP = X * Y * C
TOTAL = 8192
UNIT = LOG2E / (WIDTH * EPS)
LOG2N = math.log2(TOTAL)
F32, BF16 = jnp.float32, jnp.bfloat16
VMEM = pl.BlockSpec(memory_space=pltpu.VMEM)
SMEM = pl.BlockSpec(memory_space=pltpu.SMEM)


def shift(x, axis, by):
    n = {"z": Z, "x": X, "y": Y, "core": C}[axis]
    return lax.ppermute(x, axis, [(j, (j + by) % n) for j in range(n)])


def params(mib):
    return pltpu.CompilerParams(vmem_limit_bytes=mib * 2**20)


def ring_z(x):
    forward = backward = x
    got = [x]
    for _ in range(1, Z // 2):
        forward, backward = shift(forward, "z", 1), shift(backward, "z", -1)
        got += [forward, backward]
    cut = x.shape[0] // 2
    return got + [shift(forward[:cut], "z", 1), shift(backward[cut:], "z", -1)]


def squares(ref, pieces):
    total = None
    for view in pieces:
        part = ref[view].astype(F32)
        total = part * part if total is None else total + part * part
    return total


def assemble_kernel(place, *refs):
    ins, (out_ref, sq_ref) = refs[:-2], refs[-2:]
    z = place[0]
    plan = [(0, 0)] + [(r, 0) for s in range(1, Z // 2) for r in (-s, s)] + [(Z // 2, 0), (Z // 2, X // 2)]
    for ref, (rel, first) in zip(ins, plan, strict=True):
        piece = lax.rem(z + rel + Z, Z)
        for n in range(ref.shape[0]):
            lanes = pl.ds(pl.multiple_of(piece * SHARE + (first + n) * SLICE, SLICE), SLICE)
            out_ref[:, lanes] = ref[n]
    step = 64
    for start in range(0, QUARTER, step):
        rows = pl.ds(start, step)
        total = squares(out_ref, [(rows, pl.ds(lane, 128)) for lane in range(0, WIDTH, 128)])
        sq_ref[rows, :] = jnp.broadcast_to(jnp.sum(total, axis=1, keepdims=True), (step, 128))


def assemble(place, parts):
    return pl.pallas_call(
        assemble_kernel,
        out_shape=(jax.ShapeDtypeStruct((QUARTER, WIDTH), BF16), jax.ShapeDtypeStruct((QUARTER, 128), F32)),
        in_specs=[SMEM] + [VMEM] * len(parts),
        out_specs=(VMEM, VMEM),
        compiler_params=params(16),
        cost_estimate=pl.CostEstimate(flops=2 * QUARTER * WIDTH, bytes_accessed=4 * 2**20, transcendentals=0),
        name="assemble",
    )(place, *parts)


def lse(t, axis):
    top = jnp.max(t, axis=axis, keepdims=True)
    return top + jnp.log2(jnp.sum(jnp.exp2(t - top), axis=axis, keepdims=True))


def merged(ref):
    parts = ref[...]
    top = jnp.max(parts, axis=0)
    return top + jnp.log2(jnp.sum(jnp.exp2(parts - top[None]), axis=0))


def chunk(r):
    return pl.ds(r * 128, 128)


def score_kernel(place, data_ref, sq_ref, noise_ref, q_ref, out_ref, sqn_ref, lse_ref):
    n = pl.program_id(0)
    gram = jnp.zeros((QUARTER, ROWS), F32)
    for p in range(Y * C):
        gram = gram + lax.dot_general(
            data_ref[:, pl.ds(p * SHARE, SHARE)], noise_ref[0, p], (((1,), (1,)), ((), ())), preferred_element_type=F32
        )
    gram = gram * (2.0 * UNIT)
    q_ref[:, pl.ds(pl.multiple_of(n * ROWS, ROWS), ROWS)] = gram
    t = gram - UNIT * jnp.concatenate([sq_ref[...]] * 2, axis=1)
    rows = lse(t, 0)
    lse_ref[pl.ds(2 * n, 1), :] = rows[:, :128]
    lse_ref[pl.ds(2 * n + 1, 1), :] = rows[:, 128:]

    @pl.when(n == place[1])
    def _():
        views = [(0, p, slice(None), pl.ds(lane, 128)) for p in range(Y * C) for lane in range(0, SHARE, 128)]
        total = squares(noise_ref, views)
        sqn_ref[...] = jnp.sum(jnp.transpose(total), axis=0, keepdims=True)

    @pl.when(n == X - 1)
    def _():
        out_ref[...] = jnp.broadcast_to(lse_ref[...][None], (GROUP, CHUNKS, 128))


def score(place, data, sq, noise):
    whole = lambda n, place: (0, 0)
    return pl.pallas_call(
        score_kernel,
        grid_spec=pltpu.PrefetchScalarGridSpec(
            num_scalar_prefetch=1,
            grid=(X,),
            in_specs=[
                pl.BlockSpec((QUARTER, WIDTH), whole),
                pl.BlockSpec((QUARTER, 128), whole),
                pl.BlockSpec((1, Y * C, ROWS, SHARE), lambda n, place: (n, 0, 0, 0)),
            ],
            out_specs=(
                pl.BlockSpec((QUARTER, TALL), whole),
                pl.BlockSpec((GROUP, CHUNKS, 128), lambda n, place: (0, 0, 0)),
                pl.BlockSpec((1, ROWS), whole),
            ),
            scratch_shapes=[pltpu.VMEM((CHUNKS, 128), F32)],
        ),
        out_shape=(
            jax.ShapeDtypeStruct((QUARTER, TALL), F32),
            jax.ShapeDtypeStruct((GROUP, CHUNKS, 128), F32),
            jax.ShapeDtypeStruct((1, ROWS), F32),
        ),
        compiler_params=params(58),
        name="score",
    )(place, data, sq, noise)


def to_column(g):
    return jnp.concatenate([jnp.transpose(jnp.broadcast_to(g[r : r + 1], (128, 128))) for r in range(2)], axis=0)


def noise_kernel(q_ref, part_ref, out_ref, lse_ref, g_ref):
    g_ref[...] = to_column(-LOG2N - merged(part_ref))
    for r in range(CHUNKS):
        lse_ref[pl.ds(r, 1), :] = lse(q_ref[:, chunk(r)] + g_ref[...], 0)
    out_ref[...] = jnp.broadcast_to(lse_ref[...][None], (GROUP, CHUNKS, 128))


def noise_lse(q, parts):
    return pl.pallas_call(
        noise_kernel,
        out_shape=jax.ShapeDtypeStruct((GROUP, CHUNKS, 128), F32),
        in_specs=[VMEM] * 2,
        out_specs=VMEM,
        scratch_shapes=[pltpu.VMEM((CHUNKS, 128), F32), pltpu.VMEM((QUARTER, 128), F32)],
        compiler_params=params(16),
        name="noise_lse",
    )(q, parts)


def data_kernel(q_ref, part_ref, out_ref, f_ref, lane_ref):
    f_ref[...] = -LOG2N - merged(part_ref)
    step = 32
    for start in range(0, QUARTER, step):
        rows = pl.ds(start, step)
        t = [q_ref[rows, chunk(r)] + f_ref[pl.ds(r, 1), :] for r in range(CHUNKS)]
        top = functools.reduce(jnp.maximum, t)
        lane_ref[rows, :] = top + jnp.log2(sum(jnp.exp2(part - top) for part in t))
    row = lse(jnp.transpose(lane_ref[...]), 0)
    tile = jnp.concatenate([row[:, :128], row[:, 128:], jnp.zeros((6, 128), F32)], axis=0)
    out_ref[...] = jnp.broadcast_to(tile[None], (Z, 8, 128))


def data_lse(q, parts):
    return pl.pallas_call(
        data_kernel,
        out_shape=(jax.ShapeDtypeStruct((Z, 8, 128), F32), jax.ShapeDtypeStruct((CHUNKS, 128), F32)),
        in_specs=[VMEM] * 2,
        out_specs=(VMEM, VMEM),
        scratch_shapes=[pltpu.VMEM((QUARTER, 128), F32)],
        compiler_params=params(16),
        name="data_lse",
    )(q, parts)


def weights_kernel(q_ref, f_ref, part_ref, sq_ref, w_ref, pot_ref):
    g = -LOG2N - merged(part_ref)
    column = to_column(g) + LOG2N
    for r in range(CHUNKS):
        w = jnp.exp2((q_ref[:, chunk(r)] + f_ref[pl.ds(r, 1), :]) + column)
        w_ref[r // 2, pl.ds(r % 2 * 128, 128), :] = jnp.transpose(w).astype(BF16)
    row = jnp.concatenate([g[0:1], g[1:2]], axis=1)
    pot_ref[...] = row * (EPS / LOG2E) + jnp.transpose(sq_ref[...])[0:1, :] * (1.0 / WIDTH)


def weigh(q, f, parts, sq):
    return pl.pallas_call(
        weights_kernel,
        out_shape=(jax.ShapeDtypeStruct((X, ROWS, QUARTER), BF16), jax.ShapeDtypeStruct((1, QUARTER), F32)),
        in_specs=[VMEM] * 4,
        out_specs=(VMEM, VMEM),
        compiler_params=params(16),
        name="weights",
    )(q, f, parts, sq)


def transport_kernel(place, w_ref, data_ref, out_ref):
    total = jnp.dot(w_ref[0], data_ref[0], preferred_element_type=F32)
    for n in range(1, X):
        total = total + jnp.dot(w_ref[n], data_ref[n], preferred_element_type=F32)
    out_ref[0] = total.astype(out_ref.dtype)


def transport(place, w, data, mine):
    def piece(s, place):
        core = place[3] if mine else 1 - place[3]
        return (0, 0, lax.rem(place[2] + s, Y) * C + core)

    return pl.pallas_call(
        transport_kernel,
        grid_spec=pltpu.PrefetchScalarGridSpec(
            num_scalar_prefetch=1,
            grid=(Y,),
            in_specs=[
                pl.BlockSpec((X, ROWS, QUARTER), lambda s, place: (0, 0, 0)),
                pl.BlockSpec((X, QUARTER, SHARE), piece),
            ],
            out_specs=pl.BlockSpec((1, ROWS, SHARE), lambda s, place: (s, 0, 0)),
        ),
        out_shape=jax.ShapeDtypeStruct((Y, ROWS, SHARE), F32 if mine else BF16),
        compiler_params=params(58),
        cost_estimate=pl.CostEstimate(flops=ROWS * COUNT * WIDTH, bytes_accessed=8 * 2**20, transcendentals=0),
        name="keep" if mine else "give",
    )(place, w, data)


def body(noise, data):
    z, x, y, c = (lax.axis_index(a) for a in ("z", "x", "y", "core"))
    place = jnp.stack([z, x, y, c]).astype(jnp.int32)
    noise_all = lax.all_gather(noise, ("x", "y", "core")).reshape(X, Y * C, ROWS, SHARE)
    mine = lax.all_to_all(data.reshape(X, QUARTER, SLICE), "x", 0, 0)
    samples, sq = assemble(place, ring_z(mine))
    data_all = lax.all_gather(samples, "x")
    q, rows, sq_noise = score(place, samples, sq, noise_all)
    for step in range(ITERS):
        if step:
            rows = noise_lse(q, columns)
        columns, f = data_lse(q, lax.all_to_all(rows, ("x", "y", "core"), 0, 0))
        columns = lax.all_to_all(columns, "z", 0, 0)
    w, pot_g = weigh(q, f, columns, sq)
    w = lax.all_to_all(w, "x", 0, 0)
    give = transport(place, w, data_all, False)
    got = shift(give, "core", 1)
    keep = transport(place, w, data_all, True)
    both = keep + got.astype(F32)
    target = both[0]
    for by in (2, 1, 3):
        target = target + shift(both[by].astype(BF16), "y", by).astype(F32)
    velocity = (target - noise.astype(F32)).astype(BF16)
    own = lax.dynamic_slice_in_dim(f, 2 * x, 2, 0).reshape(ROWS)
    pot_f = own * (EPS / LOG2E) + sq_noise[0] / WIDTH
    turn = jnp.stack([shift(pot_g[0], "x", by) if by else pot_g[0] for by in range(X)])
    pot_g = jnp.concatenate([lax.dynamic_index_in_dim(turn, lax.rem(x - j + X, X), 0, False) for j in range(X)])
    return pot_f, pot_g, velocity


def solution(mesh):
    fine = Mesh(mesh.devices.reshape(Z, X, Y, C), ("z", "x", "y", "core"))
    row, col = ("z", "x"), ("y", "core")
    return jax.shard_map(
        body,
        mesh=fine,
        in_specs=(P(row, col), P(col, row)),
        out_specs=(P(row), P(col), P(row, col)),
        check_vma=False,
    )
```

```python
import functools
import math

import jax
import jax.numpy as jnp
from jax import lax
from jax.experimental import pallas as pl
from jax.experimental.pallas import tpu as pltpu
from jax.sharding import Mesh, PartitionSpec as P

ITERS = 3
EPS = 0.01
LOG2E = math.log2(math.e)
Z, X, Y, C = 8, 4, 4, 2
ROWS, SHARE = 256, 512
COUNT, SLICE = 1024, 128
WIDTH = 4096
QUARTER = COUNT // X
TALL = ROWS * X
CHUNKS = TALL // 128
GROUP = X * Y * C
TOTAL = 8192
UNIT = LOG2E / (WIDTH * EPS)
LOG2N = math.log2(TOTAL)
F32, BF16 = jnp.float32, jnp.bfloat16
VMEM = pl.BlockSpec(memory_space=pltpu.VMEM)
SMEM = pl.BlockSpec(memory_space=pltpu.SMEM)


def shift(x, axis, by):
    n = {"z": Z, "x": X, "y": Y, "core": C}[axis]
    return lax.ppermute(x, axis, [(j, (j + by) % n) for j in range(n)])


def params(mib):
    return pltpu.CompilerParams(vmem_limit_bytes=mib * 2**20)


def ring_z(x):
    forward = backward = x
    got = [x]
    for _ in range(1, Z // 2):
        forward, backward = shift(forward, "z", 1), shift(backward, "z", -1)
        got += [forward, backward]
    cut = x.shape[0] // 2
    return got + [shift(forward[:cut], "z", 1), shift(backward[cut:], "z", -1)]


def squares(ref, pieces):
    total = None
    for view in pieces:
        part = ref[view].astype(F32)
        total = part * part if total is None else total + part * part
    return total


def slot_of(place, piece):
    core, y = lax.rem(piece, C), lax.div(piece, C)
    return lax.rem(core - place[3] + C, C) * Y + lax.rem(y - place[2] + Y, Y)


def assemble_kernel(place, *refs):
    ins, (out_ref, sq_ref) = refs[:-2], refs[-2:]
    z = place[0]
    plan = [(0, 0)] + [(r, 0) for s in range(1, Z // 2) for r in (-s, s)] + [(Z // 2, 0), (Z // 2, X // 2)]
    for ref, (rel, first) in zip(ins, plan, strict=True):
        slot = slot_of(place, lax.rem(z + rel + Z, Z))
        for n in range(ref.shape[0]):
            out_ref[slot, :, pl.ds((first + n) * SLICE, SLICE)] = ref[n]
    step = 64
    for start in range(0, QUARTER, step):
        rows = pl.ds(start, step)
        views = [(p, rows, pl.ds(lane, 128)) for p in range(Y * C) for lane in range(0, SHARE, 128)]
        total = squares(out_ref, views)
        sq_ref[rows, :] = jnp.broadcast_to(jnp.sum(total, axis=1, keepdims=True), (step, 128))


def assemble(place, parts):
    return pl.pallas_call(
        assemble_kernel,
        out_shape=(jax.ShapeDtypeStruct((Y * C, QUARTER, SHARE), BF16), jax.ShapeDtypeStruct((QUARTER, 128), F32)),
        in_specs=[SMEM] + [VMEM] * len(parts),
        out_specs=(VMEM, VMEM),
        compiler_params=params(16),
        cost_estimate=pl.CostEstimate(flops=2 * QUARTER * WIDTH, bytes_accessed=4 * 2**20, transcendentals=0),
        name="assemble",
    )(place, *parts)


def lse(t, axis):
    top = jnp.max(t, axis=axis, keepdims=True)
    return top + jnp.log2(jnp.sum(jnp.exp2(t - top), axis=axis, keepdims=True))


def merged(ref):
    parts = ref[...]
    top = jnp.max(parts, axis=0)
    return top + jnp.log2(jnp.sum(jnp.exp2(parts - top[None]), axis=0))


def chunk(r):
    return pl.ds(r * 128, 128)


def score_kernel(place, data_ref, sq_ref, noise_ref, q_ref, out_ref, sqn_ref, lse_ref):
    data = jnp.concatenate([data_ref[slot_of(place, p)] for p in range(Y * C)], axis=1)
    for n in range(X):
        block = jnp.concatenate([noise_ref[n, p] for p in range(Y * C)], axis=1)
        gram = lax.dot_general(data, block, (((1,), (1,)), ((), ())), preferred_element_type=F32)
        gram = gram * (2.0 * UNIT)
        q_ref[:, pl.ds(n * ROWS, ROWS)] = gram
        t = gram - UNIT * jnp.concatenate([sq_ref[...]] * 2, axis=1)
        rows = lse(t, 0)
        lse_ref[pl.ds(2 * n, 1), :] = rows[:, :128]
        lse_ref[pl.ds(2 * n + 1, 1), :] = rows[:, 128:]
    out_ref[...] = jnp.broadcast_to(lse_ref[...][None], (GROUP, CHUNKS, 128))
    x = place[1]
    views = [(x, p, slice(None), pl.ds(lane, 128)) for p in range(Y * C) for lane in range(0, SHARE, 128)]
    sqn_ref[...] = jnp.sum(jnp.transpose(squares(noise_ref, views)), axis=0, keepdims=True)


def score(place, data, sq, noise):
    return pl.pallas_call(
        score_kernel,
        out_shape=(
            jax.ShapeDtypeStruct((QUARTER, TALL), F32),
            jax.ShapeDtypeStruct((GROUP, CHUNKS, 128), F32),
            jax.ShapeDtypeStruct((1, ROWS), F32),
        ),
        in_specs=[SMEM] + [VMEM] * 3,
        out_specs=(VMEM,) * 3,
        scratch_shapes=[pltpu.VMEM((CHUNKS, 128), F32)],
        compiler_params=params(32),
        name="score",
    )(place, data, sq, noise)


def to_column(g):
    return jnp.concatenate([jnp.transpose(jnp.broadcast_to(g[r : r + 1], (128, 128))) for r in range(2)], axis=0)


def noise_kernel(q_ref, part_ref, out_ref, lse_ref, g_ref):
    g_ref[...] = to_column(-LOG2N - merged(part_ref))
    for r in range(CHUNKS):
        lse_ref[pl.ds(r, 1), :] = lse(q_ref[:, chunk(r)] + g_ref[...], 0)
    out_ref[...] = jnp.broadcast_to(lse_ref[...][None], (GROUP, CHUNKS, 128))


def noise_lse(q, parts):
    return pl.pallas_call(
        noise_kernel,
        out_shape=jax.ShapeDtypeStruct((GROUP, CHUNKS, 128), F32),
        in_specs=[VMEM] * 2,
        out_specs=VMEM,
        scratch_shapes=[pltpu.VMEM((CHUNKS, 128), F32), pltpu.VMEM((QUARTER, 128), F32)],
        compiler_params=params(16),
        name="noise_lse",
    )(q, parts)


def data_kernel(q_ref, part_ref, out_ref, f_ref, lane_ref):
    f_ref[...] = -LOG2N - merged(part_ref)
    row = data_row(q_ref, f_ref, lane_ref)
    out_ref[...] = jnp.broadcast_to(two_rows(row)[None], (Z, 8, 128))


def data_row(q_ref, f_ref, lane_ref):
    step = 32
    for start in range(0, QUARTER, step):
        rows = pl.ds(start, step)
        t = [q_ref[rows, chunk(r)] + f_ref[pl.ds(r, 1), :] for r in range(CHUNKS)]
        top = functools.reduce(jnp.maximum, t)
        lane_ref[rows, :] = top + jnp.log2(sum(jnp.exp2(part - top) for part in t))
    return lse(jnp.transpose(lane_ref[...]), 0)


def two_rows(*rows):
    halves = [half for row in rows for half in (row[:, :128], row[:, 128:])]
    return jnp.concatenate(halves + [jnp.zeros((8 - len(halves), 128), F32)], axis=0)


def data_lse(q, parts):
    return pl.pallas_call(
        data_kernel,
        out_shape=(jax.ShapeDtypeStruct((Z, 8, 128), F32), jax.ShapeDtypeStruct((CHUNKS, 128), F32)),
        in_specs=[VMEM] * 2,
        out_specs=(VMEM, VMEM),
        scratch_shapes=[pltpu.VMEM((QUARTER, 128), F32)],
        compiler_params=params(16),
        name="data_lse",
    )(q, parts)


def last_kernel(place, q_ref, part_ref, sq_ref, out_ref, f_ref, *refs):
    w_refs, lane_ref = refs[:X], refs[X]
    f_ref[...] = -LOG2N - merged(part_ref)
    tile = two_rows(data_row(q_ref, f_ref, lane_ref), jnp.transpose(sq_ref[...])[0:1, :])
    out_ref[...] = jnp.broadcast_to(tile[None], (Z * X, 8, 128))
    column = to_column(tile)
    for by in range(X):
        block = lax.rem(place[1] + by, X)
        for h in range(2):
            lanes = pl.ds(pl.multiple_of(block * ROWS + h * 128, 128), 128)
            w = jnp.exp2((q_ref[:, lanes] + f_ref[pl.ds(2 * block + h, 1), :]) - column)
            w_refs[by][:, pl.ds(h * 128, 128)] = w.astype(BF16)


def last_lse(place, q, parts, sq):
    return pl.pallas_call(
        last_kernel,
        out_shape=(jax.ShapeDtypeStruct((Z * X, 8, 128), F32), jax.ShapeDtypeStruct((CHUNKS, 128), F32))
        + (jax.ShapeDtypeStruct((QUARTER, ROWS), BF16),) * X,
        in_specs=[SMEM] + [VMEM] * 3,
        out_specs=(VMEM,) * (2 + X),
        scratch_shapes=[pltpu.VMEM((QUARTER, 128), F32)],
        compiler_params=params(16),
        name="last_lse",
    )(place, q, parts, sq)


def give_kernel(place, part_ref, *refs):
    w_refs, (data_ref, out_ref, w_ref, pot_ref) = refs[:X], refs[X:]

    @pl.when(pl.program_id(0) == 0)
    def _():
        scale(place, part_ref, w_refs, w_ref, pot_ref)

    transport(w_ref, data_ref, out_ref)


def scale(place, part_ref, w_refs, w_ref, pot_ref):
    z, x = place[0], place[1]
    for n in range(X):
        parts = jnp.stack([part_ref[k * X + n, 0:4, :] for k in range(Z)])
        top = jnp.max(parts, axis=0)
        total = top + jnp.log2(jnp.sum(jnp.exp2(parts - top[None]), axis=0))
        pot_ref[pl.ds(2 * n, 2), :] = (-LOG2N - total[0:2]) * (EPS / LOG2E) + parts[0, 2:4] * (1.0 / WIDTH)
    for by in range(X):
        n = lax.rem(x - by + X, X)
        parts = jnp.stack([part_ref[k * X + n] for k in range(Z)])
        top = jnp.max(parts, axis=0)
        total = top + jnp.log2(jnp.sum(jnp.exp2(parts - top[None]), axis=0))
        factor = to_column(jnp.exp2(part_ref[z * X + n] - total))
        rows = pl.ds(pl.multiple_of(n * QUARTER, QUARTER), QUARTER)
        for h in range(2):
            w = w_refs[by][:, pl.ds(h * 128, 128)].astype(F32) * factor
            w_ref[rows, pl.ds(h * 128, 128)] = w.astype(BF16)


def transport(w_ref, data_ref, out_ref):
    block = jnp.concatenate([data_ref[n, 0] for n in range(X)], axis=0)
    total = lax.dot_general(w_ref[...], block, (((0,), (0,)), ((), ())), preferred_element_type=F32)
    out_ref[0] = total.astype(out_ref.dtype)


HALF_COST = pl.CostEstimate(flops=ROWS * COUNT * WIDTH, bytes_accessed=5 * 2**20, transcendentals=0)


def half_of(which):
    return pl.BlockSpec((X, 1, QUARTER, SHARE), lambda s: (0, which * Y + s, 0, 0))


PIECE = pl.BlockSpec((1, ROWS, SHARE), lambda s: (s, 0, 0))


def give(place, parts, blocks, data):
    return pl.pallas_call(
        give_kernel,
        grid=(Y,),
        out_shape=(
            jax.ShapeDtypeStruct((Y, ROWS, SHARE), BF16),
            jax.ShapeDtypeStruct((COUNT, ROWS), BF16),
            jax.ShapeDtypeStruct((2 * X, 128), F32),
        ),
        in_specs=[SMEM] + [VMEM] * (1 + X) + [half_of(1)],
        out_specs=(PIECE, VMEM, VMEM),
        compiler_params=params(53),
        cost_estimate=HALF_COST,
        name="give",
    )(place, parts, *blocks, data)


def keep(w, data):
    return pl.pallas_call(
        transport,
        grid=(Y,),
        out_shape=jax.ShapeDtypeStruct((Y, ROWS, SHARE), F32),
        in_specs=[VMEM, half_of(0)],
        out_specs=PIECE,
        compiler_params=params(53),
        cost_estimate=HALF_COST,
        name="keep",
    )(w, data)


def body(noise, data):
    z, x, y, c = (lax.axis_index(a) for a in ("z", "x", "y", "core"))
    place = jnp.stack([z, x, y, c]).astype(jnp.int32)
    noise_all = lax.all_gather(noise, ("x", "y", "core")).reshape(X, Y * C, ROWS, SHARE)
    swapped = lax.all_to_all(data.reshape(X, QUARTER, SLICE), "x", 0, 0)
    samples, sq = assemble(place, ring_z(swapped))
    data_all = lax.all_gather(samples, "x")
    q, rows, sq_noise = score(place, samples, sq, noise_all)
    for step in range(ITERS):
        if step:
            rows = noise_lse(q, columns)
        parts = lax.all_to_all(rows, ("x", "y", "core"), 0, 0)
        if step < ITERS - 1:
            columns, f = data_lse(q, parts)
            columns = lax.all_to_all(columns, "z", 0, 0)
    columns, f, *blocks = last_lse(place, q, parts, sq)
    blocks = [blocks[0]] + [shift(blocks[by], "x", by) for by in range(1, X)]
    columns = lax.all_to_all(columns, ("z", "x"), 0, 0)
    theirs, w, pot_g = give(place, columns, blocks, data_all)
    got = shift(theirs, "core", 1)
    mine = keep(w, data_all)
    both = mine + got.astype(F32)
    target = both[0]
    for by in (2, 1, 3):
        target = target + shift(both[by].astype(BF16), "y", by).astype(F32)
    velocity = (target - noise.astype(F32)).astype(BF16)
    own = lax.dynamic_slice_in_dim(f, 2 * x, 2, 0).reshape(ROWS)
    pot_f = own * (EPS / LOG2E) + sq_noise[0] / WIDTH
    return pot_f, pot_g.reshape(COUNT), velocity


def solution(mesh):
    fine = Mesh(mesh.devices.reshape(Z, X, Y, C), ("z", "x", "y", "core"))
    row, col = ("z", "x"), ("y", "core")
    return jax.shard_map(
        body,
        mesh=fine,
        in_specs=(P(row, col), P(col, row)),
        out_specs=(P(row), P(col), P(row, col)),
        check_vma=False,
    )
```

```python
import functools
import math

import jax
import jax.numpy as jnp
from jax import lax
from jax.experimental import pallas as pl
from jax.experimental.pallas import tpu as pltpu
from jax.sharding import Mesh, PartitionSpec as P

ITERS = 3
EPS = 0.01
LOG2E = math.log2(math.e)
Z, X, Y, C = 8, 4, 4, 2
ROWS, SHARE = 256, 512
COUNT, SLICE = 1024, 128
WIDTH = 4096
QUARTER = COUNT // X
TALL = ROWS * X
CHUNKS = TALL // 128
GROUP = X * Y * C
CUT = ROWS // 2
TOTAL = 8192
UNIT = LOG2E / (WIDTH * EPS)
LOG2N = math.log2(TOTAL)
F32, BF16 = jnp.float32, jnp.bfloat16
VMEM = pl.BlockSpec(memory_space=pltpu.VMEM)
SMEM = pl.BlockSpec(memory_space=pltpu.SMEM)


def shift(x, axis, by):
    n = {"z": Z, "x": X, "y": Y, "core": C}[axis]
    return lax.ppermute(x, axis, [(j, (j + by) % n) for j in range(n)])


def params(mib):
    return pltpu.CompilerParams(vmem_limit_bytes=mib * 2**20)


def both_ways(forward, backward, axis):
    return shift(forward, axis, 1), shift(backward, axis, -1)


def halves(forward, backward, axis):
    cut = forward.shape[0] // 2
    return both_ways(forward[:cut], backward[cut:], axis)


def gather(noise, data):
    hold = lax.optimization_barrier
    across = shift(noise, "x", 1), shift(noise, "x", -1), shift(noise, "x", 2)
    swapped = lax.all_to_all(data.reshape(X, QUARTER, SLICE), "x", 0, 0)
    swapped, *across = hold((swapped, *across))
    block = jnp.stack([noise, *across])
    y1 = both_ways(block, block, "y")
    z1 = both_ways(swapped, swapped, "z")
    z2 = both_ways(*z1, "z")
    y1, z2 = hold((y1, z2))
    y2 = halves(*y1, "y")
    z3 = both_ways(*z2, "z")
    mine = [block, *y1]
    theirs = [shift(block, "core", 1)]
    y2, z3, theirs = hold((y2, z3, theirs))
    z4 = halves(*z3, "z")
    mine += y2
    theirs += [shift(part, "core", 1) for part in mine[1:]]
    return mine + theirs, [swapped, *z1, *z2, *z3, *z4]


def squares(ref, pieces):
    total = None
    for view in pieces:
        part = ref[view].astype(F32)
        total = part * part if total is None else total + part * part
    return total


def slot_of(place, piece):
    core, y = lax.rem(piece, C), lax.div(piece, C)
    return lax.rem(core - place[3] + C, C) * Y + lax.rem(y - place[2] + Y, Y)


def assemble_kernel(place, *refs):
    ins, (out_ref, sq_ref) = refs[:-2], refs[-2:]
    z = place[0]
    plan = [(0, 0)] + [(r, 0) for s in range(1, Z // 2) for r in (-s, s)] + [(Z // 2, 0), (Z // 2, X // 2)]
    for ref, (rel, first) in zip(ins, plan, strict=True):
        slot = slot_of(place, lax.rem(z + rel + Z, Z))
        for n in range(ref.shape[0]):
            out_ref[slot, :, pl.ds((first + n) * SLICE, SLICE)] = ref[n]
    step = 64
    for start in range(0, QUARTER, step):
        rows = pl.ds(start, step)
        views = [(p, rows, pl.ds(lane, 128)) for p in range(Y * C) for lane in range(0, SHARE, 128)]
        total = squares(out_ref, views)
        sq_ref[rows, :] = jnp.broadcast_to(jnp.sum(total, axis=1, keepdims=True), (step, 128))


def assemble(place, parts):
    return pl.pallas_call(
        assemble_kernel,
        out_shape=(jax.ShapeDtypeStruct((Y * C, QUARTER, SHARE), BF16), jax.ShapeDtypeStruct((QUARTER, 128), F32)),
        in_specs=[SMEM] + [VMEM] * len(parts),
        out_specs=(VMEM, VMEM),
        compiler_params=params(16),
        cost_estimate=pl.CostEstimate(flops=2 * QUARTER * WIDTH, bytes_accessed=4 * 2**20, transcendentals=0),
        name="assemble",
    )(place, *parts)


def lse(t, axis):
    top = jnp.max(t, axis=axis, keepdims=True)
    return top + jnp.log2(jnp.sum(jnp.exp2(t - top), axis=axis, keepdims=True))


def merged(ref):
    parts = ref[...]
    top = jnp.max(parts, axis=0)
    return top + jnp.log2(jnp.sum(jnp.exp2(parts - top[None]), axis=0))


def chunk(r):
    return pl.ds(r * 128, 128)


def scored(data_ref, order, blocks, sq_ref):
    data = jnp.concatenate([data_ref[p] for p in order], axis=1)
    gram = lax.dot_general(
        data, jnp.concatenate(blocks, axis=1), (((1,), (1,)), ((), ())), preferred_element_type=F32
    ) * (2.0 * UNIT)
    return gram, lse(gram - UNIT * jnp.concatenate([sq_ref[...]] * (gram.shape[1] // 128), axis=1), 0)


def low_kernel(place, data_ref, sq_ref, *refs):
    ins, (q_ref, lse_ref, sqn_ref) = refs[:-3], refs[-3:]
    blocks, order = [], []
    for core in range(C):
        own, before, after, top, low = ins[5 * core : 5 * core + 5]
        for s, part in ((0, own), (Y - 1, before), (1, after)):
            blocks.append(part[...].reshape(X * CUT, SHARE))
            order.append(core * Y + s)
        blocks.append(jnp.concatenate([top[...], low[...]], axis=0).reshape(X * CUT, SHARE))
        order.append(core * Y + Y // 2)
    gram, rows = scored(data_ref, order, blocks, sq_ref)
    for n, rel in enumerate((0, -1, 1, 2)):
        block = lax.rem(place[1] + rel + X, X)
        q_ref[:, pl.ds(pl.multiple_of(block * 128, 128), 128)] = gram[:, n * 128 : (n + 1) * 128]
        lse_ref[pl.ds(block, 1), :] = rows[:, n * 128 : (n + 1) * 128]
    total = None
    for core in range(C):
        own, before, after, top, _ = ins[5 * core : 5 * core + 5]
        for part in (own, before, after, top):
            more = squares(part, [(0, slice(None), pl.ds(lane, 128)) for lane in range(0, SHARE, 128)])
            total = more if total is None else total + more
    sqn_ref[...] = jnp.sum(jnp.transpose(total), axis=0, keepdims=True)


def low_score(place, data, sq, parts):
    return pl.pallas_call(
        low_kernel,
        out_shape=(
            jax.ShapeDtypeStruct((QUARTER, X * CUT), F32),
            jax.ShapeDtypeStruct((X, 128), F32),
            jax.ShapeDtypeStruct((1, 128), F32),
        ),
        in_specs=[SMEM] + [VMEM] * (2 + len(parts)),
        out_specs=(VMEM,) * 3,
        compiler_params=params(24),
        cost_estimate=pl.CostEstimate(flops=QUARTER * TALL * WIDTH, bytes_accessed=6 * 2**20, transcendentals=0),
        name="low_score",
    )(place, data, sq, *parts)


def high_kernel(place, data_ref, sq_ref, noise_ref, low_ref, low_lse_ref, low_sqn_ref, q_ref, out_ref, sqn_ref):
    order = [slot_of(place, p) for p in range(Y * C)]
    blocks = [noise_ref[:, p].reshape(X * CUT, SHARE) for p in range(Y * C)]
    gram, rows = scored(data_ref, order, blocks, sq_ref)
    q_ref[:, : X * CUT] = gram
    q_ref[:, X * CUT :] = low_ref[...]
    parts = [rows[:, n * 128 : (n + 1) * 128] for n in range(X)] + [low_lse_ref[...]]
    out_ref[...] = jnp.broadcast_to(jnp.concatenate(parts, axis=0)[None], (GROUP, CHUNKS, 128))
    views = [(place[1], p, slice(None), pl.ds(lane, 128)) for p in range(Y * C) for lane in range(0, SHARE, 128)]
    own = jnp.sum(jnp.transpose(squares(noise_ref, views)), axis=0, keepdims=True)
    sqn_ref[...] = jnp.concatenate([own, low_sqn_ref[...]], axis=0)


def score(place, data, sq, noise, low):
    return pl.pallas_call(
        high_kernel,
        out_shape=(
            jax.ShapeDtypeStruct((QUARTER, TALL), F32),
            jax.ShapeDtypeStruct((GROUP, CHUNKS, 128), F32),
            jax.ShapeDtypeStruct((2, 128), F32),
        ),
        in_specs=[SMEM] + [VMEM] * 6,
        out_specs=(VMEM,) * 3,
        compiler_params=params(24),
        name="score",
    )(place, data, sq, noise, *low)


def to_column(g):
    return jnp.concatenate([jnp.transpose(jnp.broadcast_to(g[r : r + 1], (128, 128))) for r in range(2)], axis=0)


def noise_kernel(q_ref, part_ref, out_ref, lse_ref, g_ref):
    g_ref[...] = to_column(-LOG2N - merged(part_ref))
    for r in range(CHUNKS):
        lse_ref[pl.ds(r, 1), :] = lse(q_ref[:, chunk(r)] + g_ref[...], 0)
    out_ref[...] = jnp.broadcast_to(lse_ref[...][None], (GROUP, CHUNKS, 128))


def noise_lse(q, parts):
    return pl.pallas_call(
        noise_kernel,
        out_shape=jax.ShapeDtypeStruct((GROUP, CHUNKS, 128), F32),
        in_specs=[VMEM] * 2,
        out_specs=VMEM,
        scratch_shapes=[pltpu.VMEM((CHUNKS, 128), F32), pltpu.VMEM((QUARTER, 128), F32)],
        compiler_params=params(16),
        name="noise_lse",
    )(q, parts)


def data_kernel(q_ref, part_ref, out_ref, f_ref, lane_ref):
    f_ref[...] = -LOG2N - merged(part_ref)
    row = data_row(q_ref, f_ref, lane_ref)
    out_ref[...] = jnp.broadcast_to(two_rows(row)[None], (Z, 8, 128))


def data_row(q_ref, f_ref, lane_ref):
    step = 32
    for start in range(0, QUARTER, step):
        rows = pl.ds(start, step)
        t = [q_ref[rows, chunk(r)] + f_ref[pl.ds(r, 1), :] for r in range(CHUNKS)]
        top = functools.reduce(jnp.maximum, t)
        lane_ref[rows, :] = top + jnp.log2(sum(jnp.exp2(part - top) for part in t))
    return lse(jnp.transpose(lane_ref[...]), 0)


def two_rows(*rows):
    halves = [half for row in rows for half in (row[:, :128], row[:, 128:])]
    return jnp.concatenate(halves + [jnp.zeros((8 - len(halves), 128), F32)], axis=0)


def data_lse(q, parts):
    return pl.pallas_call(
        data_kernel,
        out_shape=(jax.ShapeDtypeStruct((Z, 8, 128), F32), jax.ShapeDtypeStruct((CHUNKS, 128), F32)),
        in_specs=[VMEM] * 2,
        out_specs=(VMEM, VMEM),
        scratch_shapes=[pltpu.VMEM((QUARTER, 128), F32)],
        compiler_params=params(16),
        name="data_lse",
    )(q, parts)


def last_kernel(place, q_ref, part_ref, sq_ref, out_ref, f_ref, *refs):
    w_refs, lane_ref = refs[:X], refs[X]
    f_ref[...] = -LOG2N - merged(part_ref)
    tile = two_rows(data_row(q_ref, f_ref, lane_ref), jnp.transpose(sq_ref[...])[0:1, :])
    out_ref[...] = jnp.broadcast_to(tile[None], (Z * X, 8, 128))
    column = to_column(tile)
    for by in range(X):
        block = lax.rem(place[1] + by, X)
        for h in range(2):
            lanes = pl.ds(pl.multiple_of((h * X + block) * 128, 128), 128)
            w = jnp.exp2((q_ref[:, lanes] + f_ref[pl.ds(h * X + block, 1), :]) - column)
            w_refs[by][:, pl.ds(h * 128, 128)] = w.astype(BF16)


def last_lse(place, q, parts, sq):
    return pl.pallas_call(
        last_kernel,
        out_shape=(jax.ShapeDtypeStruct((Z * X, 8, 128), F32), jax.ShapeDtypeStruct((CHUNKS, 128), F32))
        + (jax.ShapeDtypeStruct((QUARTER, ROWS), BF16),) * X,
        in_specs=[SMEM] + [VMEM] * 3,
        out_specs=(VMEM,) * (2 + X),
        scratch_shapes=[pltpu.VMEM((QUARTER, 128), F32)],
        compiler_params=params(16),
        name="last_lse",
    )(place, q, parts, sq)


def give_kernel(place, part_ref, *refs):
    w_refs, (data_ref, out_ref, w_ref, pot_ref) = refs[:X], refs[X:]

    @pl.when(pl.program_id(0) == 0)
    def _():
        scale(place, part_ref, w_refs, w_ref, pot_ref)

    transport(w_ref, data_ref, out_ref)


def scale(place, part_ref, w_refs, w_ref, pot_ref):
    z, x = place[0], place[1]
    for n in range(X):
        parts = jnp.stack([part_ref[k * X + n, 0:4, :] for k in range(Z)])
        top = jnp.max(parts, axis=0)
        total = top + jnp.log2(jnp.sum(jnp.exp2(parts - top[None]), axis=0))
        pot_ref[pl.ds(2 * n, 2), :] = (-LOG2N - total[0:2]) * (EPS / LOG2E) + parts[0, 2:4] * (1.0 / WIDTH)
    for by in range(X):
        n = lax.rem(x - by + X, X)
        parts = jnp.stack([part_ref[k * X + n] for k in range(Z)])
        top = jnp.max(parts, axis=0)
        total = top + jnp.log2(jnp.sum(jnp.exp2(parts - top[None]), axis=0))
        factor = jnp.exp2(part_ref[z * X + n] - total)
        factor = jnp.concatenate([factor[0:1], factor[1:2]], axis=1)
        lanes = pl.ds(pl.multiple_of(n * QUARTER, QUARTER), QUARTER)
        for h in range(2):
            w = jnp.transpose(w_refs[by][:, pl.ds(h * 128, 128)].astype(F32)) * factor
            w_ref[pl.ds(h * 128, 128), lanes] = w.astype(BF16)


def transport(w_ref, data_ref, out_ref):
    block = jnp.concatenate([data_ref[n, 0] for n in range(X)], axis=0)
    total = jnp.dot(w_ref[...], block, preferred_element_type=F32)
    out_ref[0] = total.astype(out_ref.dtype)


HALF_COST = pl.CostEstimate(flops=ROWS * COUNT * WIDTH, bytes_accessed=5 * 2**20, transcendentals=0)


def half_of(which):
    return pl.BlockSpec((X, 1, QUARTER, SHARE), lambda s: (0, which * Y + s, 0, 0))


PIECE = pl.BlockSpec((1, ROWS, SHARE), lambda s: (s, 0, 0))


def give(place, parts, blocks, data):
    return pl.pallas_call(
        give_kernel,
        grid=(Y,),
        out_shape=(
            jax.ShapeDtypeStruct((Y, ROWS, SHARE), BF16),
            jax.ShapeDtypeStruct((ROWS, COUNT), BF16),
            jax.ShapeDtypeStruct((2 * X, 128), F32),
        ),
        in_specs=[SMEM] + [VMEM] * (1 + X) + [half_of(1)],
        out_specs=(PIECE, VMEM, VMEM),
        compiler_params=params(53),
        cost_estimate=HALF_COST,
        name="give",
    )(place, parts, *blocks, data)


def keep(w, data):
    return pl.pallas_call(
        transport,
        grid=(Y,),
        out_shape=jax.ShapeDtypeStruct((Y, ROWS, SHARE), F32),
        in_specs=[VMEM, half_of(0)],
        out_specs=PIECE,
        compiler_params=params(53),
        cost_estimate=HALF_COST,
        name="keep",
    )(w, data)


def body(noise, data):
    z, x, y, c = (lax.axis_index(a) for a in ("z", "x", "y", "core"))
    place = jnp.stack([z, x, y, c]).astype(jnp.int32)
    noise_all = lax.all_gather(noise[:CUT], ("x", "y", "core")).reshape(X, Y * C, CUT, SHARE)
    noise_low, data_parts = gather(noise[CUT:], data)
    samples, sq = assemble(place, data_parts)
    data_all = lax.all_gather(samples, "x")
    low = low_score(place, samples, sq, noise_low)
    q, rows, sq_noise = score(place, samples, sq, noise_all, low)
    for step in range(ITERS):
        if step:
            rows = noise_lse(q, columns)
        parts = lax.all_to_all(rows, ("x", "y", "core"), 0, 0)
        if step < ITERS - 1:
            columns, f = data_lse(q, parts)
            columns = lax.all_to_all(columns, "z", 0, 0)
    columns, f, *blocks = last_lse(place, q, parts, sq)
    blocks = [blocks[0]] + [shift(blocks[by], "x", by) for by in range(1, X)]
    columns = lax.all_to_all(columns, ("z", "x"), 0, 0)
    theirs, w, pot_g = give(place, columns, blocks, data_all)
    got = shift(theirs, "core", 1)
    mine = keep(w, data_all)
    both = mine + got.astype(F32)
    target = both[0]
    for by in (2, 1, 3):
        target = target + shift(both[by].astype(BF16), "y", by).astype(F32)
    velocity = (target - noise.astype(F32)).astype(BF16)
    own = lax.dynamic_index_in_dim(f.reshape(2, X, 128), x, 1, False)
    pot_f = (own * (EPS / LOG2E) + sq_noise / WIDTH).reshape(ROWS)
    return pot_f, pot_g.reshape(COUNT), velocity


def solution(mesh):
    fine = Mesh(mesh.devices.reshape(Z, X, Y, C), ("z", "x", "y", "core"))
    row, col = ("z", "x"), ("y", "core")
    return jax.shard_map(
        body,
        mesh=fine,
        in_specs=(P(row, col), P(col, row)),
        out_specs=(P(row), P(col), P(row, col)),
        check_vma=False,
    )
```

```python
import functools
import math

import jax
import jax.numpy as jnp
from jax import lax
from jax.experimental import pallas as pl
from jax.experimental.pallas import tpu as pltpu
from jax.sharding import Mesh, PartitionSpec as P

ITERS = 3
EPS = 0.01
LOG2E = math.log2(math.e)
Z, X, Y, C = 8, 4, 4, 2
ROWS, SHARE = 256, 512
COUNT, SLICE = 1024, 128
WIDTH = 4096
QUARTER = COUNT // X
TALL = ROWS * X
CHUNKS = TALL // 128
GROUP = X * Y * C
TOTAL = 8192
UNIT = LOG2E / (WIDTH * EPS)
LOG2N = math.log2(TOTAL)
F32, BF16 = jnp.float32, jnp.bfloat16
VMEM = pl.BlockSpec(memory_space=pltpu.VMEM)
SMEM = pl.BlockSpec(memory_space=pltpu.SMEM)


def shift(x, axis, by):
    n = {"z": Z, "x": X, "y": Y, "core": C}[axis]
    return lax.ppermute(x, axis, [(j, (j + by) % n) for j in range(n)])


def params(mib):
    return pltpu.CompilerParams(vmem_limit_bytes=mib * 2**20)


def ring_z(x):
    forward = backward = x
    got = [x]
    for _ in range(1, Z // 2):
        forward, backward = shift(forward, "z", 1), shift(backward, "z", -1)
        got += [forward, backward]
    cut = x.shape[0] // 2
    return got + [shift(forward[:cut], "z", 1), shift(backward[cut:], "z", -1)]


def squares(ref, pieces):
    total = None
    for view in pieces:
        part = ref[view].astype(F32)
        total = part * part if total is None else total + part * part
    return total


def slot_of(place, piece):
    core, y = lax.rem(piece, C), lax.div(piece, C)
    return lax.rem(core - place[3] + C, C) * Y + lax.rem(y - place[2] + Y, Y)


def assemble_kernel(place, *refs):
    ins, (out_ref, sq_ref) = refs[:-2], refs[-2:]
    z = place[0]
    plan = [(0, 0)] + [(r, 0) for s in range(1, Z // 2) for r in (-s, s)] + [(Z // 2, 0), (Z // 2, X // 2)]
    for ref, (rel, first) in zip(ins, plan, strict=True):
        slot = slot_of(place, lax.rem(z + rel + Z, Z))
        for n in range(ref.shape[0]):
            out_ref[slot, :, pl.ds((first + n) * SLICE, SLICE)] = ref[n]
    step = 64
    for start in range(0, QUARTER, step):
        rows = pl.ds(start, step)
        views = [(p, rows, pl.ds(lane, 128)) for p in range(Y * C) for lane in range(0, SHARE, 128)]
        total = squares(out_ref, views)
        sq_ref[rows, :] = jnp.broadcast_to(jnp.sum(total, axis=1, keepdims=True), (step, 128))


def assemble(place, parts):
    return pl.pallas_call(
        assemble_kernel,
        out_shape=(jax.ShapeDtypeStruct((Y * C, QUARTER, SHARE), BF16), jax.ShapeDtypeStruct((QUARTER, 128), F32)),
        in_specs=[SMEM] + [VMEM] * len(parts),
        out_specs=(VMEM, VMEM),
        compiler_params=params(16),
        cost_estimate=pl.CostEstimate(flops=2 * QUARTER * WIDTH, bytes_accessed=4 * 2**20, transcendentals=0),
        name="assemble",
    )(place, *parts)


def lse(t, axis):
    top = jnp.max(t, axis=axis, keepdims=True)
    return top + jnp.log2(jnp.sum(jnp.exp2(t - top), axis=axis, keepdims=True))


def merged(ref):
    parts = ref[...]
    top = jnp.max(parts, axis=0)
    return top + jnp.log2(jnp.sum(jnp.exp2(parts - top[None]), axis=0))


def chunk(r):
    return pl.ds(r * 128, 128)


def score_kernel(place, data_ref, sq_ref, noise_ref, q_ref, out_ref, sqn_ref, lse_ref):
    data = jnp.concatenate([data_ref[slot_of(place, p)] for p in range(Y * C)], axis=1)
    for n in range(X):
        block = jnp.concatenate([noise_ref[n, p] for p in range(Y * C)], axis=1)
        gram = lax.dot_general(data, block, (((1,), (1,)), ((), ())), preferred_element_type=F32)
        gram = gram * (2.0 * UNIT)
        q_ref[:, pl.ds(n * ROWS, ROWS)] = gram
        t = gram - UNIT * jnp.concatenate([sq_ref[...]] * 2, axis=1)
        rows = lse(t, 0)
        lse_ref[pl.ds(2 * n, 1), :] = rows[:, :128]
        lse_ref[pl.ds(2 * n + 1, 1), :] = rows[:, 128:]
    out_ref[...] = jnp.broadcast_to(lse_ref[...][None], (GROUP, CHUNKS, 128))
    x = place[1]
    views = [(x, p, slice(None), pl.ds(lane, 128)) for p in range(Y * C) for lane in range(0, SHARE, 128)]
    sqn_ref[...] = jnp.sum(jnp.transpose(squares(noise_ref, views)), axis=0, keepdims=True)


def score(place, data, sq, noise):
    return pl.pallas_call(
        score_kernel,
        out_shape=(
            jax.ShapeDtypeStruct((QUARTER, TALL), F32),
            jax.ShapeDtypeStruct((GROUP, CHUNKS, 128), F32),
            jax.ShapeDtypeStruct((1, ROWS), F32),
        ),
        in_specs=[SMEM] + [VMEM] * 3,
        out_specs=(VMEM,) * 3,
        scratch_shapes=[pltpu.VMEM((CHUNKS, 128), F32)],
        compiler_params=params(32),
        name="score",
    )(place, data, sq, noise)


def to_column(g):
    return jnp.concatenate([jnp.transpose(jnp.broadcast_to(g[r : r + 1], (128, 128))) for r in range(2)], axis=0)


def noise_kernel(q_ref, part_ref, out_ref, lse_ref, g_ref):
    g_ref[...] = to_column(-LOG2N - merged(part_ref))
    for r in range(CHUNKS):
        lse_ref[pl.ds(r, 1), :] = lse(q_ref[:, chunk(r)] + g_ref[...], 0)
    out_ref[...] = jnp.broadcast_to(lse_ref[...][None], (GROUP, CHUNKS, 128))


def noise_lse(q, parts):
    return pl.pallas_call(
        noise_kernel,
        out_shape=jax.ShapeDtypeStruct((GROUP, CHUNKS, 128), F32),
        in_specs=[VMEM] * 2,
        out_specs=VMEM,
        scratch_shapes=[pltpu.VMEM((CHUNKS, 128), F32), pltpu.VMEM((QUARTER, 128), F32)],
        compiler_params=params(16),
        name="noise_lse",
    )(q, parts)


def data_kernel(q_ref, part_ref, out_ref, f_ref, lane_ref):
    f_ref[...] = -LOG2N - merged(part_ref)
    row = data_row(q_ref, f_ref, lane_ref)
    out_ref[...] = jnp.broadcast_to(two_rows(row)[None], (Z, 8, 128))


def data_row(q_ref, f_ref, lane_ref):
    step = 32
    for start in range(0, QUARTER, step):
        rows = pl.ds(start, step)
        t = [q_ref[rows, chunk(r)] + f_ref[pl.ds(r, 1), :] for r in range(CHUNKS)]
        top = functools.reduce(jnp.maximum, t)
        lane_ref[rows, :] = top + jnp.log2(sum(jnp.exp2(part - top) for part in t))
    return lse(jnp.transpose(lane_ref[...]), 0)


def two_rows(*rows):
    halves = [half for row in rows for half in (row[:, :128], row[:, 128:])]
    return jnp.concatenate(halves + [jnp.zeros((8 - len(halves), 128), F32)], axis=0)


def data_lse(q, parts):
    return pl.pallas_call(
        data_kernel,
        out_shape=(jax.ShapeDtypeStruct((Z, 8, 128), F32), jax.ShapeDtypeStruct((CHUNKS, 128), F32)),
        in_specs=[VMEM] * 2,
        out_specs=(VMEM, VMEM),
        scratch_shapes=[pltpu.VMEM((QUARTER, 128), F32)],
        compiler_params=params(16),
        name="data_lse",
    )(q, parts)


def last_kernel(place, q_ref, part_ref, sq_ref, out_ref, f_ref, *refs):
    w_refs, lane_ref = refs[:X], refs[X]
    f_ref[...] = -LOG2N - merged(part_ref)
    tile = two_rows(data_row(q_ref, f_ref, lane_ref), jnp.transpose(sq_ref[...])[0:1, :])
    out_ref[...] = jnp.broadcast_to(tile[None], (Z * X, 8, 128))
    column = to_column(tile)
    for by in range(X):
        block = lax.rem(place[1] + by, X)
        for h in range(2):
            lanes = pl.ds(pl.multiple_of(block * ROWS + h * 128, 128), 128)
            w = jnp.exp2((q_ref[:, lanes] + f_ref[pl.ds(2 * block + h, 1), :]) - column)
            w_refs[by][:, pl.ds(h * 128, 128)] = w.astype(BF16)


def last_lse(place, q, parts, sq):
    return pl.pallas_call(
        last_kernel,
        out_shape=(jax.ShapeDtypeStruct((Z * X, 8, 128), F32), jax.ShapeDtypeStruct((CHUNKS, 128), F32))
        + (jax.ShapeDtypeStruct((QUARTER, ROWS), BF16),) * X,
        in_specs=[SMEM] + [VMEM] * 3,
        out_specs=(VMEM,) * (2 + X),
        scratch_shapes=[pltpu.VMEM((QUARTER, 128), F32)],
        compiler_params=params(16),
        name="last_lse",
    )(place, q, parts, sq)


HALF_COST = pl.CostEstimate(flops=ROWS * COUNT * WIDTH, bytes_accessed=5 * 2**20, transcendentals=0)


def transport(w_ref, data_ref, first, out_ref):
    for s in range(Y):
        block = jnp.concatenate([data_ref[n, first + s] for n in range(X)], axis=0)
        out_ref[s] = jnp.dot(w_ref[...], block, preferred_element_type=F32).astype(out_ref.dtype)


def give_kernel(place, part_ref, *refs):
    w_refs, (data_ref, out_ref, w_ref, pot_ref) = refs[:X], refs[X:]
    scale(place, part_ref, w_refs, w_ref, pot_ref)
    transport(w_ref, data_ref, Y, out_ref)


def keep_kernel(w_ref, data_ref, out_ref):
    transport(w_ref, data_ref, 0, out_ref)


def scale(place, part_ref, w_refs, w_ref, pot_ref):
    z, x = place[0], place[1]
    for n in range(X):
        parts = jnp.stack([part_ref[k * X + n, 0:4, :] for k in range(Z)])
        top = jnp.max(parts, axis=0)
        total = top + jnp.log2(jnp.sum(jnp.exp2(parts - top[None]), axis=0))
        pot_ref[pl.ds(2 * n, 2), :] = (-LOG2N - total[0:2]) * (EPS / LOG2E) + parts[0, 2:4] * (1.0 / WIDTH)
    for by in range(X):
        n = lax.rem(x - by + X, X)
        parts = jnp.stack([part_ref[k * X + n] for k in range(Z)])
        top = jnp.max(parts, axis=0)
        total = top + jnp.log2(jnp.sum(jnp.exp2(parts - top[None]), axis=0))
        factor = jnp.exp2(part_ref[z * X + n] - total)
        factor = jnp.concatenate([factor[0:1], factor[1:2]], axis=1)
        lanes = pl.ds(pl.multiple_of(n * QUARTER, QUARTER), QUARTER)
        for h in range(2):
            w = jnp.transpose(w_refs[by][:, pl.ds(h * 128, 128)].astype(F32)) * factor
            w_ref[pl.ds(h * 128, 128), lanes] = w.astype(BF16)


def give(place, parts, blocks, data):
    return pl.pallas_call(
        give_kernel,
        out_shape=(
            jax.ShapeDtypeStruct((Y, ROWS, SHARE), BF16),
            jax.ShapeDtypeStruct((ROWS, COUNT), BF16),
            jax.ShapeDtypeStruct((2 * X, 128), F32),
        ),
        in_specs=[SMEM] + [VMEM] * (2 + X),
        out_specs=(VMEM,) * 3,
        compiler_params=params(24),
        cost_estimate=HALF_COST,
        name="give",
    )(place, parts, *blocks, data)


def keep(w, data):
    return pl.pallas_call(
        keep_kernel,
        out_shape=jax.ShapeDtypeStruct((Y, ROWS, SHARE), F32),
        in_specs=[VMEM] * 2,
        out_specs=VMEM,
        compiler_params=params(24),
        cost_estimate=HALF_COST,
        name="keep",
    )(w, data)


def join_kernel(mine_ref, got_ref, own_ref, *out_refs):
    own_ref[...] = mine_ref[0] + got_ref[0].astype(F32)
    for s, ref in enumerate(out_refs, 1):
        ref[...] = (mine_ref[s] + got_ref[s].astype(F32)).astype(BF16)


def join(mine, got):
    return pl.pallas_call(
        join_kernel,
        out_shape=(jax.ShapeDtypeStruct((ROWS, SHARE), F32),)
        + (jax.ShapeDtypeStruct((ROWS, SHARE), BF16),) * (Y - 1),
        in_specs=[VMEM] * 2,
        out_specs=(VMEM,) * Y,
        compiler_params=params(16),
        name="join",
    )(mine, got)


def body(noise, data):
    z, x, y, c = (lax.axis_index(a) for a in ("z", "x", "y", "core"))
    place = jnp.stack([z, x, y, c]).astype(jnp.int32)
    noise_all = lax.all_gather(noise, ("x", "y", "core")).reshape(X, Y * C, ROWS, SHARE)
    swapped = lax.all_to_all(data.reshape(X, QUARTER, SLICE), "x", 0, 0)
    samples, sq = assemble(place, ring_z(swapped))
    data_all = lax.all_gather(samples, "x")
    q, rows, sq_noise = score(place, samples, sq, noise_all)
    for step in range(ITERS):
        if step:
            rows = noise_lse(q, columns)
        parts = lax.all_to_all(rows, ("x", "y", "core"), 0, 0)
        if step < ITERS - 1:
            columns, f = data_lse(q, parts)
            columns = lax.all_to_all(columns, "z", 0, 0)
    columns, f, *blocks = last_lse(place, q, parts, sq)
    blocks = [blocks[0]] + [shift(blocks[by], "x", by) for by in range(1, X)]
    columns = lax.all_to_all(columns, ("z", "x"), 0, 0)
    theirs, w, pot_g = give(place, columns, blocks, data_all)
    got = shift(theirs, "core", 1)
    target, *rest = join(keep(w, data_all), got)
    for by in (2, 1, 3):
        target = target + shift(rest[by - 1], "y", by).astype(F32)
    velocity = (target - noise.astype(F32)).astype(BF16)
    own = lax.dynamic_slice_in_dim(f, 2 * x, 2, 0).reshape(ROWS)
    pot_f = own * (EPS / LOG2E) + sq_noise[0] / WIDTH
    return pot_f, pot_g.reshape(COUNT), velocity


def solution(mesh):
    fine = Mesh(mesh.devices.reshape(Z, X, Y, C), ("z", "x", "y", "core"))
    row, col = ("z", "x"), ("y", "core")
    return jax.shard_map(
        body,
        mesh=fine,
        in_specs=(P(row, col), P(col, row)),
        out_specs=(P(row), P(col), P(row, col)),
        check_vma=False,
    )
```

```python
import functools
import math

import jax
import jax.numpy as jnp
from jax import lax
from jax.experimental import pallas as pl
from jax.experimental.pallas import tpu as pltpu
from jax.sharding import Mesh, PartitionSpec as P

ITERS = 3
EPS = 0.01
LOG2E = math.log2(math.e)
Z, X, Y, C = 8, 4, 4, 2
ROWS, SHARE = 256, 512
COUNT, SLICE = 1024, 128
WIDTH = 4096
QUARTER = COUNT // X
TALL = ROWS * X
CHUNKS = TALL // 128
GROUP = X * Y * C
CUT = ROWS // 2
AROUND = (0, -1, 1, 2)
TOTAL = 8192
UNIT = LOG2E / (WIDTH * EPS)
LOG2N = math.log2(TOTAL)
F32, BF16 = jnp.float32, jnp.bfloat16
VMEM = pl.BlockSpec(memory_space=pltpu.VMEM)
SMEM = pl.BlockSpec(memory_space=pltpu.SMEM)


def shift(x, axis, by):
    n = {"z": Z, "x": X, "y": Y, "core": C}[axis]
    return lax.ppermute(x, axis, [(j, (j + by) % n) for j in range(n)])


def params(mib):
    return pltpu.CompilerParams(vmem_limit_bytes=mib * 2**20)


def both_ways(forward, backward, axis):
    return shift(forward, axis, 1), shift(backward, axis, -1)


def halves(forward, backward, axis):
    cut = forward.shape[0] // 2
    return both_ways(forward[:cut], backward[cut:], axis)


def around(block, axis):
    return [block, shift(block, axis, 1), shift(block, axis, -1), shift(block, axis, 2)]


def gather_noise(noise):
    hold = lax.optimization_barrier
    across, along = hold((around(noise[:CUT], "x"), around(noise[CUT:], "y")))
    across, along = jnp.stack(across), jnp.stack(along)
    y1, x1 = hold((both_ways(across, across, "y"), both_ways(along, along, "x")))
    return [across, *y1, *halves(*y1, "y"), along, *x1, *halves(*x1, "x")]


def squares(ref, pieces):
    total = None
    for view in pieces:
        part = ref[view].astype(F32)
        total = part * part if total is None else total + part * part
    return total


def lse(t, axis):
    top = jnp.max(t, axis=axis, keepdims=True)
    return top + jnp.log2(jnp.sum(jnp.exp2(t - top), axis=axis, keepdims=True))


def merged(ref):
    parts = ref[...]
    top = jnp.max(parts, axis=0)
    return top + jnp.log2(jnp.sum(jnp.exp2(parts - top[None]), axis=0))


def chunk(r):
    return pl.ds(r * 128, 128)


def at(place, which, rel, size):
    return lax.rem(place[which] + rel + size, size)


def blocks_of(parts):
    first, second = parts[:5], parts[5:]

    def of(five, far, near):
        if far < 3:
            return five[far].at[near]
        return five[3 + near // 2].at[near % 2]

    return (
        [[of(first, k, j) for k in range(Y)] for j in range(X)],
        [[of(second, j, k) for k in range(Y)] for j in range(X)],
    )


def partial_scores(place, data_ref, core, parts, q_ref, sq_ref):
    pieces = [at(place, 2, rel, Y) for rel in AROUND]
    lhs = jnp.concatenate([data_ref[p, core, n] for p in pieces for n in range(X)], axis=1)
    for h, blocks in enumerate(blocks_of(parts)):
        rhs = jnp.concatenate([jnp.concatenate([ref[...] for ref in row], axis=1) for row in blocks], axis=0)
        gram = lax.dot_general(lhs, rhs, (((1,), (1,)), ((), ())), preferred_element_type=F32) * (2.0 * UNIT)
        for j, rel in enumerate(AROUND):
            lanes = pl.ds(pl.multiple_of((h * X + at(place, 1, rel, X)) * 128, 128), 128)
            q_ref[:QUARTER, lanes] = gram[:, j * 128 : (j + 1) * 128]
    sq_ref[...] = squares(data_ref, [(p, core, n) for p in range(Y) for n in range(X)])


def theirs_kernel(place, data_ref, *refs):
    parts, (out_ref, sqn_ref, sq_ref) = refs[:10], refs[10:]
    partial_scores(place, data_ref, 1 - place[3], parts, out_ref, sq_ref)
    out_ref[:QUARTER, TALL:] = sq_ref[...]
    rows = []
    for blocks in blocks_of(parts):
        t = [squares(ref, [(slice(None), pl.ds(lane, 128)) for lane in range(0, SHARE, 128)]) for ref in blocks[0]]
        total = (t[0] + t[3]) + (t[1] + t[2])
        rows.append(jnp.sum(jnp.transpose(total), axis=0, keepdims=True))
    sqn_ref[...] = jnp.concatenate(rows, axis=0)
    out_ref[QUARTER:, :] = jnp.zeros((8, TALL + 128), F32)
    out_ref[QUARTER : QUARTER + 2, :128] = sqn_ref[...]


def theirs(place, data, parts):
    return pl.pallas_call(
        theirs_kernel,
        out_shape=(jax.ShapeDtypeStruct((QUARTER + 8, TALL + 128), F32), jax.ShapeDtypeStruct((2, 128), F32)),
        in_specs=[SMEM] + [VMEM] * 11,
        out_specs=(VMEM,) * 2,
        scratch_shapes=[pltpu.VMEM((QUARTER, 128), F32)],
        compiler_params=params(24),
        name="theirs",
    )(place, data, *parts)


def ours_kernel(place, data_ref, *refs):
    partial_scores(place, data_ref, place[3], refs[:10], refs[10], refs[11])


def ours(place, data, parts):
    return pl.pallas_call(
        ours_kernel,
        out_shape=(jax.ShapeDtypeStruct((QUARTER, TALL), F32), jax.ShapeDtypeStruct((QUARTER, 128), F32)),
        in_specs=[SMEM] + [VMEM] * 11,
        out_specs=(VMEM,) * 2,
        compiler_params=params(24),
        cost_estimate=pl.CostEstimate(flops=QUARTER * TALL * WIDTH, bytes_accessed=6 * 2**20, transcendentals=0),
        name="ours",
    )(place, data, *parts)


def score_kernel(mine_ref, sq_mine_ref, sqn_mine_ref, got_ref, q_ref, out_ref, sq_ref, sqn_ref, lse_ref):
    sq = jnp.sum(sq_mine_ref[...] + got_ref[:QUARTER, TALL:], axis=1, keepdims=True)
    sq_ref[...] = jnp.broadcast_to(sq, (QUARTER, 128))
    sqn_ref[...] = sqn_mine_ref[...] + got_ref[QUARTER : QUARTER + 2, :128]
    for r in range(CHUNKS):
        q = mine_ref[:, chunk(r)] + got_ref[:QUARTER, chunk(r)]
        q_ref[:, chunk(r)] = q
        lse_ref[pl.ds(r, 1), :] = lse(q - UNIT * sq_ref[...], 0)
    out_ref[...] = jnp.broadcast_to(lse_ref[...][None], (GROUP, CHUNKS, 128))


def score(mine, sq_mine, sqn_mine, got):
    return pl.pallas_call(
        score_kernel,
        out_shape=(
            jax.ShapeDtypeStruct((QUARTER, TALL), F32),
            jax.ShapeDtypeStruct((GROUP, CHUNKS, 128), F32),
            jax.ShapeDtypeStruct((QUARTER, 128), F32),
            jax.ShapeDtypeStruct((2, 128), F32),
        ),
        in_specs=[VMEM] * 4,
        out_specs=(VMEM,) * 4,
        scratch_shapes=[pltpu.VMEM((CHUNKS, 128), F32)],
        compiler_params=params(16),
        name="score",
    )(mine, sq_mine, sqn_mine, got)


def to_column(g):
    return jnp.concatenate([jnp.transpose(jnp.broadcast_to(g[r : r + 1], (128, 128))) for r in range(2)], axis=0)


def noise_kernel(q_ref, part_ref, out_ref, lse_ref, g_ref):
    g_ref[...] = to_column(-LOG2N - merged(part_ref))
    for r in range(CHUNKS):
        lse_ref[pl.ds(r, 1), :] = lse(q_ref[:, chunk(r)] + g_ref[...], 0)
    out_ref[...] = jnp.broadcast_to(lse_ref[...][None], (GROUP, CHUNKS, 128))


def noise_lse(q, parts):
    return pl.pallas_call(
        noise_kernel,
        out_shape=jax.ShapeDtypeStruct((GROUP, CHUNKS, 128), F32),
        in_specs=[VMEM] * 2,
        out_specs=VMEM,
        scratch_shapes=[pltpu.VMEM((CHUNKS, 128), F32), pltpu.VMEM((QUARTER, 128), F32)],
        compiler_params=params(16),
        name="noise_lse",
    )(q, parts)


def data_kernel(q_ref, part_ref, out_ref, f_ref, lane_ref):
    f_ref[...] = -LOG2N - merged(part_ref)
    row = data_row(q_ref, f_ref, lane_ref)
    out_ref[...] = jnp.broadcast_to(two_rows(row)[None], (Z, 8, 128))


def data_row(q_ref, f_ref, lane_ref):
    step = 32
    for start in range(0, QUARTER, step):
        rows = pl.ds(start, step)
        t = [q_ref[rows, chunk(r)] + f_ref[pl.ds(r, 1), :] for r in range(CHUNKS)]
        top = functools.reduce(jnp.maximum, t)
        lane_ref[rows, :] = top + jnp.log2(sum(jnp.exp2(part - top) for part in t))
    return lse(jnp.transpose(lane_ref[...]), 0)


def two_rows(*rows):
    halves = [half for row in rows for half in (row[:, :128], row[:, 128:])]
    return jnp.concatenate(halves + [jnp.zeros((8 - len(halves), 128), F32)], axis=0)


def data_lse(q, parts):
    return pl.pallas_call(
        data_kernel,
        out_shape=(jax.ShapeDtypeStruct((Z, 8, 128), F32), jax.ShapeDtypeStruct((CHUNKS, 128), F32)),
        in_specs=[VMEM] * 2,
        out_specs=(VMEM, VMEM),
        scratch_shapes=[pltpu.VMEM((QUARTER, 128), F32)],
        compiler_params=params(16),
        name="data_lse",
    )(q, parts)


def last_kernel(place, q_ref, part_ref, sq_ref, out_ref, f_ref, *refs):
    w_refs, lane_ref = refs[:X], refs[X]
    f_ref[...] = -LOG2N - merged(part_ref)
    tile = two_rows(data_row(q_ref, f_ref, lane_ref), jnp.transpose(sq_ref[...])[0:1, :])
    out_ref[...] = jnp.broadcast_to(tile[None], (Z * X, 8, 128))
    column = to_column(tile)
    for by in range(X):
        block = lax.rem(place[1] + by, X)
        for h in range(2):
            lanes = pl.ds(pl.multiple_of((h * X + block) * 128, 128), 128)
            w = jnp.exp2((q_ref[:, lanes] + f_ref[pl.ds(h * X + block, 1), :]) - column)
            w_refs[by][:, pl.ds(h * 128, 128)] = w.astype(BF16)


def last_lse(place, q, parts, sq):
    return pl.pallas_call(
        last_kernel,
        out_shape=(jax.ShapeDtypeStruct((Z * X, 8, 128), F32), jax.ShapeDtypeStruct((CHUNKS, 128), F32))
        + (jax.ShapeDtypeStruct((QUARTER, ROWS), BF16),) * X,
        in_specs=[SMEM] + [VMEM] * 3,
        out_specs=(VMEM,) * (2 + X),
        scratch_shapes=[pltpu.VMEM((QUARTER, 128), F32)],
        compiler_params=params(16),
        name="last_lse",
    )(place, q, parts, sq)


def scale_kernel(place, part_ref, *refs):
    w_refs, (w_ref, pot_ref) = refs[:X], refs[X:]
    z, x = place[0], place[1]
    for n in range(X):
        parts = jnp.stack([part_ref[k * X + n, 0:4, :] for k in range(Z)])
        top = jnp.max(parts, axis=0)
        total = top + jnp.log2(jnp.sum(jnp.exp2(parts - top[None]), axis=0))
        pot_ref[pl.ds(2 * n, 2), :] = (-LOG2N - total[0:2]) * (EPS / LOG2E) + parts[0, 2:4] * (1.0 / WIDTH)
    for by in range(X):
        n = lax.rem(x - by + X, X)
        parts = jnp.stack([part_ref[k * X + n] for k in range(Z)])
        top = jnp.max(parts, axis=0)
        total = top + jnp.log2(jnp.sum(jnp.exp2(parts - top[None]), axis=0))
        factor = jnp.exp2(part_ref[z * X + n] - total)
        factor = jnp.concatenate([factor[0:1], factor[1:2]], axis=1)
        lanes = pl.ds(pl.multiple_of(n * QUARTER, QUARTER), QUARTER)
        for h in range(2):
            w = jnp.transpose(w_refs[by][:, pl.ds(h * 128, 128)].astype(F32)) * factor
            w_ref[pl.ds(h * 128, 128), lanes] = w.astype(BF16)


def scale(place, parts, blocks):
    return pl.pallas_call(
        scale_kernel,
        out_shape=(jax.ShapeDtypeStruct((ROWS, COUNT), BF16), jax.ShapeDtypeStruct((2 * X, 128), F32)),
        in_specs=[SMEM] + [VMEM] * (1 + X),
        out_specs=(VMEM,) * 2,
        compiler_params=params(16),
        name="scale",
    )(place, parts, *blocks)


def transport_kernel(place, w_ref, got_ref, data_ref, own_ref, *out_refs):
    lhs = jnp.concatenate([w_ref[...], got_ref[...]], axis=1)
    for s in range(Y):
        y = at(place, 2, s, Y)
        rhs = []
        for core in (place[3], 1 - place[3]):
            for n in range(X):
                rhs.append(jnp.concatenate([data_ref[n, y, core, k] for k in range(X)], axis=1))
        total = jnp.dot(lhs, jnp.concatenate(rhs, axis=0), preferred_element_type=F32)
        if s:
            out_refs[s - 1][...] = total.astype(BF16)
        else:
            own_ref[...] = total


def transport(place, w, got, data):
    return pl.pallas_call(
        transport_kernel,
        out_shape=(jax.ShapeDtypeStruct((ROWS, SHARE), F32),)
        + (jax.ShapeDtypeStruct((ROWS, SHARE), BF16),) * (Y - 1),
        in_specs=[SMEM] + [VMEM] * 3,
        out_specs=(VMEM,) * Y,
        compiler_params=params(24),
        name="transport",
    )(place, w, got, data)


def body(noise, data):
    z, x, y, c = (lax.axis_index(a) for a in ("z", "x", "y", "core"))
    place = jnp.stack([z, x, y, c]).astype(jnp.int32)
    swapped = lax.all_to_all(data.reshape(X, QUARTER, SLICE), "x", 0, 0)
    noise_after, swapped = lax.optimization_barrier((noise, swapped))
    samples = lax.all_gather(swapped, ("z", "core")).reshape(Y, C, C, X, QUARTER, SLICE)
    samples, noise_parts = lax.optimization_barrier((samples, gather_noise(noise_after)))
    samples = lax.optimization_barrier(lax.dynamic_index_in_dim(samples, c, 1, False))
    data_all = lax.all_gather(samples, "x")
    given, sqn_mine = theirs(place, samples, noise_parts)
    got = shift(given, "core", 1)
    mine, sq_mine = ours(place, samples, noise_parts)
    q, rows, sq, sq_noise = score(mine, sq_mine, sqn_mine, got)
    for step in range(ITERS):
        if step:
            rows = noise_lse(q, columns)
        parts = lax.all_to_all(rows, ("x", "y", "core"), 0, 0)
        if step < ITERS - 1:
            columns, f = data_lse(q, parts)
            columns = lax.all_to_all(columns, "z", 0, 0)
    columns, f, *blocks = last_lse(place, q, parts, sq)
    blocks = [blocks[0]] + [shift(blocks[by], "x", by) for by in range(1, X)]
    columns = lax.all_to_all(columns, ("z", "x"), 0, 0)
    w, pot_g = scale(place, columns, blocks)
    target, *rest = transport(place, w, shift(w, "core", 1), data_all)
    for by in (2, 1, 3):
        target = target + shift(rest[by - 1], "y", by).astype(F32)
    velocity = (target - noise.astype(F32)).astype(BF16)
    own = lax.dynamic_index_in_dim(f.reshape(2, X, 128), x, 1, False)
    pot_f = (own * (EPS / LOG2E) + sq_noise / WIDTH).reshape(ROWS)
    return pot_f, pot_g.reshape(COUNT), velocity


def solution(mesh):
    fine = Mesh(mesh.devices.reshape(Z, X, Y, C), ("z", "x", "y", "core"))
    row, col = ("z", "x"), ("y", "core")
    return jax.shard_map(
        body,
        mesh=fine,
        in_specs=(P(row, col), P(col, row)),
        out_specs=(P(row), P(col), P(row, col)),
        check_vma=False,
    )
```

```python
import functools
import math

import jax
import jax.numpy as jnp
from jax import lax
from jax.experimental import pallas as pl
from jax.experimental.pallas import tpu as pltpu
from jax.sharding import Mesh, PartitionSpec as P

ITERS = 3
EPS = 0.01
LOG2E = math.log2(math.e)
Z, X, Y, C = 8, 4, 4, 2
ROWS, SHARE = 256, 512
COUNT, SLICE = 1024, 128
WIDTH = 4096
QUARTER = COUNT // X
TALL = ROWS * X
CHUNKS = TALL // 128
GROUP = X * Y * C
CUT = ROWS // 2
AROUND = (0, -1, 1, 2)
TOTAL = 8192
UNIT = LOG2E / (WIDTH * EPS)
LOG2N = math.log2(TOTAL)
F32, BF16 = jnp.float32, jnp.bfloat16
VMEM = pl.BlockSpec(memory_space=pltpu.VMEM)
SMEM = pl.BlockSpec(memory_space=pltpu.SMEM)


def shift(x, axis, by):
    n = {"z": Z, "x": X, "y": Y, "core": C}[axis]
    return lax.ppermute(x, axis, [(j, (j + by) % n) for j in range(n)])


def params(mib):
    return pltpu.CompilerParams(vmem_limit_bytes=mib * 2**20)


def both_ways(forward, backward, axis):
    return shift(forward, axis, 1), shift(backward, axis, -1)


def halves(forward, backward, axis):
    cut = forward.shape[0] // 2
    return both_ways(forward[:cut], backward[cut:], axis)


def around(block, axis):
    return [block, shift(block, axis, 1), shift(block, axis, -1), shift(block, axis, 2)]


def gather_noise(noise):
    hold = lax.optimization_barrier
    across, along = hold((around(noise[:CUT], "x"), around(noise[CUT:], "y")))
    across, along = jnp.stack(across), jnp.stack(along)
    y1, x1 = hold((both_ways(across, across, "y"), both_ways(along, along, "x")))
    return [across, *y1, *halves(*y1, "y"), along, *x1, *halves(*x1, "x")]


def squares(ref, pieces):
    total = None
    for view in pieces:
        part = ref[view].astype(F32)
        total = part * part if total is None else total + part * part
    return total


def lse(t, axis):
    top = jnp.max(t, axis=axis, keepdims=True)
    return top + jnp.log2(jnp.sum(jnp.exp2(t - top), axis=axis, keepdims=True))


def merged(ref):
    parts = ref[...]
    top = jnp.max(parts, axis=0)
    return top + jnp.log2(jnp.sum(jnp.exp2(parts - top[None]), axis=0))


def chunk(r):
    return pl.ds(r * 128, 128)


def at(place, which, rel, size):
    return lax.rem(place[which] + rel + size, size)


def blocks_of(parts):
    first, second = parts[:5], parts[5:]

    def of(five, far, near):
        if far < 3:
            return five[far].at[near]
        return five[3 + near // 2].at[near % 2]

    return (
        [[of(first, k, j) for k in range(Y)] for j in range(X)],
        [[of(second, j, k) for k in range(Y)] for j in range(X)],
    )


def collect_kernel(*refs):
    parts, (noise_ref, sqn_ref) = refs[:10], refs[10:]
    rows = []
    for h, blocks in enumerate(blocks_of(parts)):
        for j, row in enumerate(blocks):
            for k, ref in enumerate(row):
                noise_ref[pl.ds((h * X + j) * CUT, CUT), pl.ds(k * SHARE, SHARE)] = ref[...]
        t = [squares(ref, [(slice(None), pl.ds(lane, 128)) for lane in range(0, SHARE, 128)]) for ref in blocks[0]]
        total = (t[0] + t[3]) + (t[1] + t[2])
        rows.append(jnp.sum(jnp.transpose(total), axis=0, keepdims=True))
    sqn_ref[...] = jnp.concatenate(rows, axis=0)


def collect(parts):
    return pl.pallas_call(
        collect_kernel,
        out_shape=(jax.ShapeDtypeStruct((TALL, WIDTH // C), BF16), jax.ShapeDtypeStruct((2, 128), F32)),
        in_specs=[VMEM] * 10,
        out_specs=(VMEM,) * 2,
        compiler_params=params(16),
        name="collect",
    )(*parts)


def pick_kernel(place, all_ref, far_ref, near_ref, sems):
    copies = []
    for y in range(Y):
        for n, ref in enumerate((near_ref, far_ref)):
            copies.append(pltpu.make_async_copy(all_ref.at[y, place[3]], ref.at[y], sems.at[n, y]))
    for copy in copies:
        copy.start()
    for copy in copies:
        copy.wait()


def pick(place, samples):
    half = jax.ShapeDtypeStruct((Y, C, X, QUARTER, SLICE), BF16)
    return pl.pallas_call(
        pick_kernel,
        out_shape=(half, half),
        in_specs=[SMEM, pl.BlockSpec(memory_space=pl.ANY)],
        out_specs=(pl.BlockSpec(memory_space=pl.ANY), VMEM),
        scratch_shapes=[pltpu.SemaphoreType.DMA((2, Y))],
        compiler_params=params(47),
        name="pick",
    )(place, samples)


def partial_scores(place, data_ref, core, noise_ref, q_ref, sq_ref):
    pieces = [at(place, 2, rel, Y) for rel in AROUND]
    lhs = jnp.concatenate([data_ref[p, core, n] for p in pieces for n in range(X)], axis=1)
    for h in range(2):
        rhs = noise_ref[pl.ds(h * X * CUT, X * CUT), :]
        gram = lax.dot_general(lhs, rhs, (((1,), (1,)), ((), ())), preferred_element_type=F32) * (2.0 * UNIT)
        for j, rel in enumerate(AROUND):
            lanes = pl.ds(pl.multiple_of((h * X + at(place, 1, rel, X)) * 128, 128), 128)
            q_ref[:QUARTER, lanes] = gram[:, j * 128 : (j + 1) * 128]
    sq_ref[...] = squares(data_ref, [(p, core, n) for p in range(Y) for n in range(X)])


def theirs_kernel(place, data_ref, noise_ref, sqn_ref, out_ref, sq_ref):
    partial_scores(place, data_ref, 1 - place[3], noise_ref, out_ref, sq_ref)
    out_ref[:QUARTER, TALL:] = sq_ref[...]
    out_ref[QUARTER:, :] = jnp.zeros((8, TALL + 128), F32)
    out_ref[QUARTER : QUARTER + 2, :128] = sqn_ref[...]


def theirs(place, data, noise, sqn):
    return pl.pallas_call(
        theirs_kernel,
        out_shape=jax.ShapeDtypeStruct((QUARTER + 8, TALL + 128), F32),
        in_specs=[SMEM] + [VMEM] * 3,
        out_specs=VMEM,
        scratch_shapes=[pltpu.VMEM((QUARTER, 128), F32)],
        compiler_params=params(24),
        name="theirs",
    )(place, data, noise, sqn)


def ours_kernel(place, data_ref, noise_ref, q_ref, sq_ref):
    partial_scores(place, data_ref, place[3], noise_ref, q_ref, sq_ref)


def ours(place, data, noise):
    return pl.pallas_call(
        ours_kernel,
        out_shape=(jax.ShapeDtypeStruct((QUARTER, TALL), F32), jax.ShapeDtypeStruct((QUARTER, 128), F32)),
        in_specs=[SMEM] + [VMEM] * 2,
        out_specs=(VMEM,) * 2,
        compiler_params=params(24),
        cost_estimate=pl.CostEstimate(flops=QUARTER * TALL * WIDTH, bytes_accessed=6 * 2**20, transcendentals=0),
        name="ours",
    )(place, data, noise)


def score_kernel(mine_ref, sq_mine_ref, sqn_mine_ref, got_ref, q_ref, out_ref, sq_ref, sqn_ref, lse_ref):
    sq = jnp.sum(sq_mine_ref[...] + got_ref[:QUARTER, TALL:], axis=1, keepdims=True)
    sq_ref[...] = jnp.broadcast_to(sq, (QUARTER, 128))
    sqn_ref[...] = sqn_mine_ref[...] + got_ref[QUARTER : QUARTER + 2, :128]
    for r in range(CHUNKS):
        q = mine_ref[:, chunk(r)] + got_ref[:QUARTER, chunk(r)]
        q_ref[:, chunk(r)] = q
        lse_ref[pl.ds(r, 1), :] = lse(q - UNIT * sq_ref[...], 0)
    out_ref[...] = jnp.broadcast_to(lse_ref[...][None], (GROUP, CHUNKS, 128))


def score(mine, sq_mine, sqn_mine, got):
    return pl.pallas_call(
        score_kernel,
        out_shape=(
            jax.ShapeDtypeStruct((QUARTER, TALL), F32),
            jax.ShapeDtypeStruct((GROUP, CHUNKS, 128), F32),
            jax.ShapeDtypeStruct((QUARTER, 128), F32),
            jax.ShapeDtypeStruct((2, 128), F32),
        ),
        in_specs=[VMEM] * 4,
        out_specs=(VMEM,) * 4,
        scratch_shapes=[pltpu.VMEM((CHUNKS, 128), F32)],
        compiler_params=params(16),
        name="score",
    )(mine, sq_mine, sqn_mine, got)


def to_column(g):
    return jnp.concatenate([jnp.transpose(jnp.broadcast_to(g[r : r + 1], (128, 128))) for r in range(2)], axis=0)


def noise_kernel(q_ref, part_ref, out_ref, lse_ref, g_ref):
    g_ref[...] = to_column(-LOG2N - merged(part_ref))
    for r in range(CHUNKS):
        lse_ref[pl.ds(r, 1), :] = lse(q_ref[:, chunk(r)] + g_ref[...], 0)
    out_ref[...] = jnp.broadcast_to(lse_ref[...][None], (GROUP, CHUNKS, 128))


def noise_lse(q, parts):
    return pl.pallas_call(
        noise_kernel,
        out_shape=jax.ShapeDtypeStruct((GROUP, CHUNKS, 128), F32),
        in_specs=[VMEM] * 2,
        out_specs=VMEM,
        scratch_shapes=[pltpu.VMEM((CHUNKS, 128), F32), pltpu.VMEM((QUARTER, 128), F32)],
        compiler_params=params(16),
        name="noise_lse",
    )(q, parts)


def data_kernel(q_ref, part_ref, out_ref, f_ref, lane_ref):
    f_ref[...] = -LOG2N - merged(part_ref)
    row = data_row(q_ref, f_ref, lane_ref)
    out_ref[...] = jnp.broadcast_to(two_rows(row)[None], (Z, 8, 128))


def data_row(q_ref, f_ref, lane_ref):
    step = 32
    for start in range(0, QUARTER, step):
        rows = pl.ds(start, step)
        t = [q_ref[rows, chunk(r)] + f_ref[pl.ds(r, 1), :] for r in range(CHUNKS)]
        top = functools.reduce(jnp.maximum, t)
        lane_ref[rows, :] = top + jnp.log2(sum(jnp.exp2(part - top) for part in t))
    return lse(jnp.transpose(lane_ref[...]), 0)


def two_rows(*rows):
    halves = [half for row in rows for half in (row[:, :128], row[:, 128:])]
    return jnp.concatenate(halves + [jnp.zeros((8 - len(halves), 128), F32)], axis=0)


def data_lse(q, parts):
    return pl.pallas_call(
        data_kernel,
        out_shape=(jax.ShapeDtypeStruct((Z, 8, 128), F32), jax.ShapeDtypeStruct((CHUNKS, 128), F32)),
        in_specs=[VMEM] * 2,
        out_specs=(VMEM, VMEM),
        scratch_shapes=[pltpu.VMEM((QUARTER, 128), F32)],
        compiler_params=params(16),
        name="data_lse",
    )(q, parts)


def last_kernel(place, q_ref, part_ref, sq_ref, out_ref, f_ref, *refs):
    w_refs, lane_ref = refs[:X], refs[X]
    f_ref[...] = -LOG2N - merged(part_ref)
    tile = two_rows(data_row(q_ref, f_ref, lane_ref), jnp.transpose(sq_ref[...])[0:1, :])
    out_ref[...] = jnp.broadcast_to(tile[None], (Z * X, 8, 128))
    column = to_column(tile)
    for by in range(X):
        block = lax.rem(place[1] + by, X)
        for h in range(2):
            lanes = pl.ds(pl.multiple_of((h * X + block) * 128, 128), 128)
            w = jnp.exp2((q_ref[:, lanes] + f_ref[pl.ds(h * X + block, 1), :]) - column)
            w_refs[by][:, pl.ds(h * 128, 128)] = w.astype(BF16)


def last_lse(place, q, parts, sq):
    return pl.pallas_call(
        last_kernel,
        out_shape=(jax.ShapeDtypeStruct((Z * X, 8, 128), F32), jax.ShapeDtypeStruct((CHUNKS, 128), F32))
        + (jax.ShapeDtypeStruct((QUARTER, ROWS), BF16),) * X,
        in_specs=[SMEM] + [VMEM] * 3,
        out_specs=(VMEM,) * (2 + X),
        scratch_shapes=[pltpu.VMEM((QUARTER, 128), F32)],
        compiler_params=params(16),
        name="last_lse",
    )(place, q, parts, sq)


def scale_kernel(place, part_ref, *refs):
    w_refs, (w_ref, pot_ref) = refs[:X], refs[X:]
    z, x = place[0], place[1]
    for n in range(X):
        parts = jnp.stack([part_ref[k * X + n, 0:4, :] for k in range(Z)])
        top = jnp.max(parts, axis=0)
        total = top + jnp.log2(jnp.sum(jnp.exp2(parts - top[None]), axis=0))
        pot_ref[pl.ds(2 * n, 2), :] = (-LOG2N - total[0:2]) * (EPS / LOG2E) + parts[0, 2:4] * (1.0 / WIDTH)
    for by in range(X):
        n = lax.rem(x - by + X, X)
        parts = jnp.stack([part_ref[k * X + n] for k in range(Z)])
        top = jnp.max(parts, axis=0)
        total = top + jnp.log2(jnp.sum(jnp.exp2(parts - top[None]), axis=0))
        factor = jnp.exp2(part_ref[z * X + n] - total)
        factor = jnp.concatenate([factor[0:1], factor[1:2]], axis=1)
        lanes = pl.ds(pl.multiple_of(n * QUARTER, QUARTER), QUARTER)
        for h in range(2):
            w = jnp.transpose(w_refs[by][:, pl.ds(h * 128, 128)].astype(F32)) * factor
            w_ref[pl.ds(h * 128, 128), lanes] = w.astype(BF16)


def scale(place, parts, blocks):
    return pl.pallas_call(
        scale_kernel,
        out_shape=(jax.ShapeDtypeStruct((ROWS, COUNT), BF16), jax.ShapeDtypeStruct((2 * X, 128), F32)),
        in_specs=[SMEM] + [VMEM] * (1 + X),
        out_specs=(VMEM,) * 2,
        compiler_params=params(16),
        name="scale",
    )(place, parts, *blocks)


def transport_kernel(pieces, place, w_ref, got_ref, data_ref, *out_refs):
    lhs = jnp.concatenate([w_ref[...], got_ref[...]], axis=1)
    for s, out_ref in zip(pieces, out_refs):
        y = at(place, 2, s, Y)
        rhs = []
        for core in (place[3], 1 - place[3]):
            for n in range(X):
                rhs.append(jnp.concatenate([data_ref[n, y, core, k] for k in range(X)], axis=1))
        total = jnp.dot(lhs, jnp.concatenate(rhs, axis=0), preferred_element_type=F32)
        out_ref[...] = total.astype(out_ref.dtype)


def transport(place, w, got, data, pieces, hand_on):
    kinds = [jax.ShapeDtypeStruct((ROWS, SHARE), BF16 if s else F32) for s in pieces]
    if hand_on:
        kinds.append(jax.ShapeDtypeStruct(data.shape, data.dtype))
    return pl.pallas_call(
        functools.partial(transport_kernel, pieces),
        out_shape=kinds,
        in_specs=[SMEM] + [VMEM] * 3,
        out_specs=[VMEM] * len(kinds),
        input_output_aliases={3: len(pieces)} if hand_on else {},
        compiler_params=params(24),
        cost_estimate=pl.CostEstimate(
            flops=2 * ROWS * COUNT * C * SHARE * len(pieces), bytes_accessed=2 * 2**20 * len(pieces), transcendentals=0
        ),
        name="transport",
    )(place, w, got, data)


def body(noise, data):
    z, x, y, c = (lax.axis_index(a) for a in ("z", "x", "y", "core"))
    place = jnp.stack([z, x, y, c]).astype(jnp.int32)
    swapped = lax.all_to_all(data.reshape(X, QUARTER, SLICE), "x", 0, 0)
    noise_after, swapped = lax.optimization_barrier((noise, swapped))
    samples = lax.all_gather(swapped, ("z", "core")).reshape(Y, C, C, X, QUARTER, SLICE)
    samples, noise_all, sqn_mine = lax.optimization_barrier((samples, *collect(gather_noise(noise_after))))
    far, near = pick(place, samples)
    data_all = lax.all_gather(far, "x")
    got = shift(theirs(place, near, noise_all, sqn_mine), "core", 1)
    mine, sq_mine = ours(place, near, noise_all)
    q, rows, sq, sq_noise = score(mine, sq_mine, sqn_mine, got)
    for step in range(ITERS):
        if step:
            rows = noise_lse(q, columns)
        parts = lax.all_to_all(rows, ("x", "y", "core"), 0, 0)
        if step < ITERS - 1:
            columns, f = data_lse(q, parts)
            columns = lax.all_to_all(columns, "z", 0, 0)
    columns, f, *blocks = last_lse(place, q, parts, sq)
    blocks = [blocks[0]] + [shift(blocks[by], "x", by) for by in range(1, X)]
    columns = lax.all_to_all(columns, ("z", "x"), 0, 0)
    data_all, blocks = lax.optimization_barrier((data_all, blocks))
    w, pot_g = scale(place, columns, blocks)
    got = shift(w, "core", 1)
    *parts, data_all = transport(place, w, got, data_all, (2, 1, 3), True)
    (target,) = transport(place, w, got, data_all, (0,), False)
    for by, part in zip((2, 1, 3), parts):
        target = target + shift(part, "y", by).astype(F32)
    velocity = (target - noise.astype(F32)).astype(BF16)
    own = lax.dynamic_index_in_dim(f.reshape(2, X, 128), x, 1, False)
    pot_f = (own * (EPS / LOG2E) + sq_noise / WIDTH).reshape(ROWS)
    return pot_f, pot_g.reshape(COUNT), velocity


def solution(mesh):
    fine = Mesh(mesh.devices.reshape(Z, X, Y, C), ("z", "x", "y", "core"))
    row, col = ("z", "x"), ("y", "core")
    return jax.shard_map(
        body,
        mesh=fine,
        in_specs=(P(row, col), P(col, row)),
        out_specs=(P(row), P(col), P(row, col)),
        check_vma=False,
    )
```

```python
import functools
import math

import jax
import jax.numpy as jnp
from jax import lax
from jax.experimental import pallas as pl
from jax.experimental.pallas import tpu as pltpu
from jax.sharding import Mesh, PartitionSpec as P

ITERS = 3
EPS = 0.01
LOG2E = math.log2(math.e)
Z, X, Y, C = 8, 4, 4, 2
ROWS, SHARE = 256, 512
COUNT, SLICE = 1024, 128
WIDTH = 4096
QUARTER = COUNT // X
TALL = ROWS * X
CHUNKS = TALL // 128
GROUP = X * Y * C
CUT = ROWS // 2
AROUND = (0, -1, 1, 2)
TOTAL = 8192
UNIT = LOG2E / (WIDTH * EPS)
LOG2N = math.log2(TOTAL)
F32, BF16 = jnp.float32, jnp.bfloat16
VMEM = pl.BlockSpec(memory_space=pltpu.VMEM)
SMEM = pl.BlockSpec(memory_space=pltpu.SMEM)


def shift(x, axis, by):
    n = {"z": Z, "x": X, "y": Y, "core": C}[axis]
    return lax.ppermute(x, axis, [(j, (j + by) % n) for j in range(n)])


def params(mib):
    return pltpu.CompilerParams(vmem_limit_bytes=mib * 2**20)


def both_ways(forward, backward, axis):
    return shift(forward, axis, 1), shift(backward, axis, -1)


def halves(forward, backward, axis):
    cut = forward.shape[0] // 2
    return both_ways(forward[:cut], backward[cut:], axis)


def around(block, axis):
    return [block, shift(block, axis, 1), shift(block, axis, -1), shift(block, axis, 2)]


def gather_noise(noise):
    hold = lax.optimization_barrier
    across, along = hold((around(noise[:CUT], "x"), around(noise[CUT:], "y")))
    across, along = jnp.stack(across), jnp.stack(along)
    y1, x1 = hold((both_ways(across, across, "y"), both_ways(along, along, "x")))
    return [across, *y1, *halves(*y1, "y"), along, *x1, *halves(*x1, "x")]


def squares(ref, pieces):
    total = None
    for view in pieces:
        part = ref[view].astype(F32)
        total = part * part if total is None else total + part * part
    return total


def lse(t, axis):
    top = jnp.max(t, axis=axis, keepdims=True)
    return top + jnp.log2(jnp.sum(jnp.exp2(t - top), axis=axis, keepdims=True))


def merged(ref):
    parts = ref[...]
    top = jnp.max(parts, axis=0)
    return top + jnp.log2(jnp.sum(jnp.exp2(parts - top[None]), axis=0))


def chunk(r):
    return pl.ds(r * 128, 128)


def at(place, which, rel, size):
    return lax.rem(place[which] + rel + size, size)


def blocks_of(parts):
    first, second = parts[:5], parts[5:]

    def of(five, far, near):
        if far < 3:
            return five[far].at[near]
        return five[3 + near // 2].at[near % 2]

    return (
        [[of(first, k, j) for k in range(Y)] for j in range(X)],
        [[of(second, j, k) for k in range(Y)] for j in range(X)],
    )


def collect_kernel(*refs):
    parts, (noise_ref, sqn_ref) = refs[:10], refs[10:]
    rows = []
    for h, blocks in enumerate(blocks_of(parts)):
        for j, row in enumerate(blocks):
            for k, ref in enumerate(row):
                noise_ref[pl.ds((h * X + j) * CUT, CUT), pl.ds(k * SHARE, SHARE)] = ref[...]
        t = [squares(ref, [(slice(None), pl.ds(lane, 128)) for lane in range(0, SHARE, 128)]) for ref in blocks[0]]
        total = (t[0] + t[3]) + (t[1] + t[2])
        rows.append(jnp.sum(jnp.transpose(total), axis=0, keepdims=True))
    sqn_ref[...] = jnp.concatenate(rows, axis=0)


def collect(parts):
    return pl.pallas_call(
        collect_kernel,
        out_shape=(jax.ShapeDtypeStruct((TALL, WIDTH // C), BF16), jax.ShapeDtypeStruct((2, 128), F32)),
        in_specs=[VMEM] * 10,
        out_specs=(VMEM,) * 2,
        compiler_params=params(16),
        name="collect",
    )(*parts)


def pick_kernel(place, all_ref, far_ref, near_ref, sems):
    copies = []
    for y in range(Y):
        for n, ref in enumerate((near_ref, far_ref)):
            copies.append(pltpu.make_async_copy(all_ref.at[y, place[3]], ref.at[y], sems.at[n, y]))
    for copy in copies:
        copy.start()
    for copy in copies:
        copy.wait()


def pick(place, samples):
    half = jax.ShapeDtypeStruct((Y, C, X, QUARTER, SLICE), BF16)
    return pl.pallas_call(
        pick_kernel,
        out_shape=(half, half),
        in_specs=[SMEM, pl.BlockSpec(memory_space=pl.ANY)],
        out_specs=(pl.BlockSpec(memory_space=pl.ANY), VMEM),
        scratch_shapes=[pltpu.SemaphoreType.DMA((2, Y))],
        compiler_params=params(16),
        name="pick",
    )(place, samples)


def partial_scores(place, data_ref, core, noise_ref, q_ref, sq_ref):
    pieces = [at(place, 2, rel, Y) for rel in AROUND]
    lhs = jnp.concatenate([data_ref[p, core, n] for p in pieces for n in range(X)], axis=1)
    for h in range(2):
        rhs = noise_ref[pl.ds(h * X * CUT, X * CUT), :]
        gram = lax.dot_general(lhs, rhs, (((1,), (1,)), ((), ())), preferred_element_type=F32) * (2.0 * UNIT)
        for j, rel in enumerate(AROUND):
            lanes = pl.ds(pl.multiple_of((h * X + at(place, 1, rel, X)) * 128, 128), 128)
            q_ref[:QUARTER, lanes] = gram[:, j * 128 : (j + 1) * 128]
    sq_ref[...] = squares(data_ref, [(p, core, n) for p in range(Y) for n in range(X)])


def theirs_kernel(place, data_ref, noise_ref, sqn_ref, out_ref, sq_ref):
    partial_scores(place, data_ref, 1 - place[3], noise_ref, out_ref, sq_ref)
    out_ref[:QUARTER, TALL:] = sq_ref[...]
    out_ref[QUARTER:, :] = jnp.zeros((8, TALL + 128), F32)
    out_ref[QUARTER : QUARTER + 2, :128] = sqn_ref[...]


def theirs(place, data, noise, sqn):
    return pl.pallas_call(
        theirs_kernel,
        out_shape=jax.ShapeDtypeStruct((QUARTER + 8, TALL + 128), F32),
        in_specs=[SMEM] + [VMEM] * 3,
        out_specs=VMEM,
        scratch_shapes=[pltpu.VMEM((QUARTER, 128), F32)],
        compiler_params=params(24),
        name="theirs",
    )(place, data, noise, sqn)


def ours_kernel(place, data_ref, noise_ref, q_ref, sq_ref):
    partial_scores(place, data_ref, place[3], noise_ref, q_ref, sq_ref)


def ours(place, data, noise):
    return pl.pallas_call(
        ours_kernel,
        out_shape=(jax.ShapeDtypeStruct((QUARTER, TALL), F32), jax.ShapeDtypeStruct((QUARTER, 128), F32)),
        in_specs=[SMEM] + [VMEM] * 2,
        out_specs=(VMEM,) * 2,
        compiler_params=params(24),
        cost_estimate=pl.CostEstimate(flops=QUARTER * TALL * WIDTH, bytes_accessed=6 * 2**20, transcendentals=0),
        name="ours",
    )(place, data, noise)


def score_kernel(mine_ref, sq_mine_ref, sqn_mine_ref, got_ref, q_ref, out_ref, sq_ref, sqn_ref, lse_ref):
    sq = jnp.sum(sq_mine_ref[...] + got_ref[:QUARTER, TALL:], axis=1, keepdims=True)
    sq_ref[...] = jnp.broadcast_to(sq, (QUARTER, 128))
    sqn_ref[...] = sqn_mine_ref[...] + got_ref[QUARTER : QUARTER + 2, :128]
    for r in range(CHUNKS):
        q = mine_ref[:, chunk(r)] + got_ref[:QUARTER, chunk(r)]
        q_ref[:, chunk(r)] = q
        lse_ref[pl.ds(r, 1), :] = lse(q - UNIT * sq_ref[...], 0)
    out_ref[...] = jnp.broadcast_to(lse_ref[...][None], (GROUP, CHUNKS, 128))


def score(mine, sq_mine, sqn_mine, got):
    return pl.pallas_call(
        score_kernel,
        out_shape=(
            jax.ShapeDtypeStruct((QUARTER, TALL), F32),
            jax.ShapeDtypeStruct((GROUP, CHUNKS, 128), F32),
            jax.ShapeDtypeStruct((QUARTER, 128), F32),
            jax.ShapeDtypeStruct((2, 128), F32),
        ),
        in_specs=[VMEM] * 4,
        out_specs=(VMEM,) * 4,
        scratch_shapes=[pltpu.VMEM((CHUNKS, 128), F32)],
        compiler_params=params(16),
        name="score",
    )(mine, sq_mine, sqn_mine, got)


def to_column(g):
    return jnp.concatenate([jnp.transpose(jnp.broadcast_to(g[r : r + 1], (128, 128))) for r in range(2)], axis=0)


def noise_kernel(q_ref, part_ref, out_ref, lse_ref, g_ref):
    g_ref[...] = to_column(-LOG2N - merged(part_ref))
    for r in range(CHUNKS):
        lse_ref[pl.ds(r, 1), :] = lse(q_ref[:, chunk(r)] + g_ref[...], 0)
    out_ref[...] = jnp.broadcast_to(lse_ref[...][None], (GROUP, CHUNKS, 128))


def noise_lse(q, parts):
    return pl.pallas_call(
        noise_kernel,
        out_shape=jax.ShapeDtypeStruct((GROUP, CHUNKS, 128), F32),
        in_specs=[VMEM] * 2,
        out_specs=VMEM,
        scratch_shapes=[pltpu.VMEM((CHUNKS, 128), F32), pltpu.VMEM((QUARTER, 128), F32)],
        compiler_params=params(16),
        name="noise_lse",
    )(q, parts)


def data_kernel(q_ref, part_ref, out_ref, f_ref, lane_ref):
    f_ref[...] = -LOG2N - merged(part_ref)
    row = data_row(q_ref, f_ref, lane_ref)
    out_ref[...] = jnp.broadcast_to(two_rows(row)[None], (Z, 8, 128))


def data_row(q_ref, f_ref, lane_ref):
    step = 32
    for start in range(0, QUARTER, step):
        rows = pl.ds(start, step)
        t = [q_ref[rows, chunk(r)] + f_ref[pl.ds(r, 1), :] for r in range(CHUNKS)]
        top = functools.reduce(jnp.maximum, t)
        lane_ref[rows, :] = top + jnp.log2(sum(jnp.exp2(part - top) for part in t))
    return lse(jnp.transpose(lane_ref[...]), 0)


def two_rows(*rows):
    halves = [half for row in rows for half in (row[:, :128], row[:, 128:])]
    return jnp.concatenate(halves + [jnp.zeros((8 - len(halves), 128), F32)], axis=0)


def data_lse(q, parts):
    return pl.pallas_call(
        data_kernel,
        out_shape=(jax.ShapeDtypeStruct((Z, 8, 128), F32), jax.ShapeDtypeStruct((CHUNKS, 128), F32)),
        in_specs=[VMEM] * 2,
        out_specs=(VMEM, VMEM),
        scratch_shapes=[pltpu.VMEM((QUARTER, 128), F32)],
        compiler_params=params(16),
        name="data_lse",
    )(q, parts)


def last_kernel(place, q_ref, part_ref, sq_ref, out_ref, f_ref, *refs):
    w_refs, lane_ref = refs[:X], refs[X]
    f_ref[...] = -LOG2N - merged(part_ref)
    tile = two_rows(data_row(q_ref, f_ref, lane_ref), jnp.transpose(sq_ref[...])[0:1, :])
    out_ref[...] = jnp.broadcast_to(tile[None], (Z * X, 8, 128))
    column = to_column(tile)
    for by in range(X):
        block = lax.rem(place[1] + by, X)
        for h in range(2):
            lanes = pl.ds(pl.multiple_of((h * X + block) * 128, 128), 128)
            w = jnp.exp2((q_ref[:, lanes] + f_ref[pl.ds(h * X + block, 1), :]) - column)
            w_refs[by][:, pl.ds(h * 128, 128)] = w.astype(BF16)


def last_lse(place, q, parts, sq):
    return pl.pallas_call(
        last_kernel,
        out_shape=(jax.ShapeDtypeStruct((Z * X, 8, 128), F32), jax.ShapeDtypeStruct((CHUNKS, 128), F32))
        + (jax.ShapeDtypeStruct((QUARTER, ROWS), BF16),) * X,
        in_specs=[SMEM] + [VMEM] * 3,
        out_specs=(VMEM,) * (2 + X),
        scratch_shapes=[pltpu.VMEM((QUARTER, 128), F32)],
        compiler_params=params(16),
        name="last_lse",
    )(place, q, parts, sq)


def scale_kernel(place, part_ref, *refs):
    w_refs, (w_ref, pot_ref) = refs[:X], refs[X:]
    z, x = place[0], place[1]
    for n in range(X):
        parts = jnp.stack([part_ref[k * X + n, 0:4, :] for k in range(Z)])
        top = jnp.max(parts, axis=0)
        total = top + jnp.log2(jnp.sum(jnp.exp2(parts - top[None]), axis=0))
        pot_ref[pl.ds(2 * n, 2), :] = (-LOG2N - total[0:2]) * (EPS / LOG2E) + parts[0, 2:4] * (1.0 / WIDTH)
    for by in range(X):
        n = lax.rem(x - by + X, X)
        parts = jnp.stack([part_ref[k * X + n] for k in range(Z)])
        top = jnp.max(parts, axis=0)
        total = top + jnp.log2(jnp.sum(jnp.exp2(parts - top[None]), axis=0))
        factor = jnp.exp2(part_ref[z * X + n] - total)
        factor = jnp.concatenate([factor[0:1], factor[1:2]], axis=1)
        lanes = pl.ds(pl.multiple_of(n * QUARTER, QUARTER), QUARTER)
        for h in range(2):
            w = jnp.transpose(w_refs[by][:, pl.ds(h * 128, 128)].astype(F32)) * factor
            w_ref[pl.ds(h * 128, 128), lanes] = w.astype(BF16)


def scale(place, parts, blocks):
    return pl.pallas_call(
        scale_kernel,
        out_shape=(jax.ShapeDtypeStruct((ROWS, COUNT), BF16), jax.ShapeDtypeStruct((2 * X, 128), F32)),
        in_specs=[SMEM] + [VMEM] * (1 + X),
        out_specs=(VMEM,) * 2,
        compiler_params=params(16),
        name="scale",
    )(place, parts, *blocks)


def transport_kernel(pieces, place, w_ref, got_ref, data_ref, *out_refs):
    lhs = jnp.concatenate([w_ref[...], got_ref[...]], axis=1)
    for s, out_ref in zip(pieces, out_refs):
        y = at(place, 2, s, Y)
        rhs = []
        for core in (place[3], 1 - place[3]):
            for n in range(X):
                rhs.append(jnp.concatenate([data_ref[n, y, core, k] for k in range(X)], axis=1))
        total = jnp.dot(lhs, jnp.concatenate(rhs, axis=0), preferred_element_type=F32)
        out_ref[...] = total.astype(out_ref.dtype)


def transport(place, w, got, data, pieces, hand_on):
    kinds = [jax.ShapeDtypeStruct((ROWS, SHARE), BF16 if s else F32) for s in pieces]
    if hand_on:
        kinds.append(jax.ShapeDtypeStruct(data.shape, data.dtype))
    return pl.pallas_call(
        functools.partial(transport_kernel, pieces),
        out_shape=kinds,
        in_specs=[SMEM] + [VMEM] * 3,
        out_specs=[VMEM] * len(kinds),
        input_output_aliases={3: len(pieces)} if hand_on else {},
        compiler_params=params(24),
        cost_estimate=pl.CostEstimate(
            flops=2 * ROWS * COUNT * C * SHARE * len(pieces), bytes_accessed=2 * 2**20 * len(pieces), transcendentals=0
        ),
        name="transport",
    )(place, w, got, data)


def body(noise, data):
    z, x, y, c = (lax.axis_index(a) for a in ("z", "x", "y", "core"))
    place = jnp.stack([z, x, y, c]).astype(jnp.int32)
    swapped = lax.all_to_all(data.reshape(X, QUARTER, SLICE), "x", 0, 0)
    noise_after, swapped = lax.optimization_barrier((noise, swapped))
    samples = lax.all_gather(swapped, ("z", "core")).reshape(Y, C, C, X, QUARTER, SLICE)
    samples, noise_all, sqn_mine = lax.optimization_barrier((samples, *collect(gather_noise(noise_after))))
    far, near = pick(place, samples)
    data_all = lax.all_gather(far, "x")
    got = shift(theirs(place, near, noise_all, sqn_mine), "core", 1)
    mine, sq_mine = ours(place, near, noise_all)
    q, rows, sq, sq_noise = score(mine, sq_mine, sqn_mine, got)
    for step in range(ITERS):
        if step:
            rows = noise_lse(q, columns)
        parts = lax.all_to_all(rows, ("x", "y", "core"), 0, 0)
        if step < ITERS - 1:
            columns, f = data_lse(q, parts)
            columns = lax.all_to_all(columns, "z", 0, 0)
    columns, f, *blocks = last_lse(place, q, parts, sq)
    blocks = [blocks[0]] + [shift(blocks[by], "x", by) for by in range(1, X)]
    columns = lax.all_to_all(columns, ("z", "x"), 0, 0)
    w, pot_g = scale(place, columns, blocks)
    data_all, pot_g = lax.optimization_barrier((data_all, pot_g))
    got = shift(w, "core", 1)
    *parts, data_all = transport(place, w, got, data_all, (2, 1, 3), True)
    (target,) = transport(place, w, got, data_all, (0,), False)
    for by, part in zip((2, 1, 3), parts):
        target = target + shift(part, "y", by).astype(F32)
    velocity = (target - noise.astype(F32)).astype(BF16)
    own = lax.dynamic_index_in_dim(f.reshape(2, X, 128), x, 1, False)
    pot_f = (own * (EPS / LOG2E) + sq_noise / WIDTH).reshape(ROWS)
    return pot_f, pot_g.reshape(COUNT), velocity


def solution(mesh):
    fine = Mesh(mesh.devices.reshape(Z, X, Y, C), ("z", "x", "y", "core"))
    row, col = ("z", "x"), ("y", "core")
    return jax.shard_map(
        body,
        mesh=fine,
        in_specs=(P(row, col), P(col, row)),
        out_specs=(P(row), P(col), P(row, col)),
        check_vma=False,
    )
```

```python
import functools
import math

import jax
import jax.numpy as jnp
from jax import lax
from jax.experimental import pallas as pl
from jax.experimental.pallas import tpu as pltpu
from jax.sharding import Mesh, PartitionSpec as P

ITERS = 3
EPS = 0.01
LOG2E = math.log2(math.e)
Z, X, Y, C = 8, 4, 4, 2
ROWS, SHARE = 256, 512
COUNT, SLICE = 1024, 128
WIDTH = 4096
QUARTER = COUNT // X
TALL = ROWS * X
CHUNKS = TALL // 128
GROUP = X * Y * C
CUT = ROWS // 2
AROUND = (0, -1, 1, 2)
TOTAL = 8192
UNIT = LOG2E / (WIDTH * EPS)
LOG2N = math.log2(TOTAL)
F32, BF16 = jnp.float32, jnp.bfloat16
VMEM = pl.BlockSpec(memory_space=pltpu.VMEM)
SMEM = pl.BlockSpec(memory_space=pltpu.SMEM)


def shift(x, axis, by):
    n = {"z": Z, "x": X, "y": Y, "core": C}[axis]
    return lax.ppermute(x, axis, [(j, (j + by) % n) for j in range(n)])


def params(mib):
    return pltpu.CompilerParams(vmem_limit_bytes=mib * 2**20)


def both_ways(forward, backward, axis):
    return shift(forward, axis, 1), shift(backward, axis, -1)


def halves(forward, backward, axis):
    cut = forward.shape[0] // 2
    return both_ways(forward[:cut], backward[cut:], axis)


def around(block, axis):
    return [block, shift(block, axis, 1), shift(block, axis, -1), shift(block, axis, 2)]


def gather_noise(noise):
    hold = lax.optimization_barrier
    across, along = hold((around(noise[:CUT], "x"), around(noise[CUT:], "y")))
    across, along = jnp.stack(across), jnp.stack(along)
    y1, x1 = hold((both_ways(across, across, "y"), both_ways(along, along, "x")))
    return [across, *y1, *halves(*y1, "y"), along, *x1, *halves(*x1, "x")]


def squares(ref, pieces):
    total = None
    for view in pieces:
        part = ref[view].astype(F32)
        total = part * part if total is None else total + part * part
    return total


def lse(t, axis):
    top = jnp.max(t, axis=axis, keepdims=True)
    return top + jnp.log2(jnp.sum(jnp.exp2(t - top), axis=axis, keepdims=True))


def merged(ref):
    parts = ref[...]
    top = jnp.max(parts, axis=0)
    return top + jnp.log2(jnp.sum(jnp.exp2(parts - top[None]), axis=0))


def chunk(r):
    return pl.ds(r * 128, 128)


def at(place, which, rel, size):
    return lax.rem(place[which] + rel + size, size)


def blocks_of(parts):
    first, second = parts[:5], parts[5:]

    def of(five, far, near):
        if far < 3:
            return five[far].at[near]
        return five[3 + near // 2].at[near % 2]

    return (
        [[of(first, k, j) for k in range(Y)] for j in range(X)],
        [[of(second, j, k) for k in range(Y)] for j in range(X)],
    )


def collect_kernel(*refs):
    parts, (noise_ref, sqn_ref) = refs[:10], refs[10:]
    rows = []
    for h, blocks in enumerate(blocks_of(parts)):
        for j, row in enumerate(blocks):
            for k, ref in enumerate(row):
                noise_ref[pl.ds((h * X + j) * CUT, CUT), pl.ds(k * SHARE, SHARE)] = ref[...]
        t = [squares(ref, [(slice(None), pl.ds(lane, 128)) for lane in range(0, SHARE, 128)]) for ref in blocks[0]]
        total = (t[0] + t[3]) + (t[1] + t[2])
        rows.append(jnp.sum(jnp.transpose(total), axis=0, keepdims=True))
    sqn_ref[...] = jnp.concatenate(rows, axis=0)


def collect(parts):
    return pl.pallas_call(
        collect_kernel,
        out_shape=(jax.ShapeDtypeStruct((TALL, WIDTH // C), BF16), jax.ShapeDtypeStruct((2, 128), F32)),
        in_specs=[VMEM] * 10,
        out_specs=(VMEM,) * 2,
        compiler_params=params(16),
        name="collect",
    )(*parts)


def pick_kernel(place, all_ref, far_ref, side_ref, near_ref, sems):
    copies = []
    for y in range(Y):
        own = all_ref.at[y, place[3]]
        copies.append(pltpu.make_async_copy(own, near_ref.at[y], sems.at[0, y]))
        copies.append(pltpu.make_async_copy(own.at[:, : X - 1], far_ref.at[y], sems.at[1, y]))
        copies.append(pltpu.make_async_copy(own.at[:, X - 1], side_ref.at[y], sems.at[2, y]))
    for copy in copies:
        copy.start()
    for copy in copies:
        copy.wait()


def pick(place, samples):
    return pl.pallas_call(
        pick_kernel,
        out_shape=(
            jax.ShapeDtypeStruct((Y, C, X - 1, QUARTER, SLICE), BF16),
            jax.ShapeDtypeStruct((Y, C, QUARTER, SLICE), BF16),
            jax.ShapeDtypeStruct((Y, C, X, QUARTER, SLICE), BF16),
        ),
        in_specs=[SMEM, pl.BlockSpec(memory_space=pl.ANY)],
        out_specs=(pl.BlockSpec(memory_space=pl.ANY), pl.BlockSpec(memory_space=pl.ANY), VMEM),
        scratch_shapes=[pltpu.SemaphoreType.DMA((3, Y))],
        compiler_params=params(16),
        name="pick",
    )(place, samples)


def partial_scores(place, data_ref, core, noise_ref, q_ref, sq_ref):
    pieces = [at(place, 2, rel, Y) for rel in AROUND]
    lhs = jnp.concatenate([data_ref[p, core, n] for p in pieces for n in range(X)], axis=1)
    for h in range(2):
        rhs = noise_ref[pl.ds(h * X * CUT, X * CUT), :]
        gram = lax.dot_general(lhs, rhs, (((1,), (1,)), ((), ())), preferred_element_type=F32) * (2.0 * UNIT)
        for j, rel in enumerate(AROUND):
            lanes = pl.ds(pl.multiple_of((h * X + at(place, 1, rel, X)) * 128, 128), 128)
            q_ref[:QUARTER, lanes] = gram[:, j * 128 : (j + 1) * 128]
    sq_ref[...] = squares(data_ref, [(p, core, n) for p in range(Y) for n in range(X)])


def theirs_kernel(place, data_ref, noise_ref, sqn_ref, out_ref, sq_ref):
    partial_scores(place, data_ref, 1 - place[3], noise_ref, out_ref, sq_ref)
    out_ref[:QUARTER, TALL:] = sq_ref[...]
    out_ref[QUARTER:, :] = jnp.zeros((8, TALL + 128), F32)
    out_ref[QUARTER : QUARTER + 2, :128] = sqn_ref[...]


def theirs(place, data, noise, sqn):
    return pl.pallas_call(
        theirs_kernel,
        out_shape=jax.ShapeDtypeStruct((QUARTER + 8, TALL + 128), F32),
        in_specs=[SMEM] + [VMEM] * 3,
        out_specs=VMEM,
        scratch_shapes=[pltpu.VMEM((QUARTER, 128), F32)],
        compiler_params=params(24),
        name="theirs",
    )(place, data, noise, sqn)


def ours_kernel(place, data_ref, noise_ref, q_ref, sq_ref):
    partial_scores(place, data_ref, place[3], noise_ref, q_ref, sq_ref)


def ours(place, data, noise):
    return pl.pallas_call(
        ours_kernel,
        out_shape=(jax.ShapeDtypeStruct((QUARTER, TALL), F32), jax.ShapeDtypeStruct((QUARTER, 128), F32)),
        in_specs=[SMEM] + [VMEM] * 2,
        out_specs=(VMEM,) * 2,
        compiler_params=params(24),
        cost_estimate=pl.CostEstimate(flops=QUARTER * TALL * WIDTH, bytes_accessed=6 * 2**20, transcendentals=0),
        name="ours",
    )(place, data, noise)


def score_kernel(place, mine_ref, sq_mine_ref, sqn_mine_ref, got_ref, q_ref, out_ref, sq_ref, sqn_ref, *refs):
    block_refs, lse_ref = refs[:X], refs[X]
    sq = jnp.sum(sq_mine_ref[...] + got_ref[:QUARTER, TALL:], axis=1, keepdims=True)
    sq_ref[...] = jnp.broadcast_to(sq, (QUARTER, 128))
    sqn_ref[...] = sqn_mine_ref[...] + got_ref[QUARTER : QUARTER + 2, :128]
    for r in range(CHUNKS):
        q = mine_ref[:, chunk(r)] + got_ref[:QUARTER, chunk(r)]
        q_ref[:, chunk(r)] = q
        lse_ref[pl.ds(r, 1), :] = lse(q - UNIT * sq_ref[...], 0)
    out_ref[...] = jnp.broadcast_to(lse_ref[...][None], (GROUP, CHUNKS, 128))
    for rel, ref in zip(AROUND, block_refs):
        for h in range(2):
            lanes = pl.ds(pl.multiple_of((h * X + at(place, 1, -rel, X)) * 128, 128), 128)
            ref[:, chunk(h)] = q_ref[:, lanes]


def score(place, mine, sq_mine, sqn_mine, got):
    return pl.pallas_call(
        score_kernel,
        out_shape=(
            jax.ShapeDtypeStruct((QUARTER, TALL), F32),
            jax.ShapeDtypeStruct((GROUP, CHUNKS, 128), F32),
            jax.ShapeDtypeStruct((QUARTER, 128), F32),
            jax.ShapeDtypeStruct((2, 128), F32),
        )
        + (jax.ShapeDtypeStruct((QUARTER, ROWS), F32),) * X,
        in_specs=[SMEM] + [VMEM] * 4,
        out_specs=(VMEM,) * (4 + X),
        scratch_shapes=[pltpu.VMEM((CHUNKS, 128), F32)],
        compiler_params=params(16),
        name="score",
    )(place, mine, sq_mine, sqn_mine, got)


def to_column(g):
    return jnp.concatenate([jnp.transpose(jnp.broadcast_to(g[r : r + 1], (128, 128))) for r in range(2)], axis=0)


def noise_kernel(q_ref, part_ref, out_ref, lse_ref, g_ref):
    g_ref[...] = to_column(-LOG2N - merged(part_ref))
    for r in range(CHUNKS):
        lse_ref[pl.ds(r, 1), :] = lse(q_ref[:, chunk(r)] + g_ref[...], 0)
    out_ref[...] = jnp.broadcast_to(lse_ref[...][None], (GROUP, CHUNKS, 128))


def noise_lse(q, parts):
    return pl.pallas_call(
        noise_kernel,
        out_shape=jax.ShapeDtypeStruct((GROUP, CHUNKS, 128), F32),
        in_specs=[VMEM] * 2,
        out_specs=VMEM,
        scratch_shapes=[pltpu.VMEM((CHUNKS, 128), F32), pltpu.VMEM((QUARTER, 128), F32)],
        compiler_params=params(16),
        name="noise_lse",
    )(q, parts)


def data_kernel(q_ref, part_ref, out_ref, f_ref, lane_ref):
    f_ref[...] = -LOG2N - merged(part_ref)
    row = data_row(q_ref, f_ref, lane_ref)
    out_ref[...] = jnp.broadcast_to(two_rows(row)[None], (Z, 8, 128))


def data_row(q_ref, f_ref, lane_ref):
    step = 32
    for start in range(0, QUARTER, step):
        rows = pl.ds(start, step)
        t = [q_ref[rows, chunk(r)] + f_ref[pl.ds(r, 1), :] for r in range(CHUNKS)]
        top = functools.reduce(jnp.maximum, t)
        lane_ref[rows, :] = top + jnp.log2(sum(jnp.exp2(part - top) for part in t))
    return lse(jnp.transpose(lane_ref[...]), 0)


def two_rows(*rows):
    halves = [half for row in rows for half in (row[:, :128], row[:, 128:])]
    return jnp.concatenate(halves + [jnp.zeros((8 - len(halves), 128), F32)], axis=0)


def data_lse(q, parts):
    return pl.pallas_call(
        data_kernel,
        out_shape=(jax.ShapeDtypeStruct((Z, 8, 128), F32), jax.ShapeDtypeStruct((CHUNKS, 128), F32)),
        in_specs=[VMEM] * 2,
        out_specs=(VMEM, VMEM),
        scratch_shapes=[pltpu.VMEM((QUARTER, 128), F32)],
        compiler_params=params(16),
        name="data_lse",
    )(q, parts)


def last_kernel(q_ref, part_ref, sq_ref, out_ref, f_ref, lane_ref):
    f_ref[...] = -LOG2N - merged(part_ref)
    tile = two_rows(data_row(q_ref, f_ref, lane_ref), jnp.transpose(sq_ref[...])[0:1, :])
    out_ref[...] = jnp.broadcast_to(tile[None], (Z * X, 8, 128))


def last_lse(q, parts, sq):
    return pl.pallas_call(
        last_kernel,
        out_shape=(jax.ShapeDtypeStruct((Z * X, 8, 128), F32), jax.ShapeDtypeStruct((CHUNKS, 128), F32)),
        in_specs=[VMEM] * 3,
        out_specs=(VMEM,) * 2,
        scratch_shapes=[pltpu.VMEM((QUARTER, 128), F32)],
        compiler_params=params(16),
        name="last_lse",
    )(q, parts, sq)


def weigh_kernel(place, part_ref, f_ref, *refs):
    q_refs, (w_ref, pot_ref) = refs[:X], refs[X:]
    for n in range(X):
        parts = jnp.stack([part_ref[k * X + n, 0:4, :] for k in range(Z)])
        top = jnp.max(parts, axis=0)
        total = top + jnp.log2(jnp.sum(jnp.exp2(parts - top[None]), axis=0))
        pot_ref[pl.ds(2 * n, 2), :] = (-LOG2N - total[0:2]) * (EPS / LOG2E) + parts[0, 2:4] * (1.0 / WIDTH)
    for j, rel in enumerate(AROUND):
        n = at(place, 1, rel, X)
        parts = jnp.stack([part_ref[k * X + n] for k in range(Z)])
        top = jnp.max(parts, axis=0)
        column = to_column(top + jnp.log2(jnp.sum(jnp.exp2(parts - top[None]), axis=0)))
        for h in range(2):
            f = f_ref[pl.ds(h * X + place[1], 1), :]
            w = jnp.exp2((q_refs[j][:, chunk(h)] + f) - column)
            w_ref[pl.ds(h * 128, 128), pl.ds(j * QUARTER, QUARTER)] = jnp.transpose(w).astype(BF16)


def weigh(place, parts, f, blocks):
    return pl.pallas_call(
        weigh_kernel,
        out_shape=(jax.ShapeDtypeStruct((ROWS, COUNT), BF16), jax.ShapeDtypeStruct((2 * X, 128), F32)),
        in_specs=[SMEM] + [VMEM] * (2 + X),
        out_specs=(VMEM,) * 2,
        compiler_params=params(16),
        name="weigh",
    )(place, parts, f, *blocks)


def transport_kernel(pieces, place, w_ref, got_ref, *refs):
    side_refs, data_ref, out_refs = refs[:X], refs[X], refs[X + 1 :]
    lhs = jnp.concatenate([w_ref[...], got_ref[...]], axis=1)
    for s, out_ref in zip(pieces, out_refs):
        y = at(place, 2, s, Y)
        rhs = []
        for core in (place[3], 1 - place[3]):
            for rel, side_ref in zip(AROUND, side_refs):
                n = at(place, 1, rel, X)
                rhs.append(jnp.concatenate([data_ref[n, y, core, k] for k in range(X - 1)] + [side_ref[y, core]], axis=1))
        total = jnp.dot(lhs, jnp.concatenate(rhs, axis=0), preferred_element_type=F32)
        out_ref[...] = total.astype(out_ref.dtype)


def transport(place, w, got, sides, data, pieces, hand_on):
    kinds = [jax.ShapeDtypeStruct((ROWS, SHARE), BF16 if s else F32) for s in pieces]
    if hand_on:
        kinds.append(jax.ShapeDtypeStruct(data.shape, data.dtype))
    return pl.pallas_call(
        functools.partial(transport_kernel, pieces),
        out_shape=kinds,
        in_specs=[SMEM] + [VMEM] * (3 + X),
        out_specs=[VMEM] * len(kinds),
        input_output_aliases={3 + X: len(pieces)} if hand_on else {},
        compiler_params=params(24),
        cost_estimate=pl.CostEstimate(
            flops=2 * ROWS * COUNT * C * SHARE * len(pieces), bytes_accessed=2 * 2**20 * len(pieces), transcendentals=0
        ),
        name="transport",
    )(place, w, got, *sides, data)


def body(noise, data):
    z, x, y, c = (lax.axis_index(a) for a in ("z", "x", "y", "core"))
    place = jnp.stack([z, x, y, c]).astype(jnp.int32)
    swapped = lax.all_to_all(data.reshape(X, QUARTER, SLICE), "x", 0, 0)
    noise_after, swapped = lax.optimization_barrier((noise, swapped))
    samples = lax.all_gather(swapped, ("z", "core")).reshape(Y, C, C, X, QUARTER, SLICE)
    samples, noise_all, sqn_mine = lax.optimization_barrier((samples, *collect(gather_noise(noise_after))))
    far, side, near = pick(place, samples)
    data_all = lax.all_gather(far, "x")
    sides = around(side, "x")
    got = shift(theirs(place, near, noise_all, sqn_mine), "core", 1)
    mine, sq_mine = ours(place, near, noise_all)
    q, rows, sq, sq_noise, *blocks = score(place, mine, sq_mine, sqn_mine, got)
    blocks = [blocks[0]] + [shift(block, "x", by) for block, by in zip(blocks[1:], (1, -1, 2))]
    for step in range(ITERS):
        if step == 1:
            columns, sides = lax.optimization_barrier((columns, sides))
        if step:
            rows = noise_lse(q, columns)
        parts = lax.all_to_all(rows, ("x", "y", "core"), 0, 0)
        if step < ITERS - 1:
            columns, f = data_lse(q, parts)
            columns = lax.all_to_all(columns, "z", 0, 0)
    columns, f = last_lse(q, parts, sq)
    data_all, columns = lax.optimization_barrier((data_all, columns))
    columns = lax.all_to_all(columns, ("z", "x"), 0, 0)
    w, pot_g = weigh(place, columns, f, blocks)
    got = shift(w, "core", 1)
    *parts, data_all = transport(place, w, got, sides, data_all, (2, 1, 3), True)
    (target,) = transport(place, w, got, sides, data_all, (0,), False)
    for by, part in zip((2, 1, 3), parts):
        target = target + shift(part, "y", by).astype(F32)
    velocity = (target - noise.astype(F32)).astype(BF16)
    own = lax.dynamic_index_in_dim(f.reshape(2, X, 128), x, 1, False)
    pot_f = (own * (EPS / LOG2E) + sq_noise / WIDTH).reshape(ROWS)
    return pot_f, pot_g.reshape(COUNT), velocity


def solution(mesh):
    fine = Mesh(mesh.devices.reshape(Z, X, Y, C), ("z", "x", "y", "core"))
    row, col = ("z", "x"), ("y", "core")
    return jax.shard_map(
        body,
        mesh=fine,
        in_specs=(P(row, col), P(col, row)),
        out_specs=(P(row), P(col), P(row, col)),
        check_vma=False,
    )
```

```python
import functools
import math

import jax
import jax.numpy as jnp
from jax import lax
from jax.experimental import pallas as pl
from jax.experimental.pallas import tpu as pltpu
from jax.sharding import Mesh, PartitionSpec as P

ITERS = 3
EPS = 0.01
LOG2E = math.log2(math.e)
Z, X, Y, C = 8, 4, 4, 2
ROWS, SHARE = 256, 512
COUNT, SLICE = 1024, 128
WIDTH = 4096
QUARTER = COUNT // X
TALL = ROWS * X
CHUNKS = TALL // 128
GROUP = X * Y * C
CUT = ROWS // 2
AROUND = (0, -1, 1, 2)
TOTAL = 8192
UNIT = LOG2E / (WIDTH * EPS)
LOG2N = math.log2(TOTAL)
F32, BF16 = jnp.float32, jnp.bfloat16
VMEM = pl.BlockSpec(memory_space=pltpu.VMEM)
SMEM = pl.BlockSpec(memory_space=pltpu.SMEM)


def shift(x, axis, by):
    n = {"z": Z, "x": X, "y": Y, "core": C}[axis]
    return lax.ppermute(x, axis, [(j, (j + by) % n) for j in range(n)])


def params(mib):
    return pltpu.CompilerParams(vmem_limit_bytes=mib * 2**20)


def both_ways(forward, backward, axis):
    return shift(forward, axis, 1), shift(backward, axis, -1)


def halves(forward, backward, axis):
    cut = forward.shape[0] // 2
    return both_ways(forward[:cut], backward[cut:], axis)


def around(block, axis):
    return [block, shift(block, axis, 1), shift(block, axis, -1), shift(block, axis, 2)]


def gather_noise(noise):
    hold = lax.optimization_barrier
    across, along = hold((around(noise[:CUT], "x"), around(noise[CUT:], "y")))
    across, along = jnp.stack(across), jnp.stack(along)
    y1, x1 = hold((both_ways(across, across, "y"), both_ways(along, along, "x")))
    return [across, *y1, *halves(*y1, "y"), along, *x1, *halves(*x1, "x")]


def squares(ref, pieces):
    total = None
    for view in pieces:
        part = ref[view].astype(F32)
        total = part * part if total is None else total + part * part
    return total


def lse(t, axis):
    top = jnp.max(t, axis=axis, keepdims=True)
    return top + jnp.log2(jnp.sum(jnp.exp2(t - top), axis=axis, keepdims=True))


def merged(ref):
    parts = ref[...]
    top = jnp.max(parts, axis=0)
    return top + jnp.log2(jnp.sum(jnp.exp2(parts - top[None]), axis=0))


def chunk(r):
    return pl.ds(r * 128, 128)


def at(place, which, rel, size):
    return lax.rem(place[which] + rel + size, size)


def blocks_of(parts):
    first, second = parts[:5], parts[5:]

    def of(five, far, near):
        if far < 3:
            return five[far].at[near]
        return five[3 + near // 2].at[near % 2]

    return (
        [[of(first, k, j) for k in range(Y)] for j in range(X)],
        [[of(second, j, k) for k in range(Y)] for j in range(X)],
    )


def collect_kernel(*refs):
    parts, (noise_ref, sqn_ref) = refs[:10], refs[10:]
    rows = []
    for h, blocks in enumerate(blocks_of(parts)):
        for j, row in enumerate(blocks):
            for k, ref in enumerate(row):
                noise_ref[pl.ds((h * X + j) * CUT, CUT), pl.ds(k * SHARE, SHARE)] = ref[...]
        t = [squares(ref, [(slice(None), pl.ds(lane, 128)) for lane in range(0, SHARE, 128)]) for ref in blocks[0]]
        total = (t[0] + t[3]) + (t[1] + t[2])
        rows.append(jnp.sum(jnp.transpose(total), axis=0, keepdims=True))
    sqn_ref[...] = jnp.concatenate(rows, axis=0)


def collect(parts):
    return pl.pallas_call(
        collect_kernel,
        out_shape=(jax.ShapeDtypeStruct((TALL, WIDTH // C), BF16), jax.ShapeDtypeStruct((2, 128), F32)),
        in_specs=[VMEM] * 10,
        out_specs=(VMEM,) * 2,
        compiler_params=params(16),
        name="collect",
    )(*parts)


def pick_kernel(place, all_ref, far_ref, near_ref, sems):
    copies = []
    for y in range(Y):
        for n, ref in enumerate((near_ref, far_ref)):
            copies.append(pltpu.make_async_copy(all_ref.at[y, place[3]], ref.at[y], sems.at[n, y]))
    for copy in copies:
        copy.start()
    for copy in copies:
        copy.wait()


def pick(place, samples):
    half = jax.ShapeDtypeStruct((Y, C, X, QUARTER, SLICE), BF16)
    return pl.pallas_call(
        pick_kernel,
        out_shape=(half, half),
        in_specs=[SMEM, pl.BlockSpec(memory_space=pl.ANY)],
        out_specs=(pl.BlockSpec(memory_space=pl.ANY), VMEM),
        scratch_shapes=[pltpu.SemaphoreType.DMA((2, Y))],
        compiler_params=params(16),
        name="pick",
    )(place, samples)


def partial_scores(place, data_ref, core, noise_ref, q_ref, sq_ref):
    pieces = [at(place, 2, rel, Y) for rel in AROUND]
    lhs = jnp.concatenate([data_ref[p, core, n] for p in pieces for n in range(X)], axis=1)
    for h in range(2):
        rhs = noise_ref[pl.ds(h * X * CUT, X * CUT), :]
        gram = lax.dot_general(lhs, rhs, (((1,), (1,)), ((), ())), preferred_element_type=F32) * (2.0 * UNIT)
        for j, rel in enumerate(AROUND):
            lanes = pl.ds(pl.multiple_of((h * X + at(place, 1, rel, X)) * 128, 128), 128)
            q_ref[:QUARTER, lanes] = gram[:, j * 128 : (j + 1) * 128]
    sq_ref[...] = squares(data_ref, [(p, core, n) for p in range(Y) for n in range(X)])


def theirs_kernel(place, data_ref, noise_ref, sqn_ref, out_ref, sq_ref):
    partial_scores(place, data_ref, 1 - place[3], noise_ref, out_ref, sq_ref)
    out_ref[:QUARTER, TALL:] = sq_ref[...]
    out_ref[QUARTER:, :] = jnp.zeros((8, TALL + 128), F32)
    out_ref[QUARTER : QUARTER + 2, :128] = sqn_ref[...]


def theirs(place, data, noise, sqn):
    return pl.pallas_call(
        theirs_kernel,
        out_shape=jax.ShapeDtypeStruct((QUARTER + 8, TALL + 128), F32),
        in_specs=[SMEM] + [VMEM] * 3,
        out_specs=VMEM,
        scratch_shapes=[pltpu.VMEM((QUARTER, 128), F32)],
        compiler_params=params(24),
        name="theirs",
    )(place, data, noise, sqn)


def ours_kernel(place, data_ref, noise_ref, q_ref, sq_ref):
    partial_scores(place, data_ref, place[3], noise_ref, q_ref, sq_ref)


def ours(place, data, noise):
    return pl.pallas_call(
        ours_kernel,
        out_shape=(jax.ShapeDtypeStruct((QUARTER, TALL), F32), jax.ShapeDtypeStruct((QUARTER, 128), F32)),
        in_specs=[SMEM] + [VMEM] * 2,
        out_specs=(VMEM,) * 2,
        compiler_params=params(24),
        cost_estimate=pl.CostEstimate(flops=QUARTER * TALL * WIDTH, bytes_accessed=6 * 2**20, transcendentals=0),
        name="ours",
    )(place, data, noise)


def score_kernel(place, mine_ref, sq_mine_ref, sqn_mine_ref, got_ref, q_ref, out_ref, sq_ref, sqn_ref, *refs):
    block_refs, lse_ref = refs[:X], refs[X]
    sq = jnp.sum(sq_mine_ref[...] + got_ref[:QUARTER, TALL:], axis=1, keepdims=True)
    sq_ref[...] = jnp.broadcast_to(sq, (QUARTER, 128))
    sqn_ref[...] = sqn_mine_ref[...] + got_ref[QUARTER : QUARTER + 2, :128]
    for r in range(CHUNKS):
        q = mine_ref[:, chunk(r)] + got_ref[:QUARTER, chunk(r)]
        q_ref[:, chunk(r)] = q
        lse_ref[pl.ds(r, 1), :] = lse(q - UNIT * sq_ref[...], 0)
    out_ref[...] = jnp.broadcast_to(lse_ref[...][None], (GROUP, CHUNKS, 128))
    for rel, ref in zip(AROUND, block_refs):
        for h in range(2):
            lanes = pl.ds(pl.multiple_of((h * X + at(place, 1, -rel, X)) * 128, 128), 128)
            ref[:, chunk(h)] = q_ref[:, lanes]


def score(place, mine, sq_mine, sqn_mine, got):
    return pl.pallas_call(
        score_kernel,
        out_shape=(
            jax.ShapeDtypeStruct((QUARTER, TALL), F32),
            jax.ShapeDtypeStruct((GROUP, CHUNKS, 128), F32),
            jax.ShapeDtypeStruct((QUARTER, 128), F32),
            jax.ShapeDtypeStruct((2, 128), F32),
        )
        + (jax.ShapeDtypeStruct((QUARTER, ROWS), F32),) * X,
        in_specs=[SMEM] + [VMEM] * 4,
        out_specs=(VMEM,) * (4 + X),
        scratch_shapes=[pltpu.VMEM((CHUNKS, 128), F32)],
        compiler_params=params(16),
        name="score",
    )(place, mine, sq_mine, sqn_mine, got)


def to_column(g):
    return jnp.concatenate([jnp.transpose(jnp.broadcast_to(g[r : r + 1], (128, 128))) for r in range(2)], axis=0)


def noise_kernel(q_ref, part_ref, out_ref, lse_ref, g_ref):
    g_ref[...] = to_column(-LOG2N - merged(part_ref))
    for r in range(CHUNKS):
        lse_ref[pl.ds(r, 1), :] = lse(q_ref[:, chunk(r)] + g_ref[...], 0)
    out_ref[...] = jnp.broadcast_to(lse_ref[...][None], (GROUP, CHUNKS, 128))


def noise_lse(q, parts):
    return pl.pallas_call(
        noise_kernel,
        out_shape=jax.ShapeDtypeStruct((GROUP, CHUNKS, 128), F32),
        in_specs=[VMEM] * 2,
        out_specs=VMEM,
        scratch_shapes=[pltpu.VMEM((CHUNKS, 128), F32), pltpu.VMEM((QUARTER, 128), F32)],
        compiler_params=params(16),
        name="noise_lse",
    )(q, parts)


def data_kernel(q_ref, part_ref, out_ref, f_ref, lane_ref):
    f_ref[...] = -LOG2N - merged(part_ref)
    row = data_row(q_ref, f_ref, lane_ref)
    out_ref[...] = jnp.broadcast_to(two_rows(row)[None], (Z, 8, 128))


def data_row(q_ref, f_ref, lane_ref):
    step = 32
    for start in range(0, QUARTER, step):
        rows = pl.ds(start, step)
        t = [q_ref[rows, chunk(r)] + f_ref[pl.ds(r, 1), :] for r in range(CHUNKS)]
        top = functools.reduce(jnp.maximum, t)
        lane_ref[rows, :] = top + jnp.log2(sum(jnp.exp2(part - top) for part in t))
    return lse(jnp.transpose(lane_ref[...]), 0)


def two_rows(*rows):
    halves = [half for row in rows for half in (row[:, :128], row[:, 128:])]
    return jnp.concatenate(halves + [jnp.zeros((8 - len(halves), 128), F32)], axis=0)


def data_lse(q, parts):
    return pl.pallas_call(
        data_kernel,
        out_shape=(jax.ShapeDtypeStruct((Z, 8, 128), F32), jax.ShapeDtypeStruct((CHUNKS, 128), F32)),
        in_specs=[VMEM] * 2,
        out_specs=(VMEM, VMEM),
        scratch_shapes=[pltpu.VMEM((QUARTER, 128), F32)],
        compiler_params=params(16),
        name="data_lse",
    )(q, parts)


def last_kernel(q_ref, part_ref, sq_ref, out_ref, f_ref, lane_ref):
    f_ref[...] = -LOG2N - merged(part_ref)
    tile = two_rows(data_row(q_ref, f_ref, lane_ref), jnp.transpose(sq_ref[...])[0:1, :])
    out_ref[...] = jnp.broadcast_to(tile[None], (Z * X, 8, 128))


def last_lse(q, parts, sq):
    return pl.pallas_call(
        last_kernel,
        out_shape=(jax.ShapeDtypeStruct((Z * X, 8, 128), F32), jax.ShapeDtypeStruct((CHUNKS, 128), F32)),
        in_specs=[VMEM] * 3,
        out_specs=(VMEM,) * 2,
        scratch_shapes=[pltpu.VMEM((QUARTER, 128), F32)],
        compiler_params=params(16),
        name="last_lse",
    )(q, parts, sq)


def weigh_kernel(place, part_ref, f_ref, *refs):
    q_refs, (w_ref, pot_ref) = refs[:X], refs[X:]
    for n in range(X):
        parts = jnp.stack([part_ref[k * X + n, 0:4, :] for k in range(Z)])
        top = jnp.max(parts, axis=0)
        total = top + jnp.log2(jnp.sum(jnp.exp2(parts - top[None]), axis=0))
        pot_ref[pl.ds(2 * n, 2), :] = (-LOG2N - total[0:2]) * (EPS / LOG2E) + parts[0, 2:4] * (1.0 / WIDTH)
    for j, rel in enumerate(AROUND):
        n = at(place, 1, rel, X)
        parts = jnp.stack([part_ref[k * X + n] for k in range(Z)])
        top = jnp.max(parts, axis=0)
        column = to_column(top + jnp.log2(jnp.sum(jnp.exp2(parts - top[None]), axis=0)))
        for h in range(2):
            f = f_ref[pl.ds(h * X + place[1], 1), :]
            w = jnp.exp2((q_refs[j][:, chunk(h)] + f) - column)
            w_ref[pl.ds(h * 128, 128), pl.ds(j * QUARTER, QUARTER)] = jnp.transpose(w).astype(BF16)


def weigh(place, parts, f, blocks):
    return pl.pallas_call(
        weigh_kernel,
        out_shape=(jax.ShapeDtypeStruct((ROWS, COUNT), BF16), jax.ShapeDtypeStruct((2 * X, 128), F32)),
        in_specs=[SMEM] + [VMEM] * (2 + X),
        out_specs=(VMEM,) * 2,
        compiler_params=params(16),
        name="weigh",
    )(place, parts, f, *blocks)


def transport_kernel(pieces, place, w_ref, got_ref, data_ref, *refs):
    out_refs, (buffer_ref, sems) = refs[:-2], refs[-2:]
    copies = []
    for i, s in enumerate(pieces):
        for j, rel in enumerate(AROUND):
            for k in range(C):
                block = data_ref.at[at(place, 1, rel, X), at(place, 2, s, Y), at(place, 3, k, C)]
                copies.append(pltpu.make_async_copy(block, buffer_ref.at[i, k, j], sems.at[i, k, j]))
    for copy in copies:
        copy.start()
    lhs = jnp.concatenate([w_ref[...], got_ref[...]], axis=1)
    for i, out_ref in enumerate(out_refs):
        for copy in copies[i * X * C : (i + 1) * X * C]:
            copy.wait()
        rhs = [jnp.concatenate([buffer_ref[i, k, j, n] for n in range(X)], axis=1) for k in range(C) for j in range(X)]
        total = jnp.dot(lhs, jnp.concatenate(rhs, axis=0), preferred_element_type=F32)
        out_ref[...] = total.astype(out_ref.dtype)


def transport(place, w, got, data, pieces):
    return pl.pallas_call(
        functools.partial(transport_kernel, pieces),
        out_shape=[jax.ShapeDtypeStruct((ROWS, SHARE), BF16 if s else F32) for s in pieces],
        in_specs=[SMEM] + [VMEM] * 2 + [pl.BlockSpec(memory_space=pl.ANY)],
        out_specs=[VMEM] * len(pieces),
        scratch_shapes=[
            pltpu.VMEM((len(pieces), C, X, X, QUARTER, SLICE), BF16),
            pltpu.SemaphoreType.DMA((len(pieces), C, X)),
        ],
        compiler_params=params(53),
        cost_estimate=pl.CostEstimate(
            flops=2 * ROWS * COUNT * C * SHARE * len(pieces), bytes_accessed=2 * 2**20 * len(pieces), transcendentals=0
        ),
        name="transport",
    )(place, w, got, data)


def body(noise, data):
    z, x, y, c = (lax.axis_index(a) for a in ("z", "x", "y", "core"))
    place = jnp.stack([z, x, y, c]).astype(jnp.int32)
    swapped = lax.all_to_all(data.reshape(X, QUARTER, SLICE), "x", 0, 0)
    noise_after, swapped = lax.optimization_barrier((noise, swapped))
    samples = lax.all_gather(swapped, ("z", "core")).reshape(Y, C, C, X, QUARTER, SLICE)
    samples, noise_all, sqn_mine = lax.optimization_barrier((samples, *collect(gather_noise(noise_after))))
    far, near = pick(place, samples)
    data_all = lax.all_gather(far, "x")
    got = shift(theirs(place, near, noise_all, sqn_mine), "core", 1)
    mine, sq_mine = ours(place, near, noise_all)
    q, rows, sq, sq_noise, *blocks = score(place, mine, sq_mine, sqn_mine, got)
    blocks = [blocks[0]] + [shift(block, "x", by) for block, by in zip(blocks[1:], (1, -1, 2))]
    for step in range(ITERS):
        if step:
            rows = noise_lse(q, columns)
        parts = lax.all_to_all(rows, ("x", "y", "core"), 0, 0)
        if step < ITERS - 1:
            columns, f = data_lse(q, parts)
            columns = lax.all_to_all(columns, "z", 0, 0)
    columns, f = last_lse(q, parts, sq)
    columns = lax.all_to_all(columns, ("z", "x"), 0, 0)
    w, pot_g = weigh(place, columns, f, blocks)
    got = shift(w, "core", 1)
    data_all, pot_g = lax.optimization_barrier((data_all, pot_g))
    parts = [part for pieces in ((2,), (1, 3)) for part in transport(place, w, got, data_all, pieces)]
    (target,) = transport(place, w, got, data_all, (0,))
    for by, part in zip((2, 1, 3), parts):
        target = target + shift(part, "y", by).astype(F32)
    velocity = (target - noise.astype(F32)).astype(BF16)
    own = lax.dynamic_index_in_dim(f.reshape(2, X, 128), x, 1, False)
    pot_f = (own * (EPS / LOG2E) + sq_noise / WIDTH).reshape(ROWS)
    return pot_f, pot_g.reshape(COUNT), velocity


def solution(mesh):
    fine = Mesh(mesh.devices.reshape(Z, X, Y, C), ("z", "x", "y", "core"))
    row, col = ("z", "x"), ("y", "core")
    return jax.shard_map(
        body,
        mesh=fine,
        in_specs=(P(row, col), P(col, row)),
        out_specs=(P(row), P(col), P(row, col)),
        check_vma=False,
    )
```

```python
import functools
import math

import jax
import jax.numpy as jnp
from jax import lax
from jax.experimental import pallas as pl
from jax.experimental.pallas import tpu as pltpu
from jax.sharding import Mesh, PartitionSpec as P

ITERS = 3
EPS = 0.01
LOG2E = math.log2(math.e)
Z, X, Y, C = 8, 4, 4, 2
ROWS, SHARE = 256, 512
COUNT, SLICE = 1024, 128
WIDTH = 4096
QUARTER = COUNT // X
TALL = ROWS * X
CHUNKS = TALL // 128
GROUP = X * Y * C
CUT = ROWS // 2
AROUND = (0, -1, 1, 2)
TOTAL = 8192
UNIT = LOG2E / (WIDTH * EPS)
LOG2N = math.log2(TOTAL)
F32, BF16 = jnp.float32, jnp.bfloat16
VMEM = pl.BlockSpec(memory_space=pltpu.VMEM)
SMEM = pl.BlockSpec(memory_space=pltpu.SMEM)


def shift(x, axis, by):
    n = {"z": Z, "x": X, "y": Y, "core": C}[axis]
    return lax.ppermute(x, axis, [(j, (j + by) % n) for j in range(n)])


def params(mib):
    return pltpu.CompilerParams(vmem_limit_bytes=mib * 2**20)


def both_ways(forward, backward, axis):
    return shift(forward, axis, 1), shift(backward, axis, -1)


def halves(forward, backward, axis):
    cut = forward.shape[0] // 2
    return both_ways(forward[:cut], backward[cut:], axis)


def around(block, axis):
    return [block, shift(block, axis, 1), shift(block, axis, -1), shift(block, axis, 2)]


def gather_noise(noise):
    hold = lax.optimization_barrier
    across, along = hold((around(noise[:CUT], "x"), around(noise[CUT:], "y")))
    across, along = jnp.stack(across), jnp.stack(along)
    y1, x1 = hold((both_ways(across, across, "y"), both_ways(along, along, "x")))
    return [across, *y1, *halves(*y1, "y"), along, *x1, *halves(*x1, "x")]


def squares(ref, pieces):
    total = None
    for view in pieces:
        part = ref[view].astype(F32)
        total = part * part if total is None else total + part * part
    return total


def lse(t, axis):
    top = jnp.max(t, axis=axis, keepdims=True)
    return top + jnp.log2(jnp.sum(jnp.exp2(t - top), axis=axis, keepdims=True))


def merged(ref):
    parts = ref[...]
    top = jnp.max(parts, axis=0)
    return top + jnp.log2(jnp.sum(jnp.exp2(parts - top[None]), axis=0))


def chunk(r):
    return pl.ds(r * 128, 128)


def at(place, which, rel, size):
    return lax.rem(place[which] + rel + size, size)


def from_x(x, n):
    return lax.rem(x - n + X, X) if not isinstance(x, int) else (x - n) % X


def blocks_of(parts):
    first, second = parts[:5], parts[5:]

    def of(five, far, near):
        if far < 3:
            return five[far].at[near]
        return five[3 + near // 2].at[near % 2]

    return (
        [[of(first, k, j) for k in range(Y)] for j in range(X)],
        [[of(second, j, k) for k in range(Y)] for j in range(X)],
    )


def collect_kernel(*refs):
    parts, (noise_ref, sqn_ref) = refs[:10], refs[10:]
    rows = []
    for h, blocks in enumerate(blocks_of(parts)):
        for j, row in enumerate(blocks):
            for k, ref in enumerate(row):
                noise_ref[pl.ds((h * X + j) * CUT, CUT), pl.ds(k * SHARE, SHARE)] = ref[...]
        t = [squares(ref, [(slice(None), pl.ds(lane, 128)) for lane in range(0, SHARE, 128)]) for ref in blocks[0]]
        total = (t[0] + t[3]) + (t[1] + t[2])
        rows.append(jnp.sum(jnp.transpose(total), axis=0, keepdims=True))
    sqn_ref[...] = jnp.concatenate(rows, axis=0)


def collect(parts):
    return pl.pallas_call(
        collect_kernel,
        out_shape=(jax.ShapeDtypeStruct((TALL, WIDTH // C), BF16), jax.ShapeDtypeStruct((2, 128), F32)),
        in_specs=[VMEM] * 10,
        out_specs=(VMEM,) * 2,
        compiler_params=params(16),
        name="collect",
    )(*parts)


def pick_kernel(place, all_ref, out_ref, sems):
    copies = [pltpu.make_async_copy(all_ref.at[y, place[3]], out_ref.at[y], sems.at[y]) for y in range(Y)]
    for copy in copies:
        copy.start()
    for copy in copies:
        copy.wait()


def pick(place, samples):
    return pl.pallas_call(
        pick_kernel,
        out_shape=jax.ShapeDtypeStruct((Y, C, X, QUARTER, SLICE), BF16),
        in_specs=[SMEM, pl.BlockSpec(memory_space=pl.ANY)],
        out_specs=pl.BlockSpec(memory_space=pl.ANY),
        scratch_shapes=[pltpu.SemaphoreType.DMA((Y,))],
        compiler_params=params(53),
        name="pick",
    )(place, samples)


def deal_kernel(place, data_ref, *out_refs):
    for by, ref in enumerate(out_refs):
        ref[...] = data_ref[at(place, 1, by, X)]


def deal(place, data):
    return pl.pallas_call(
        deal_kernel,
        out_shape=(jax.ShapeDtypeStruct((QUARTER, SLICE), BF16),) * X,
        in_specs=[SMEM, VMEM],
        out_specs=(VMEM,) * X,
        compiler_params=params(16),
        name="deal",
    )(place, data.reshape(X, QUARTER, SLICE))


def partial_scores(place, data_ref, core, noise_ref, q_ref, sq_ref):
    pieces = [at(place, 2, rel, Y) for rel in AROUND]
    lhs = jnp.concatenate([data_ref[p, core, from_x(place[1], n)] for p in pieces for n in range(X)], axis=1)
    for h in range(2):
        rhs = noise_ref[pl.ds(h * X * CUT, X * CUT), :]
        gram = lax.dot_general(lhs, rhs, (((1,), (1,)), ((), ())), preferred_element_type=F32) * (2.0 * UNIT)
        for j, rel in enumerate(AROUND):
            lanes = pl.ds(pl.multiple_of((h * X + at(place, 1, rel, X)) * 128, 128), 128)
            q_ref[:QUARTER, lanes] = gram[:, j * 128 : (j + 1) * 128]
    sq_ref[...] = squares(data_ref, [(p, core, n) for p in range(Y) for n in range(X)])


def theirs_kernel(place, data_ref, noise_ref, sqn_ref, out_ref, sq_ref):
    partial_scores(place, data_ref, 1 - place[3], noise_ref, out_ref, sq_ref)
    out_ref[:QUARTER, TALL:] = sq_ref[...]
    out_ref[QUARTER:, :] = jnp.zeros((8, TALL + 128), F32)
    out_ref[QUARTER : QUARTER + 2, :128] = sqn_ref[...]


def theirs(place, data, noise, sqn):
    return pl.pallas_call(
        theirs_kernel,
        out_shape=jax.ShapeDtypeStruct((QUARTER + 8, TALL + 128), F32),
        in_specs=[SMEM] + [VMEM] * 3,
        out_specs=VMEM,
        scratch_shapes=[pltpu.VMEM((QUARTER, 128), F32)],
        compiler_params=params(24),
        name="theirs",
    )(place, data, noise, sqn)


def ours_kernel(place, data_ref, noise_ref, q_ref, sq_ref):
    partial_scores(place, data_ref, place[3], noise_ref, q_ref, sq_ref)


def ours(place, data, noise):
    return pl.pallas_call(
        ours_kernel,
        out_shape=(jax.ShapeDtypeStruct((QUARTER, TALL), F32), jax.ShapeDtypeStruct((QUARTER, 128), F32)),
        in_specs=[SMEM] + [VMEM] * 2,
        out_specs=(VMEM,) * 2,
        compiler_params=params(24),
        cost_estimate=pl.CostEstimate(flops=QUARTER * TALL * WIDTH, bytes_accessed=6 * 2**20, transcendentals=0),
        name="ours",
    )(place, data, noise)


def score_kernel(mine_ref, sq_mine_ref, sqn_mine_ref, got_ref, q_ref, out_ref, sq_ref, sqn_ref, lse_ref):
    sq = jnp.sum(sq_mine_ref[...] + got_ref[:QUARTER, TALL:], axis=1, keepdims=True)
    sq_ref[...] = jnp.broadcast_to(sq, (QUARTER, 128))
    sqn_ref[...] = sqn_mine_ref[...] + got_ref[QUARTER : QUARTER + 2, :128]
    for r in range(CHUNKS):
        q = mine_ref[:, chunk(r)] + got_ref[:QUARTER, chunk(r)]
        q_ref[:, chunk(r)] = q
        lse_ref[pl.ds(r, 1), :] = lse(q - UNIT * sq_ref[...], 0)
    out_ref[...] = jnp.broadcast_to(lse_ref[...][None], (GROUP, CHUNKS, 128))


def score(mine, sq_mine, sqn_mine, got):
    return pl.pallas_call(
        score_kernel,
        out_shape=(
            jax.ShapeDtypeStruct((QUARTER, TALL), F32),
            jax.ShapeDtypeStruct((GROUP, CHUNKS, 128), F32),
            jax.ShapeDtypeStruct((QUARTER, 128), F32),
            jax.ShapeDtypeStruct((2, 128), F32),
        ),
        in_specs=[VMEM] * 4,
        out_specs=(VMEM,) * 4,
        scratch_shapes=[pltpu.VMEM((CHUNKS, 128), F32)],
        compiler_params=params(16),
        name="score",
    )(mine, sq_mine, sqn_mine, got)


def to_column(g):
    return jnp.concatenate([jnp.transpose(jnp.broadcast_to(g[r : r + 1], (128, 128))) for r in range(2)], axis=0)


def noise_kernel(q_ref, part_ref, out_ref, lse_ref, g_ref):
    g_ref[...] = to_column(-LOG2N - merged(part_ref))
    for r in range(CHUNKS):
        lse_ref[pl.ds(r, 1), :] = lse(q_ref[:, chunk(r)] + g_ref[...], 0)
    out_ref[...] = jnp.broadcast_to(lse_ref[...][None], (GROUP, CHUNKS, 128))


def noise_lse(q, parts):
    return pl.pallas_call(
        noise_kernel,
        out_shape=jax.ShapeDtypeStruct((GROUP, CHUNKS, 128), F32),
        in_specs=[VMEM] * 2,
        out_specs=VMEM,
        scratch_shapes=[pltpu.VMEM((CHUNKS, 128), F32), pltpu.VMEM((QUARTER, 128), F32)],
        compiler_params=params(16),
        name="noise_lse",
    )(q, parts)


def data_kernel(q_ref, part_ref, out_ref, f_ref, lane_ref):
    f_ref[...] = -LOG2N - merged(part_ref)
    row = data_row(q_ref, f_ref, lane_ref)
    out_ref[...] = jnp.broadcast_to(two_rows(row)[None], (Z, 8, 128))


def data_row(q_ref, f_ref, lane_ref):
    step = 32
    for start in range(0, QUARTER, step):
        rows = pl.ds(start, step)
        t = [q_ref[rows, chunk(r)] + f_ref[pl.ds(r, 1), :] for r in range(CHUNKS)]
        top = functools.reduce(jnp.maximum, t)
        lane_ref[rows, :] = top + jnp.log2(sum(jnp.exp2(part - top) for part in t))
    return lse(jnp.transpose(lane_ref[...]), 0)


def two_rows(*rows):
    halves = [half for row in rows for half in (row[:, :128], row[:, 128:])]
    return jnp.concatenate(halves + [jnp.zeros((8 - len(halves), 128), F32)], axis=0)


def data_lse(q, parts):
    return pl.pallas_call(
        data_kernel,
        out_shape=(jax.ShapeDtypeStruct((Z, 8, 128), F32), jax.ShapeDtypeStruct((CHUNKS, 128), F32)),
        in_specs=[VMEM] * 2,
        out_specs=(VMEM, VMEM),
        scratch_shapes=[pltpu.VMEM((QUARTER, 128), F32)],
        compiler_params=params(16),
        name="data_lse",
    )(q, parts)


def last_kernel(place, q_ref, part_ref, sq_ref, out_ref, f_ref, *refs):
    w_refs, lane_ref = refs[:X], refs[X]
    f_ref[...] = -LOG2N - merged(part_ref)
    tile = two_rows(data_row(q_ref, f_ref, lane_ref), jnp.transpose(sq_ref[...])[0:1, :])
    out_ref[...] = jnp.broadcast_to(tile[None], (Z * X, 8, 128))
    column = to_column(tile)
    for by in range(X):
        block = lax.rem(place[1] + by, X)
        for h in range(2):
            lanes = pl.ds(pl.multiple_of((h * X + block) * 128, 128), 128)
            w = jnp.exp2((q_ref[:, lanes] + f_ref[pl.ds(h * X + block, 1), :]) - column)
            w_refs[by][:, pl.ds(h * 128, 128)] = w.astype(BF16)


def last_lse(place, q, parts, sq):
    return pl.pallas_call(
        last_kernel,
        out_shape=(jax.ShapeDtypeStruct((Z * X, 8, 128), F32), jax.ShapeDtypeStruct((CHUNKS, 128), F32))
        + (jax.ShapeDtypeStruct((QUARTER, ROWS), BF16),) * X,
        in_specs=[SMEM] + [VMEM] * 3,
        out_specs=(VMEM,) * (2 + X),
        scratch_shapes=[pltpu.VMEM((QUARTER, 128), F32)],
        compiler_params=params(16),
        name="last_lse",
    )(place, q, parts, sq)


def scale_kernel(place, part_ref, *refs):
    w_refs, (w_ref, pot_ref) = refs[:X], refs[X:]
    z, x = place[0], place[1]
    for n in range(X):
        parts = jnp.stack([part_ref[k * X + n, 0:4, :] for k in range(Z)])
        top = jnp.max(parts, axis=0)
        total = top + jnp.log2(jnp.sum(jnp.exp2(parts - top[None]), axis=0))
        pot_ref[pl.ds(2 * n, 2), :] = (-LOG2N - total[0:2]) * (EPS / LOG2E) + parts[0, 2:4] * (1.0 / WIDTH)
    for by in range(X):
        n = lax.rem(x - by + X, X)
        parts = jnp.stack([part_ref[k * X + n] for k in range(Z)])
        top = jnp.max(parts, axis=0)
        total = top + jnp.log2(jnp.sum(jnp.exp2(parts - top[None]), axis=0))
        factor = jnp.exp2(part_ref[z * X + n] - total)
        factor = jnp.concatenate([factor[0:1], factor[1:2]], axis=1)
        lanes = pl.ds(pl.multiple_of(n * QUARTER, QUARTER), QUARTER)
        for h in range(2):
            w = jnp.transpose(w_refs[by][:, pl.ds(h * 128, 128)].astype(F32)) * factor
            w_ref[pl.ds(h * 128, 128), lanes] = w.astype(BF16)


def scale(place, parts, blocks):
    return pl.pallas_call(
        scale_kernel,
        out_shape=(jax.ShapeDtypeStruct((ROWS, COUNT), BF16), jax.ShapeDtypeStruct((2 * X, 128), F32)),
        in_specs=[SMEM] + [VMEM] * (1 + X),
        out_specs=(VMEM,) * 2,
        compiler_params=params(16),
        name="scale",
    )(place, parts, *blocks)


def transport_kernel(pieces, place, w_ref, got_ref, data_ref, *out_refs):
    lhs = jnp.concatenate([w_ref[...], got_ref[...]], axis=1)
    for s, out_ref in zip(pieces, out_refs):
        y = at(place, 2, s, Y)
        rhs = []
        for core in (place[3], 1 - place[3]):
            for n in range(X):
                rhs.append(jnp.concatenate([data_ref[n, y, core, from_x(n, k)] for k in range(X)], axis=1))
        total = jnp.dot(lhs, jnp.concatenate(rhs, axis=0), preferred_element_type=F32)
        out_ref[...] = total.astype(out_ref.dtype)


def transport(place, w, got, data, pieces, hand_on):
    kinds = [jax.ShapeDtypeStruct((ROWS, SHARE), BF16 if s else F32) for s in pieces]
    if hand_on:
        kinds.append(jax.ShapeDtypeStruct(data.shape, data.dtype))
    return pl.pallas_call(
        functools.partial(transport_kernel, pieces),
        out_shape=kinds,
        in_specs=[SMEM] + [VMEM] * 3,
        out_specs=[VMEM] * len(kinds),
        input_output_aliases={3: len(pieces)} if hand_on else {},
        compiler_params=params(24),
        cost_estimate=pl.CostEstimate(
            flops=2 * ROWS * COUNT * C * SHARE * len(pieces), bytes_accessed=2 * 2**20 * len(pieces), transcendentals=0
        ),
        name="transport",
    )(place, w, got, data)


def body(noise, data):
    z, x, y, c = (lax.axis_index(a) for a in ("z", "x", "y", "core"))
    place = jnp.stack([z, x, y, c]).astype(jnp.int32)
    dealt = deal(place, data)
    swapped = jnp.stack([dealt[0]] + [shift(dealt[by], "x", by) for by in range(1, X)])
    noise_after, swapped = lax.optimization_barrier((noise, swapped))
    samples = lax.all_gather(swapped, ("z", "core")).reshape(Y, C, C, X, QUARTER, SLICE)
    samples, noise_all, sqn_mine = lax.optimization_barrier((samples, *collect(gather_noise(noise_after))))
    samples = pick(place, samples)
    data_all = lax.all_gather(samples, "x")
    got = shift(theirs(place, samples, noise_all, sqn_mine), "core", 1)
    mine, sq_mine = ours(place, samples, noise_all)
    q, rows, sq, sq_noise = score(mine, sq_mine, sqn_mine, got)
    for step in range(ITERS):
        if step:
            rows = noise_lse(q, columns)
        parts = lax.all_to_all(rows, ("x", "y", "core"), 0, 0)
        if step < ITERS - 1:
            columns, f = data_lse(q, parts)
            columns = lax.all_to_all(columns, "z", 0, 0)
    columns, f, *blocks = last_lse(place, q, parts, sq)
    blocks = [blocks[0]] + [shift(blocks[by], "x", by) for by in range(1, X)]
    columns = lax.all_to_all(columns, ("z", "x"), 0, 0)
    w, pot_g = scale(place, columns, blocks)
    data_all, pot_g = lax.optimization_barrier((data_all, pot_g))
    got = shift(w, "core", 1)
    opposite, data_all = transport(place, w, got, data_all, (2,), True)
    up, down, data_all = transport(place, w, got, data_all, (1, 3), True)
    (target,) = transport(place, w, got, data_all, (0,), False)
    for by, part in zip((2, 1, 3), (opposite, up, down)):
        target = target + shift(part, "y", by).astype(F32)
    velocity = (target - noise.astype(F32)).astype(BF16)
    own = lax.dynamic_index_in_dim(f.reshape(2, X, 128), x, 1, False)
    pot_f = (own * (EPS / LOG2E) + sq_noise / WIDTH).reshape(ROWS)
    return pot_f, pot_g.reshape(COUNT), velocity


def solution(mesh):
    fine = Mesh(mesh.devices.reshape(Z, X, Y, C), ("z", "x", "y", "core"))
    row, col = ("z", "x"), ("y", "core")
    return jax.shard_map(
        body,
        mesh=fine,
        in_specs=(P(row, col), P(col, row)),
        out_specs=(P(row), P(col), P(row, col)),
        check_vma=False,
    )
```

```python
import functools
import math

import jax
import jax.numpy as jnp
from jax import lax
from jax.experimental import pallas as pl
from jax.experimental.pallas import tpu as pltpu
from jax.sharding import Mesh, PartitionSpec as P

ITERS = 3
EPS = 0.01
LOG2E = math.log2(math.e)
Z, X, Y, C = 8, 4, 4, 2
ROWS, SHARE = 256, 512
COUNT, SLICE = 1024, 128
WIDTH = 4096
QUARTER = COUNT // X
TALL = ROWS * X
CHUNKS = TALL // 128
GROUP = X * Y * C
CUT = ROWS // 2
AROUND = (0, -1, 1, 2)
TOTAL = 8192
UNIT = LOG2E / (WIDTH * EPS)
LOG2N = math.log2(TOTAL)
F32, BF16 = jnp.float32, jnp.bfloat16
VMEM = pl.BlockSpec(memory_space=pltpu.VMEM)
SMEM = pl.BlockSpec(memory_space=pltpu.SMEM)


def shift(x, axis, by):
    n = {"z": Z, "x": X, "y": Y, "core": C}[axis]
    return lax.ppermute(x, axis, [(j, (j + by) % n) for j in range(n)])


def params(mib):
    return pltpu.CompilerParams(vmem_limit_bytes=mib * 2**20)


def both_ways(forward, backward, axis):
    return shift(forward, axis, 1), shift(backward, axis, -1)


def halves(forward, backward, axis):
    cut = forward.shape[0] // 2
    return both_ways(forward[:cut], backward[cut:], axis)


def around(block, axis):
    return [block, shift(block, axis, 1), shift(block, axis, -1), shift(block, axis, 2)]


def gather_noise(noise):
    hold = lax.optimization_barrier
    across, along = hold((around(noise[:CUT], "x"), around(noise[CUT:], "y")))
    across, along = jnp.stack(across), jnp.stack(along)
    y1, x1 = hold((both_ways(across, across, "y"), both_ways(along, along, "x")))
    return [across, *y1, *halves(*y1, "y"), along, *x1, *halves(*x1, "x")]


def squares(ref, pieces):
    total = None
    for view in pieces:
        part = ref[view].astype(F32)
        total = part * part if total is None else total + part * part
    return total


def lse(t, axis):
    top = jnp.max(t, axis=axis, keepdims=True)
    return top + jnp.log2(jnp.sum(jnp.exp2(t - top), axis=axis, keepdims=True))


def merged(ref):
    parts = ref[...]
    top = jnp.max(parts, axis=0)
    return top + jnp.log2(jnp.sum(jnp.exp2(parts - top[None]), axis=0))


def chunk(r):
    return pl.ds(r * 128, 128)


def at(place, which, rel, size):
    return lax.rem(place[which] + rel + size, size)


def from_x(x, n):
    return lax.rem(x - n + X, X) if not isinstance(x, int) else (x - n) % X


def blocks_of(parts):
    first, second = parts[:5], parts[5:]

    def of(five, far, near):
        if far < 3:
            return five[far].at[near]
        return five[3 + near // 2].at[near % 2]

    return (
        [[of(first, k, j) for k in range(Y)] for j in range(X)],
        [[of(second, j, k) for k in range(Y)] for j in range(X)],
    )


def collect_kernel(*refs):
    parts, (noise_ref, sqn_ref) = refs[:10], refs[10:]
    rows = []
    for h, blocks in enumerate(blocks_of(parts)):
        for j, row in enumerate(blocks):
            for k, ref in enumerate(row):
                noise_ref[pl.ds((h * X + j) * CUT, CUT), pl.ds(k * SHARE, SHARE)] = ref[...]
        t = [squares(ref, [(slice(None), pl.ds(lane, 128)) for lane in range(0, SHARE, 128)]) for ref in blocks[0]]
        total = (t[0] + t[3]) + (t[1] + t[2])
        rows.append(jnp.sum(jnp.transpose(total), axis=0, keepdims=True))
    sqn_ref[...] = jnp.concatenate(rows, axis=0)


def collect(parts):
    return pl.pallas_call(
        collect_kernel,
        out_shape=(jax.ShapeDtypeStruct((TALL, WIDTH // C), BF16), jax.ShapeDtypeStruct((2, 128), F32)),
        in_specs=[VMEM] * 10,
        out_specs=(VMEM,) * 2,
        compiler_params=params(16),
        name="collect",
    )(*parts)


def pick_kernel(place, all_ref, out_ref, buffer_ref, sems):
    ins = [pltpu.make_async_copy(all_ref.at[y, place[3]], buffer_ref.at[y], sems.at[0, y]) for y in range(Y)]
    outs = [pltpu.make_async_copy(buffer_ref.at[y], out_ref.at[y], sems.at[1, y]) for y in range(Y)]
    for copy in ins:
        copy.start()
    for y in range(Y):
        ins[y].wait()
        outs[y].start()
    for copy in outs:
        copy.wait()


def pick(place, samples):
    half = (Y, C, X, QUARTER, SLICE)
    return pl.pallas_call(
        pick_kernel,
        out_shape=jax.ShapeDtypeStruct(half, BF16),
        in_specs=[SMEM, pl.BlockSpec(memory_space=pl.ANY)],
        out_specs=pl.BlockSpec(memory_space=pl.ANY),
        scratch_shapes=[pltpu.VMEM(half, BF16), pltpu.SemaphoreType.DMA((2, Y))],
        compiler_params=params(53),
        name="pick",
    )(place, samples)


def deal_kernel(place, data_ref, *out_refs):
    for by, ref in enumerate(out_refs):
        ref[...] = data_ref[at(place, 1, by, X)]


def deal(place, data):
    return pl.pallas_call(
        deal_kernel,
        out_shape=(jax.ShapeDtypeStruct((QUARTER, SLICE), BF16),) * X,
        in_specs=[SMEM, VMEM],
        out_specs=(VMEM,) * X,
        compiler_params=params(16),
        name="deal",
    )(place, data.reshape(X, QUARTER, SLICE))


def partial_scores(place, data_ref, core, noise_ref, q_ref, sq_ref):
    pieces = [at(place, 2, rel, Y) for rel in AROUND]
    lhs = jnp.concatenate([data_ref[p, core, from_x(place[1], n)] for p in pieces for n in range(X)], axis=1)
    for h in range(2):
        rhs = noise_ref[pl.ds(h * X * CUT, X * CUT), :]
        gram = lax.dot_general(lhs, rhs, (((1,), (1,)), ((), ())), preferred_element_type=F32) * (2.0 * UNIT)
        for j, rel in enumerate(AROUND):
            lanes = pl.ds(pl.multiple_of((h * X + at(place, 1, rel, X)) * 128, 128), 128)
            q_ref[:QUARTER, lanes] = gram[:, j * 128 : (j + 1) * 128]
    sq_ref[...] = squares(data_ref, [(p, core, n) for p in range(Y) for n in range(X)])


def theirs_kernel(place, data_ref, noise_ref, sqn_ref, out_ref, sq_ref):
    partial_scores(place, data_ref, 1 - place[3], noise_ref, out_ref, sq_ref)
    out_ref[:QUARTER, TALL:] = sq_ref[...]
    out_ref[QUARTER:, :] = jnp.zeros((8, TALL + 128), F32)
    out_ref[QUARTER : QUARTER + 2, :128] = sqn_ref[...]


def theirs(place, data, noise, sqn):
    return pl.pallas_call(
        theirs_kernel,
        out_shape=jax.ShapeDtypeStruct((QUARTER + 8, TALL + 128), F32),
        in_specs=[SMEM] + [VMEM] * 3,
        out_specs=VMEM,
        scratch_shapes=[pltpu.VMEM((QUARTER, 128), F32)],
        compiler_params=params(24),
        name="theirs",
    )(place, data, noise, sqn)


def ours_kernel(place, data_ref, noise_ref, q_ref, sq_ref):
    partial_scores(place, data_ref, place[3], noise_ref, q_ref, sq_ref)


def ours(place, data, noise):
    return pl.pallas_call(
        ours_kernel,
        out_shape=(jax.ShapeDtypeStruct((QUARTER, TALL), F32), jax.ShapeDtypeStruct((QUARTER, 128), F32)),
        in_specs=[SMEM] + [VMEM] * 2,
        out_specs=(VMEM,) * 2,
        compiler_params=params(24),
        cost_estimate=pl.CostEstimate(flops=QUARTER * TALL * WIDTH, bytes_accessed=6 * 2**20, transcendentals=0),
        name="ours",
    )(place, data, noise)


def score_kernel(mine_ref, sq_mine_ref, sqn_mine_ref, got_ref, q_ref, out_ref, sq_ref, sqn_ref, lse_ref):
    sq = jnp.sum(sq_mine_ref[...] + got_ref[:QUARTER, TALL:], axis=1, keepdims=True)
    sq_ref[...] = jnp.broadcast_to(sq, (QUARTER, 128))
    sqn_ref[...] = sqn_mine_ref[...] + got_ref[QUARTER : QUARTER + 2, :128]
    for r in range(CHUNKS):
        q = mine_ref[:, chunk(r)] + got_ref[:QUARTER, chunk(r)]
        q_ref[:, chunk(r)] = q
        lse_ref[pl.ds(r, 1), :] = lse(q - UNIT * sq_ref[...], 0)
    out_ref[...] = jnp.broadcast_to(lse_ref[...][None], (GROUP, CHUNKS, 128))


def score(mine, sq_mine, sqn_mine, got):
    return pl.pallas_call(
        score_kernel,
        out_shape=(
            jax.ShapeDtypeStruct((QUARTER, TALL), F32),
            jax.ShapeDtypeStruct((GROUP, CHUNKS, 128), F32),
            jax.ShapeDtypeStruct((QUARTER, 128), F32),
            jax.ShapeDtypeStruct((2, 128), F32),
        ),
        in_specs=[VMEM] * 4,
        out_specs=(VMEM,) * 4,
        scratch_shapes=[pltpu.VMEM((CHUNKS, 128), F32)],
        compiler_params=params(16),
        name="score",
    )(mine, sq_mine, sqn_mine, got)


def to_column(g):
    return jnp.concatenate([jnp.transpose(jnp.broadcast_to(g[r : r + 1], (128, 128))) for r in range(2)], axis=0)


def noise_kernel(q_ref, part_ref, out_ref, lse_ref, g_ref):
    g_ref[...] = to_column(-LOG2N - merged(part_ref))
    for r in range(CHUNKS):
        lse_ref[pl.ds(r, 1), :] = lse(q_ref[:, chunk(r)] + g_ref[...], 0)
    out_ref[...] = jnp.broadcast_to(lse_ref[...][None], (GROUP, CHUNKS, 128))


def noise_lse(q, parts):
    return pl.pallas_call(
        noise_kernel,
        out_shape=jax.ShapeDtypeStruct((GROUP, CHUNKS, 128), F32),
        in_specs=[VMEM] * 2,
        out_specs=VMEM,
        scratch_shapes=[pltpu.VMEM((CHUNKS, 128), F32), pltpu.VMEM((QUARTER, 128), F32)],
        compiler_params=params(16),
        name="noise_lse",
    )(q, parts)


def data_kernel(q_ref, part_ref, out_ref, f_ref, lane_ref):
    f_ref[...] = -LOG2N - merged(part_ref)
    row = data_row(q_ref, f_ref, lane_ref)
    out_ref[...] = jnp.broadcast_to(two_rows(row)[None], (Z, 8, 128))


def data_row(q_ref, f_ref, lane_ref):
    step = 32
    for start in range(0, QUARTER, step):
        rows = pl.ds(start, step)
        t = [q_ref[rows, chunk(r)] + f_ref[pl.ds(r, 1), :] for r in range(CHUNKS)]
        top = functools.reduce(jnp.maximum, t)
        lane_ref[rows, :] = top + jnp.log2(sum(jnp.exp2(part - top) for part in t))
    return lse(jnp.transpose(lane_ref[...]), 0)


def two_rows(*rows):
    halves = [half for row in rows for half in (row[:, :128], row[:, 128:])]
    return jnp.concatenate(halves + [jnp.zeros((8 - len(halves), 128), F32)], axis=0)


def data_lse(q, parts):
    return pl.pallas_call(
        data_kernel,
        out_shape=(jax.ShapeDtypeStruct((Z, 8, 128), F32), jax.ShapeDtypeStruct((CHUNKS, 128), F32)),
        in_specs=[VMEM] * 2,
        out_specs=(VMEM, VMEM),
        scratch_shapes=[pltpu.VMEM((QUARTER, 128), F32)],
        compiler_params=params(16),
        name="data_lse",
    )(q, parts)


def last_kernel(place, q_ref, part_ref, sq_ref, out_ref, f_ref, *refs):
    w_refs, lane_ref = refs[:X], refs[X]
    f_ref[...] = -LOG2N - merged(part_ref)
    tile = two_rows(data_row(q_ref, f_ref, lane_ref), jnp.transpose(sq_ref[...])[0:1, :])
    out_ref[...] = jnp.broadcast_to(tile[None], (Z * X, 8, 128))
    column = to_column(tile)
    for by in range(X):
        block = lax.rem(place[1] + by, X)
        for h in range(2):
            lanes = pl.ds(pl.multiple_of((h * X + block) * 128, 128), 128)
            w = jnp.exp2((q_ref[:, lanes] + f_ref[pl.ds(h * X + block, 1), :]) - column)
            w_refs[by][:, pl.ds(h * 128, 128)] = w.astype(BF16)


def last_lse(place, q, parts, sq):
    return pl.pallas_call(
        last_kernel,
        out_shape=(jax.ShapeDtypeStruct((Z * X, 8, 128), F32), jax.ShapeDtypeStruct((CHUNKS, 128), F32))
        + (jax.ShapeDtypeStruct((QUARTER, ROWS), BF16),) * X,
        in_specs=[SMEM] + [VMEM] * 3,
        out_specs=(VMEM,) * (2 + X),
        scratch_shapes=[pltpu.VMEM((QUARTER, 128), F32)],
        compiler_params=params(16),
        name="last_lse",
    )(place, q, parts, sq)


def scale_kernel(place, part_ref, *refs):
    w_refs, (w_ref, pot_ref) = refs[:X], refs[X:]
    z, x = place[0], place[1]
    for n in range(X):
        parts = jnp.stack([part_ref[k * X + n, 0:4, :] for k in range(Z)])
        top = jnp.max(parts, axis=0)
        total = top + jnp.log2(jnp.sum(jnp.exp2(parts - top[None]), axis=0))
        pot_ref[pl.ds(2 * n, 2), :] = (-LOG2N - total[0:2]) * (EPS / LOG2E) + parts[0, 2:4] * (1.0 / WIDTH)
    for by in range(X):
        n = lax.rem(x - by + X, X)
        parts = jnp.stack([part_ref[k * X + n] for k in range(Z)])
        top = jnp.max(parts, axis=0)
        total = top + jnp.log2(jnp.sum(jnp.exp2(parts - top[None]), axis=0))
        factor = jnp.exp2(part_ref[z * X + n] - total)
        factor = jnp.concatenate([factor[0:1], factor[1:2]], axis=1)
        lanes = pl.ds(pl.multiple_of(n * QUARTER, QUARTER), QUARTER)
        for h in range(2):
            w = jnp.transpose(w_refs[by][:, pl.ds(h * 128, 128)].astype(F32)) * factor
            w_ref[pl.ds(h * 128, 128), lanes] = w.astype(BF16)


def scale(place, parts, blocks):
    return pl.pallas_call(
        scale_kernel,
        out_shape=(jax.ShapeDtypeStruct((ROWS, COUNT), BF16), jax.ShapeDtypeStruct((2 * X, 128), F32)),
        in_specs=[SMEM] + [VMEM] * (1 + X),
        out_specs=(VMEM,) * 2,
        compiler_params=params(16),
        name="scale",
    )(place, parts, *blocks)


def transport_kernel(pieces, place, w_ref, got_ref, data_ref, *out_refs):
    lhs = jnp.concatenate([w_ref[...], got_ref[...]], axis=1)
    for s, out_ref in zip(pieces, out_refs):
        y = at(place, 2, s, Y)
        rhs = []
        for core in (place[3], 1 - place[3]):
            for n in range(X):
                rhs.append(jnp.concatenate([data_ref[n, y, core, from_x(n, k)] for k in range(X)], axis=1))
        total = jnp.dot(lhs, jnp.concatenate(rhs, axis=0), preferred_element_type=F32)
        out_ref[...] = total.astype(out_ref.dtype)


def transport(place, w, got, data, pieces, hand_on):
    kinds = [jax.ShapeDtypeStruct((ROWS, SHARE), BF16 if s else F32) for s in pieces]
    if hand_on:
        kinds.append(jax.ShapeDtypeStruct(data.shape, data.dtype))
    return pl.pallas_call(
        functools.partial(transport_kernel, pieces),
        out_shape=kinds,
        in_specs=[SMEM] + [VMEM] * 3,
        out_specs=[VMEM] * len(kinds),
        input_output_aliases={3: len(pieces)} if hand_on else {},
        compiler_params=params(24),
        cost_estimate=pl.CostEstimate(
            flops=2 * ROWS * COUNT * C * SHARE * len(pieces), bytes_accessed=2 * 2**20 * len(pieces), transcendentals=0
        ),
        name="transport",
    )(place, w, got, data)


def body(noise, data):
    z, x, y, c = (lax.axis_index(a) for a in ("z", "x", "y", "core"))
    place = jnp.stack([z, x, y, c]).astype(jnp.int32)
    dealt = deal(place, data)
    swapped = jnp.stack([dealt[0]] + [shift(dealt[by], "x", by) for by in range(1, X)])
    noise_after, swapped = lax.optimization_barrier((noise, swapped))
    samples = lax.all_gather(swapped, ("z", "core")).reshape(Y, C, C, X, QUARTER, SLICE)
    samples, noise_all, sqn_mine = lax.optimization_barrier((samples, *collect(gather_noise(noise_after))))
    samples = pick(place, samples)
    data_all = lax.all_gather(samples, "x")
    got = shift(theirs(place, samples, noise_all, sqn_mine), "core", 1)
    mine, sq_mine = ours(place, samples, noise_all)
    q, rows, sq, sq_noise = score(mine, sq_mine, sqn_mine, got)
    for step in range(ITERS):
        if step:
            rows = noise_lse(q, columns)
        parts = lax.all_to_all(rows, ("x", "y", "core"), 0, 0)
        if step < ITERS - 1:
            columns, f = data_lse(q, parts)
            columns = lax.all_to_all(columns, "z", 0, 0)
    columns, f, *blocks = last_lse(place, q, parts, sq)
    blocks = [blocks[0]] + [shift(blocks[by], "x", by) for by in range(1, X)]
    columns = lax.all_to_all(columns, ("z", "x"), 0, 0)
    w, pot_g = scale(place, columns, blocks)
    data_all, pot_g = lax.optimization_barrier((data_all, pot_g))
    got = shift(w, "core", 1)
    opposite, data_all = transport(place, w, got, data_all, (2,), True)
    up, down, data_all = transport(place, w, got, data_all, (1, 3), True)
    (target,) = transport(place, w, got, data_all, (0,), False)
    for by, part in zip((2, 1, 3), (opposite, up, down)):
        target = target + shift(part, "y", by).astype(F32)
    velocity = (target - noise.astype(F32)).astype(BF16)
    own = lax.dynamic_index_in_dim(f.reshape(2, X, 128), x, 1, False)
    pot_f = (own * (EPS / LOG2E) + sq_noise / WIDTH).reshape(ROWS)
    return pot_f, pot_g.reshape(COUNT), velocity


def solution(mesh):
    fine = Mesh(mesh.devices.reshape(Z, X, Y, C), ("z", "x", "y", "core"))
    row, col = ("z", "x"), ("y", "core")
    return jax.shard_map(
        body,
        mesh=fine,
        in_specs=(P(row, col), P(col, row)),
        out_specs=(P(row), P(col), P(row, col)),
        check_vma=False,
    )
```

```python
import functools
import math

import jax
import jax.numpy as jnp
from jax import lax
from jax.experimental import pallas as pl
from jax.experimental.pallas import tpu as pltpu
from jax.sharding import Mesh, PartitionSpec as P

ITERS = 3
EPS = 0.01
LOG2E = math.log2(math.e)
Z, X, Y, C = 8, 4, 4, 2
ROWS, SHARE = 256, 512
COUNT, SLICE = 1024, 128
WIDTH = 4096
QUARTER = COUNT // X
TALL = ROWS * X
CHUNKS = TALL // 128
GROUP = X * Y * C
CUT = ROWS // 2
AROUND = (0, -1, 1, 2)
TOTAL = 8192
UNIT = LOG2E / (WIDTH * EPS)
LOG2N = math.log2(TOTAL)
F32, BF16 = jnp.float32, jnp.bfloat16
VMEM = pl.BlockSpec(memory_space=pltpu.VMEM)
SMEM = pl.BlockSpec(memory_space=pltpu.SMEM)


def shift(x, axis, by):
    n = {"z": Z, "x": X, "y": Y, "core": C}[axis]
    return lax.ppermute(x, axis, [(j, (j + by) % n) for j in range(n)])


def params(mib):
    return pltpu.CompilerParams(vmem_limit_bytes=mib * 2**20)


def both_ways(forward, backward, axis):
    return shift(forward, axis, 1), shift(backward, axis, -1)


def halves(forward, backward, axis):
    cut = forward.shape[0] // 2
    return both_ways(forward[:cut], backward[cut:], axis)


def around(block, axis):
    return [block, shift(block, axis, 1), shift(block, axis, -1), shift(block, axis, 2)]


def gather_noise(noise):
    hold = lax.optimization_barrier
    across, along = hold((around(noise[:CUT], "x"), around(noise[CUT:], "y")))
    across, along = jnp.stack(across), jnp.stack(along)
    y1, x1 = hold((both_ways(across, across, "y"), both_ways(along, along, "x")))
    return [across, *y1, *halves(*y1, "y"), along, *x1, *halves(*x1, "x")]


def squares(ref, pieces):
    total = None
    for view in pieces:
        part = ref[view].astype(F32)
        total = part * part if total is None else total + part * part
    return total


def lse(t, axis):
    top = jnp.max(t, axis=axis, keepdims=True)
    return top + jnp.log2(jnp.sum(jnp.exp2(t - top), axis=axis, keepdims=True))


def merged(ref):
    parts = ref[...]
    top = jnp.max(parts, axis=0)
    return top + jnp.log2(jnp.sum(jnp.exp2(parts - top[None]), axis=0))


def chunk(r):
    return pl.ds(r * 128, 128)


def at(place, which, rel, size):
    return lax.rem(place[which] + rel + size, size)


def from_x(x, n):
    return lax.rem(x - n + X, X) if not isinstance(x, int) else (x - n) % X


def blocks_of(parts):
    first, second = parts[:5], parts[5:]

    def of(five, far, near):
        if far < 3:
            return five[far].at[near]
        return five[3 + near // 2].at[near % 2]

    return (
        [[of(first, k, j) for k in range(Y)] for j in range(X)],
        [[of(second, j, k) for k in range(Y)] for j in range(X)],
    )


def collect_kernel(*refs):
    parts, (noise_ref, sqn_ref) = refs[:10], refs[10:]
    rows = []
    for h, blocks in enumerate(blocks_of(parts)):
        for j, row in enumerate(blocks):
            for k, ref in enumerate(row):
                noise_ref[pl.ds((h * X + j) * CUT, CUT), pl.ds(k * SHARE, SHARE)] = ref[...]
        t = [squares(ref, [(slice(None), pl.ds(lane, 128)) for lane in range(0, SHARE, 128)]) for ref in blocks[0]]
        total = (t[0] + t[3]) + (t[1] + t[2])
        rows.append(jnp.sum(jnp.transpose(total), axis=0, keepdims=True))
    sqn_ref[...] = jnp.concatenate(rows, axis=0)


def collect(parts):
    return pl.pallas_call(
        collect_kernel,
        out_shape=(jax.ShapeDtypeStruct((TALL, WIDTH // C), BF16), jax.ShapeDtypeStruct((2, 128), F32)),
        in_specs=[VMEM] * 10,
        out_specs=(VMEM,) * 2,
        compiler_params=params(16),
        name="collect",
    )(*parts)


def pick_kernel(place, all_ref, out_ref, buffer_ref, sems):
    ins = [pltpu.make_async_copy(all_ref.at[y, place[3]], buffer_ref.at[y], sems.at[0, y]) for y in range(Y)]
    outs = [pltpu.make_async_copy(buffer_ref.at[y], out_ref.at[y], sems.at[1, y]) for y in range(Y)]
    for copy in ins:
        copy.start()
    for y in range(Y):
        ins[y].wait()
        outs[y].start()
    for copy in outs:
        copy.wait()


def pick(place, samples):
    half = (Y, C, X, QUARTER, SLICE)
    return pl.pallas_call(
        pick_kernel,
        out_shape=jax.ShapeDtypeStruct(half, BF16),
        in_specs=[SMEM, pl.BlockSpec(memory_space=pl.ANY)],
        out_specs=pl.BlockSpec(memory_space=pl.ANY),
        scratch_shapes=[pltpu.VMEM(half, BF16), pltpu.SemaphoreType.DMA((2, Y))],
        compiler_params=params(53),
        name="pick",
    )(place, samples)


def deal_kernel(place, data_ref, *out_refs):
    for by, ref in enumerate(out_refs):
        ref[...] = data_ref[at(place, 1, by, X)]


def deal(place, data):
    return pl.pallas_call(
        deal_kernel,
        out_shape=(jax.ShapeDtypeStruct((QUARTER, SLICE), BF16),) * X,
        in_specs=[SMEM, VMEM],
        out_specs=(VMEM,) * X,
        compiler_params=params(16),
        name="deal",
    )(place, data.reshape(X, QUARTER, SLICE))


def partial_scores(place, data_ref, core, noise_ref, q_ref, sq_ref):
    pieces = [at(place, 2, rel, Y) for rel in AROUND]
    lhs = jnp.concatenate([data_ref[p, core, from_x(place[1], n)] for p in pieces for n in range(X)], axis=1)
    for h in range(2):
        rhs = noise_ref[pl.ds(h * X * CUT, X * CUT), :]
        gram = lax.dot_general(lhs, rhs, (((1,), (1,)), ((), ())), preferred_element_type=F32) * (2.0 * UNIT)
        for j, rel in enumerate(AROUND):
            lanes = pl.ds(pl.multiple_of((h * X + at(place, 1, rel, X)) * 128, 128), 128)
            q_ref[:QUARTER, lanes] = gram[:, j * 128 : (j + 1) * 128]
    sq_ref[...] = squares(data_ref, [(p, core, n) for p in range(Y) for n in range(X)])


def theirs_kernel(place, data_ref, noise_ref, sqn_ref, out_ref, sq_ref):
    partial_scores(place, data_ref, 1 - place[3], noise_ref, out_ref, sq_ref)
    out_ref[:QUARTER, TALL:] = sq_ref[...]
    out_ref[QUARTER:, :] = jnp.zeros((8, TALL + 128), F32)
    out_ref[QUARTER : QUARTER + 2, :128] = sqn_ref[...]


def theirs(place, data, noise, sqn):
    return pl.pallas_call(
        theirs_kernel,
        out_shape=jax.ShapeDtypeStruct((QUARTER + 8, TALL + 128), F32),
        in_specs=[SMEM] + [VMEM] * 3,
        out_specs=VMEM,
        scratch_shapes=[pltpu.VMEM((QUARTER, 128), F32)],
        compiler_params=params(24),
        name="theirs",
    )(place, data, noise, sqn)


def ours_kernel(place, data_ref, noise_ref, q_ref, sq_ref):
    partial_scores(place, data_ref, place[3], noise_ref, q_ref, sq_ref)


def ours(place, data, noise):
    return pl.pallas_call(
        ours_kernel,
        out_shape=(jax.ShapeDtypeStruct((QUARTER, TALL), F32), jax.ShapeDtypeStruct((QUARTER, 128), F32)),
        in_specs=[SMEM] + [VMEM] * 2,
        out_specs=(VMEM,) * 2,
        compiler_params=params(24),
        cost_estimate=pl.CostEstimate(flops=QUARTER * TALL * WIDTH, bytes_accessed=6 * 2**20, transcendentals=0),
        name="ours",
    )(place, data, noise)


def score_kernel(mine_ref, sq_mine_ref, sqn_mine_ref, got_ref, q_ref, out_ref, sq_ref, sqn_ref, lse_ref):
    sq = jnp.sum(sq_mine_ref[...] + got_ref[:QUARTER, TALL:], axis=1, keepdims=True)
    sq_ref[...] = jnp.broadcast_to(sq, (QUARTER, 128))
    sqn_ref[...] = sqn_mine_ref[...] + got_ref[QUARTER : QUARTER + 2, :128]
    for r in range(CHUNKS):
        q = mine_ref[:, chunk(r)] + got_ref[:QUARTER, chunk(r)]
        q_ref[:, chunk(r)] = q
        lse_ref[pl.ds(r, 1), :] = lse(q - UNIT * sq_ref[...], 0)
    out_ref[...] = jnp.broadcast_to(lse_ref[...][None], (GROUP, CHUNKS, 128))


def score(mine, sq_mine, sqn_mine, got):
    return pl.pallas_call(
        score_kernel,
        out_shape=(
            jax.ShapeDtypeStruct((QUARTER, TALL), F32),
            jax.ShapeDtypeStruct((GROUP, CHUNKS, 128), F32),
            jax.ShapeDtypeStruct((QUARTER, 128), F32),
            jax.ShapeDtypeStruct((2, 128), F32),
        ),
        in_specs=[VMEM] * 4,
        out_specs=(VMEM,) * 4,
        scratch_shapes=[pltpu.VMEM((CHUNKS, 128), F32)],
        compiler_params=params(16),
        name="score",
    )(mine, sq_mine, sqn_mine, got)


def to_column(g):
    return jnp.concatenate([jnp.transpose(jnp.broadcast_to(g[r : r + 1], (128, 128))) for r in range(2)], axis=0)


def noise_kernel(q_ref, part_ref, out_ref, lse_ref, g_ref):
    g_ref[...] = to_column(-LOG2N - merged(part_ref))
    for r in range(CHUNKS):
        lse_ref[pl.ds(r, 1), :] = lse(q_ref[:, chunk(r)] + g_ref[...], 0)
    out_ref[...] = jnp.broadcast_to(lse_ref[...][None], (GROUP, CHUNKS, 128))


def noise_lse(q, parts):
    return pl.pallas_call(
        noise_kernel,
        out_shape=jax.ShapeDtypeStruct((GROUP, CHUNKS, 128), F32),
        in_specs=[VMEM] * 2,
        out_specs=VMEM,
        scratch_shapes=[pltpu.VMEM((CHUNKS, 128), F32), pltpu.VMEM((QUARTER, 128), F32)],
        compiler_params=params(16),
        name="noise_lse",
    )(q, parts)


def data_kernel(q_ref, part_ref, out_ref, f_ref, lane_ref):
    f_ref[...] = -LOG2N - merged(part_ref)
    row = data_row(q_ref, f_ref, lane_ref)
    out_ref[...] = jnp.broadcast_to(two_rows(row)[None], (Z, 8, 128))


def data_row(q_ref, f_ref, lane_ref):
    step = 32
    for start in range(0, QUARTER, step):
        rows = pl.ds(start, step)
        t = [q_ref[rows, chunk(r)] + f_ref[pl.ds(r, 1), :] for r in range(CHUNKS)]
        top = functools.reduce(jnp.maximum, t)
        lane_ref[rows, :] = top + jnp.log2(sum(jnp.exp2(part - top) for part in t))
    return lse(jnp.transpose(lane_ref[...]), 0)


def two_rows(*rows):
    halves = [half for row in rows for half in (row[:, :128], row[:, 128:])]
    return jnp.concatenate(halves + [jnp.zeros((8 - len(halves), 128), F32)], axis=0)


def data_lse(q, parts):
    return pl.pallas_call(
        data_kernel,
        out_shape=(jax.ShapeDtypeStruct((Z, 8, 128), F32), jax.ShapeDtypeStruct((CHUNKS, 128), F32)),
        in_specs=[VMEM] * 2,
        out_specs=(VMEM, VMEM),
        scratch_shapes=[pltpu.VMEM((QUARTER, 128), F32)],
        compiler_params=params(16),
        name="data_lse",
    )(q, parts)


def last_kernel(q_ref, part_ref, sq_ref, out_ref, f_ref, w_ref, lane_ref):
    f_ref[...] = -LOG2N - merged(part_ref)
    tile = two_rows(data_row(q_ref, f_ref, lane_ref), jnp.transpose(sq_ref[...])[0:1, :])
    out_ref[...] = jnp.broadcast_to(tile[None], (Z * X, 8, 128))
    column = to_column(tile)
    for r in range(CHUNKS):
        w = jnp.exp2((q_ref[:, chunk(r)] + f_ref[pl.ds(r, 1), :]) - column)
        w_ref[r % X, :, chunk(r // X)] = w.astype(BF16)


def last_lse(q, parts, sq):
    return pl.pallas_call(
        last_kernel,
        out_shape=(
            jax.ShapeDtypeStruct((Z * X, 8, 128), F32),
            jax.ShapeDtypeStruct((CHUNKS, 128), F32),
            jax.ShapeDtypeStruct((X, QUARTER, ROWS), BF16),
        ),
        in_specs=[VMEM] * 3,
        out_specs=(VMEM,) * 3,
        scratch_shapes=[pltpu.VMEM((QUARTER, 128), F32)],
        compiler_params=params(16),
        name="last_lse",
    )(q, parts, sq)


def scale_kernel(place, part_ref, block_ref, w_ref, pot_ref):
    for n in range(X):
        parts = jnp.stack([part_ref[k * X + n] for k in range(Z)])
        top = jnp.max(parts, axis=0)
        total = top + jnp.log2(jnp.sum(jnp.exp2(parts - top[None]), axis=0))
        pot_ref[pl.ds(2 * n, 2), :] = (-LOG2N - total[0:2]) * (EPS / LOG2E) + parts[0, 2:4] * (1.0 / WIDTH)
        factor = jnp.exp2(part_ref[place[0] * X + n] - total)
        factor = jnp.concatenate([factor[0:1], factor[1:2]], axis=1)
        for h in range(2):
            w = jnp.transpose(block_ref[n, :, chunk(h)].astype(F32)) * factor
            w_ref[pl.ds(h * 128, 128), pl.ds(n * QUARTER, QUARTER)] = w.astype(BF16)


def scale(place, parts, blocks):
    return pl.pallas_call(
        scale_kernel,
        out_shape=(jax.ShapeDtypeStruct((ROWS, COUNT), BF16), jax.ShapeDtypeStruct((2 * X, 128), F32)),
        in_specs=[SMEM] + [VMEM] * 2,
        out_specs=(VMEM,) * 2,
        compiler_params=params(16),
        name="scale",
    )(place, parts, blocks)


def rows_of(place, data_ref, s, core):
    y = at(place, 2, s, Y)
    return jnp.concatenate(
        [jnp.concatenate([data_ref[n, y, core, from_x(n, k)] for k in range(X)], axis=1) for n in range(X)], axis=0
    )


def transport_kernel(pieces, place, w_ref, got_ref, data_ref, *out_refs):
    lhs = jnp.concatenate([w_ref[...], got_ref[...]], axis=1)
    for s, out_ref in zip(pieces, out_refs):
        rhs = jnp.concatenate([rows_of(place, data_ref, s, core) for core in (place[3], 1 - place[3])], axis=0)
        out_ref[...] = jnp.dot(lhs, rhs, preferred_element_type=F32).astype(out_ref.dtype)


def transport(place, w, got, data, pieces, hand_on):
    kinds = [jax.ShapeDtypeStruct((ROWS, SHARE), BF16 if s else F32) for s in pieces]
    if hand_on:
        kinds.append(jax.ShapeDtypeStruct(data.shape, data.dtype))
    return pl.pallas_call(
        functools.partial(transport_kernel, pieces),
        out_shape=kinds,
        in_specs=[SMEM] + [VMEM] * 3,
        out_specs=[VMEM] * len(kinds),
        input_output_aliases={3: len(pieces)} if hand_on else {},
        compiler_params=params(24),
        cost_estimate=pl.CostEstimate(
            flops=2 * ROWS * COUNT * C * SHARE * len(pieces), bytes_accessed=2 * 2**20 * len(pieces), transcendentals=0
        ),
        name="transport",
    )(place, w, got, data)


def body(noise, data):
    z, x, y, c = (lax.axis_index(a) for a in ("z", "x", "y", "core"))
    place = jnp.stack([z, x, y, c]).astype(jnp.int32)
    dealt = deal(place, data)
    swapped = jnp.stack([dealt[0]] + [shift(dealt[by], "x", by) for by in range(1, X)])
    noise_after, swapped = lax.optimization_barrier((noise, swapped))
    samples = lax.all_gather(swapped, ("z", "core")).reshape(Y, C, C, X, QUARTER, SLICE)
    samples, noise_all, sqn_mine = lax.optimization_barrier((samples, *collect(gather_noise(noise_after))))
    samples = pick(place, samples)
    data_all = lax.all_gather(samples, "x")
    got = shift(theirs(place, samples, noise_all, sqn_mine), "core", 1)
    mine, sq_mine = ours(place, samples, noise_all)
    q, rows, sq, sq_noise = score(mine, sq_mine, sqn_mine, got)
    for step in range(ITERS):
        if step:
            rows = noise_lse(q, columns)
        parts = lax.all_to_all(rows, ("x", "y", "core"), 0, 0)
        if step < ITERS - 1:
            columns, f = data_lse(q, parts)
            columns = lax.all_to_all(columns, "z", 0, 0)
    columns, f, blocks = last_lse(q, parts, sq)
    blocks = lax.all_to_all(blocks, "x", 0, 0)
    columns = lax.all_to_all(columns, ("z", "x"), 0, 0)
    w, pot_g = scale(place, columns, blocks)
    data_all, pot_g = lax.optimization_barrier((data_all, pot_g))
    got = shift(w, "core", 1)
    opposite, data_all = transport(place, w, got, data_all, (2,), True)
    up, down, data_all = transport(place, w, got, data_all, (1, 3), True)
    (target,) = transport(place, w, got, data_all, (0,), False)
    for by, part in zip((2, 1, 3), (opposite, up, down)):
        target = target + shift(part, "y", by).astype(F32)
    velocity = (target - noise.astype(F32)).astype(BF16)
    own = lax.dynamic_index_in_dim(f.reshape(2, X, 128), x, 1, False)
    pot_f = (own * (EPS / LOG2E) + sq_noise / WIDTH).reshape(ROWS)
    return pot_f, pot_g.reshape(COUNT), velocity


def solution(mesh):
    fine = Mesh(mesh.devices.reshape(Z, X, Y, C), ("z", "x", "y", "core"))
    row, col = ("z", "x"), ("y", "core")
    return jax.shard_map(
        body,
        mesh=fine,
        in_specs=(P(row, col), P(col, row)),
        out_specs=(P(row), P(col), P(row, col)),
        check_vma=False,
    )
```

```python
import functools
import math

import jax
import jax.numpy as jnp
from jax import lax
from jax.experimental import pallas as pl
from jax.experimental.pallas import tpu as pltpu
from jax.sharding import Mesh, PartitionSpec as P

ITERS = 3
EPS = 0.01
LOG2E = math.log2(math.e)
Z, X, Y, C = 8, 4, 4, 2
ROWS, SHARE = 256, 512
COUNT, SLICE = 1024, 128
WIDTH = 4096
QUARTER = COUNT // X
TALL = ROWS * X
CHUNKS = TALL // 128
GROUP = X * Y * C
CUT = ROWS // 2
AROUND = (0, -1, 1, 2)
TOTAL = 8192
UNIT = LOG2E / (WIDTH * EPS)
LOG2N = math.log2(TOTAL)
F32, BF16 = jnp.float32, jnp.bfloat16
VMEM = pl.BlockSpec(memory_space=pltpu.VMEM)
SMEM = pl.BlockSpec(memory_space=pltpu.SMEM)


def shift(x, axis, by):
    n = {"z": Z, "x": X, "y": Y, "core": C}[axis]
    return lax.ppermute(x, axis, [(j, (j + by) % n) for j in range(n)])


def params(mib):
    return pltpu.CompilerParams(vmem_limit_bytes=mib * 2**20)


def both_ways(forward, backward, axis):
    return shift(forward, axis, 1), shift(backward, axis, -1)


def halves(forward, backward, axis):
    cut = forward.shape[0] // 2
    return both_ways(forward[:cut], backward[cut:], axis)


def around(block, axis):
    return [block, shift(block, axis, 1), shift(block, axis, -1), shift(block, axis, 2)]


def gather_noise(noise):
    hold = lax.optimization_barrier
    across, along = hold((around(noise[:CUT], "x"), around(noise[CUT:], "y")))
    across, along = jnp.stack(across), jnp.stack(along)
    y1, x1 = hold((both_ways(across, across, "y"), both_ways(along, along, "x")))
    return [across, *y1, *halves(*y1, "y"), along, *x1, *halves(*x1, "x")]


def squares(ref, pieces):
    total = None
    for view in pieces:
        part = ref[view].astype(F32)
        total = part * part if total is None else total + part * part
    return total


def lse(t, axis):
    top = jnp.max(t, axis=axis, keepdims=True)
    return top + jnp.log2(jnp.sum(jnp.exp2(t - top), axis=axis, keepdims=True))


def merged(ref):
    parts = ref[...]
    top = jnp.max(parts, axis=0)
    return top + jnp.log2(jnp.sum(jnp.exp2(parts - top[None]), axis=0))


def chunk(r):
    return pl.ds(r * 128, 128)


def at(place, which, rel, size):
    return lax.rem(place[which] + rel + size, size)


def from_x(x, n):
    return lax.rem(x - n + X, X) if not isinstance(x, int) else (x - n) % X


def blocks_of(parts):
    first, second = parts[:5], parts[5:]

    def of(five, far, near):
        if far < 3:
            return five[far].at[near]
        return five[3 + near // 2].at[near % 2]

    return (
        [[of(first, k, j) for k in range(Y)] for j in range(X)],
        [[of(second, j, k) for k in range(Y)] for j in range(X)],
    )


def collect_kernel(*refs):
    parts, (noise_ref, sqn_ref) = refs[:10], refs[10:]
    rows = []
    for h, blocks in enumerate(blocks_of(parts)):
        for j, row in enumerate(blocks):
            for k, ref in enumerate(row):
                noise_ref[pl.ds((h * X + j) * CUT, CUT), pl.ds(k * SHARE, SHARE)] = ref[...]
        t = [squares(ref, [(slice(None), pl.ds(lane, 128)) for lane in range(0, SHARE, 128)]) for ref in blocks[0]]
        total = (t[0] + t[3]) + (t[1] + t[2])
        rows.append(jnp.sum(jnp.transpose(total), axis=0, keepdims=True))
    sqn_ref[...] = jnp.concatenate(rows, axis=0)


def collect(parts):
    return pl.pallas_call(
        collect_kernel,
        out_shape=(jax.ShapeDtypeStruct((TALL, WIDTH // C), BF16), jax.ShapeDtypeStruct((2, 128), F32)),
        in_specs=[VMEM] * 10,
        out_specs=(VMEM,) * 2,
        compiler_params=params(16),
        name="collect",
    )(*parts)


def pick_kernel(place, all_ref, far_ref, near_ref, buffer_ref, sems):
    ins, outs = [], []
    for s in range(Y):
        ins.append(pltpu.make_async_copy(all_ref.at[at(place, 2, s, Y), place[3]], buffer_ref.at[s], sems.at[0, s]))
        out = far_ref.at[s - 1] if s else near_ref
        outs.append(pltpu.make_async_copy(buffer_ref.at[s], out, sems.at[1, s]))
    for copy in ins:
        copy.start()
    for s in range(Y):
        ins[s].wait()
        outs[s].start()
    for copy in outs:
        copy.wait()


def pick(place, samples):
    part = (C, X, QUARTER, SLICE)
    return pl.pallas_call(
        pick_kernel,
        out_shape=(jax.ShapeDtypeStruct((Y - 1, *part), BF16), jax.ShapeDtypeStruct(part, BF16)),
        in_specs=[SMEM, pl.BlockSpec(memory_space=pl.ANY)],
        out_specs=(pl.BlockSpec(memory_space=pl.ANY),) * 2,
        scratch_shapes=[pltpu.VMEM((Y, *part), BF16), pltpu.SemaphoreType.DMA((2, Y))],
        compiler_params=params(53),
        name="pick",
    )(place, samples)


def deal_kernel(place, data_ref, *out_refs):
    for by, ref in enumerate(out_refs):
        ref[...] = data_ref[at(place, 1, by, X)]


def deal(place, data):
    return pl.pallas_call(
        deal_kernel,
        out_shape=(jax.ShapeDtypeStruct((QUARTER, SLICE), BF16),) * X,
        in_specs=[SMEM, VMEM],
        out_specs=(VMEM,) * X,
        compiler_params=params(16),
        name="deal",
    )(place, data.reshape(X, QUARTER, SLICE))


def partial_scores(place, far_ref, near_ref, core, noise_ref, q_ref, sq_ref):
    pieces = [far_ref.at[rel % Y - 1] if rel else near_ref for rel in AROUND]
    lhs = jnp.concatenate([piece[core, from_x(place[1], n)] for piece in pieces for n in range(X)], axis=1)
    for h in range(2):
        rhs = noise_ref[pl.ds(h * X * CUT, X * CUT), :]
        gram = lax.dot_general(lhs, rhs, (((1,), (1,)), ((), ())), preferred_element_type=F32) * (2.0 * UNIT)
        for j, rel in enumerate(AROUND):
            lanes = pl.ds(pl.multiple_of((h * X + at(place, 1, rel, X)) * 128, 128), 128)
            q_ref[:QUARTER, lanes] = gram[:, j * 128 : (j + 1) * 128]
    total = [squares(piece, [(core, n) for n in range(X)]) for piece in pieces]
    sq_ref[...] = (total[0] + total[3]) + (total[1] + total[2])


def theirs_kernel(place, far_ref, near_ref, noise_ref, sqn_ref, out_ref, sq_ref):
    partial_scores(place, far_ref, near_ref, 1 - place[3], noise_ref, out_ref, sq_ref)
    out_ref[:QUARTER, TALL:] = sq_ref[...]
    out_ref[QUARTER:, :] = jnp.zeros((8, TALL + 128), F32)
    out_ref[QUARTER : QUARTER + 2, :128] = sqn_ref[...]


def theirs(place, far, near, noise, sqn):
    return pl.pallas_call(
        theirs_kernel,
        out_shape=jax.ShapeDtypeStruct((QUARTER + 8, TALL + 128), F32),
        in_specs=[SMEM] + [VMEM] * 4,
        out_specs=VMEM,
        scratch_shapes=[pltpu.VMEM((QUARTER, 128), F32)],
        compiler_params=params(24),
        name="theirs",
    )(place, far, near, noise, sqn)


def ours_kernel(place, far_ref, near_ref, noise_ref, q_ref, sq_ref):
    partial_scores(place, far_ref, near_ref, place[3], noise_ref, q_ref, sq_ref)


def ours(place, far, near, noise):
    return pl.pallas_call(
        ours_kernel,
        out_shape=(jax.ShapeDtypeStruct((QUARTER, TALL), F32), jax.ShapeDtypeStruct((QUARTER, 128), F32)),
        in_specs=[SMEM] + [VMEM] * 3,
        out_specs=(VMEM,) * 2,
        compiler_params=params(24),
        cost_estimate=pl.CostEstimate(flops=QUARTER * TALL * WIDTH, bytes_accessed=6 * 2**20, transcendentals=0),
        name="ours",
    )(place, far, near, noise)


def score_kernel(mine_ref, sq_mine_ref, sqn_mine_ref, got_ref, q_ref, out_ref, sq_ref, sqn_ref, lse_ref):
    sq = jnp.sum(sq_mine_ref[...] + got_ref[:QUARTER, TALL:], axis=1, keepdims=True)
    sq_ref[...] = jnp.broadcast_to(sq, (QUARTER, 128))
    sqn_ref[...] = sqn_mine_ref[...] + got_ref[QUARTER : QUARTER + 2, :128]
    for r in range(CHUNKS):
        q = mine_ref[:, chunk(r)] + got_ref[:QUARTER, chunk(r)]
        q_ref[:, chunk(r)] = q
        lse_ref[pl.ds(r, 1), :] = lse(q - UNIT * sq_ref[...], 0)
    out_ref[...] = jnp.broadcast_to(lse_ref[...][None], (GROUP, CHUNKS, 128))


def score(mine, sq_mine, sqn_mine, got):
    return pl.pallas_call(
        score_kernel,
        out_shape=(
            jax.ShapeDtypeStruct((QUARTER, TALL), F32),
            jax.ShapeDtypeStruct((GROUP, CHUNKS, 128), F32),
            jax.ShapeDtypeStruct((QUARTER, 128), F32),
            jax.ShapeDtypeStruct((2, 128), F32),
        ),
        in_specs=[VMEM] * 4,
        out_specs=(VMEM,) * 4,
        scratch_shapes=[pltpu.VMEM((CHUNKS, 128), F32)],
        compiler_params=params(16),
        name="score",
    )(mine, sq_mine, sqn_mine, got)


def to_column(g):
    return jnp.concatenate([jnp.transpose(jnp.broadcast_to(g[r : r + 1], (128, 128))) for r in range(2)], axis=0)


def noise_kernel(q_ref, part_ref, out_ref, lse_ref, g_ref):
    g_ref[...] = to_column(-LOG2N - merged(part_ref))
    for r in range(CHUNKS):
        lse_ref[pl.ds(r, 1), :] = lse(q_ref[:, chunk(r)] + g_ref[...], 0)
    out_ref[...] = jnp.broadcast_to(lse_ref[...][None], (GROUP, CHUNKS, 128))


def noise_lse(q, parts):
    return pl.pallas_call(
        noise_kernel,
        out_shape=jax.ShapeDtypeStruct((GROUP, CHUNKS, 128), F32),
        in_specs=[VMEM] * 2,
        out_specs=VMEM,
        scratch_shapes=[pltpu.VMEM((CHUNKS, 128), F32), pltpu.VMEM((QUARTER, 128), F32)],
        compiler_params=params(16),
        name="noise_lse",
    )(q, parts)


def data_kernel(q_ref, part_ref, out_ref, f_ref, lane_ref):
    f_ref[...] = -LOG2N - merged(part_ref)
    row = data_row(q_ref, f_ref, lane_ref)
    out_ref[...] = jnp.broadcast_to(two_rows(row)[None], (Z, 8, 128))


def data_row(q_ref, f_ref, lane_ref):
    step = 32
    for start in range(0, QUARTER, step):
        rows = pl.ds(start, step)
        t = [q_ref[rows, chunk(r)] + f_ref[pl.ds(r, 1), :] for r in range(CHUNKS)]
        top = functools.reduce(jnp.maximum, t)
        lane_ref[rows, :] = top + jnp.log2(sum(jnp.exp2(part - top) for part in t))
    return lse(jnp.transpose(lane_ref[...]), 0)


def two_rows(*rows):
    halves = [half for row in rows for half in (row[:, :128], row[:, 128:])]
    return jnp.concatenate(halves + [jnp.zeros((8 - len(halves), 128), F32)], axis=0)


def data_lse(q, parts):
    return pl.pallas_call(
        data_kernel,
        out_shape=(jax.ShapeDtypeStruct((Z, 8, 128), F32), jax.ShapeDtypeStruct((CHUNKS, 128), F32)),
        in_specs=[VMEM] * 2,
        out_specs=(VMEM, VMEM),
        scratch_shapes=[pltpu.VMEM((QUARTER, 128), F32)],
        compiler_params=params(16),
        name="data_lse",
    )(q, parts)


def last_kernel(place, q_ref, part_ref, sq_ref, out_ref, f_ref, *refs):
    w_refs, lane_ref = refs[:X], refs[X]
    f_ref[...] = -LOG2N - merged(part_ref)
    tile = two_rows(data_row(q_ref, f_ref, lane_ref), jnp.transpose(sq_ref[...])[0:1, :])
    out_ref[...] = jnp.broadcast_to(tile[None], (Z * X, 8, 128))
    column = to_column(tile)
    for by in range(X):
        block = lax.rem(place[1] + by, X)
        for h in range(2):
            lanes = pl.ds(pl.multiple_of((h * X + block) * 128, 128), 128)
            w = jnp.exp2((q_ref[:, lanes] + f_ref[pl.ds(h * X + block, 1), :]) - column)
            w_refs[by][:, pl.ds(h * 128, 128)] = w.astype(BF16)


def last_lse(place, q, parts, sq):
    return pl.pallas_call(
        last_kernel,
        out_shape=(jax.ShapeDtypeStruct((Z * X, 8, 128), F32), jax.ShapeDtypeStruct((CHUNKS, 128), F32))
        + (jax.ShapeDtypeStruct((QUARTER, ROWS), BF16),) * X,
        in_specs=[SMEM] + [VMEM] * 3,
        out_specs=(VMEM,) * (2 + X),
        scratch_shapes=[pltpu.VMEM((QUARTER, 128), F32)],
        compiler_params=params(16),
        name="last_lse",
    )(place, q, parts, sq)


def scale_kernel(place, part_ref, *refs):
    w_refs, (w_ref, pot_ref) = refs[:X], refs[X:]
    z, x = place[0], place[1]
    for n in range(X):
        parts = jnp.stack([part_ref[k * X + n, 0:4, :] for k in range(Z)])
        top = jnp.max(parts, axis=0)
        total = top + jnp.log2(jnp.sum(jnp.exp2(parts - top[None]), axis=0))
        pot_ref[pl.ds(2 * n, 2), :] = (-LOG2N - total[0:2]) * (EPS / LOG2E) + parts[0, 2:4] * (1.0 / WIDTH)
    for by in range(X):
        n = lax.rem(x - by + X, X)
        parts = jnp.stack([part_ref[k * X + n] for k in range(Z)])
        top = jnp.max(parts, axis=0)
        total = top + jnp.log2(jnp.sum(jnp.exp2(parts - top[None]), axis=0))
        factor = jnp.exp2(part_ref[z * X + n] - total)
        factor = jnp.concatenate([factor[0:1], factor[1:2]], axis=1)
        lanes = pl.ds(pl.multiple_of(n * QUARTER, QUARTER), QUARTER)
        for h in range(2):
            w = jnp.transpose(w_refs[by][:, pl.ds(h * 128, 128)].astype(F32)) * factor
            w_ref[pl.ds(h * 128, 128), lanes] = w.astype(BF16)


def scale(place, parts, blocks):
    return pl.pallas_call(
        scale_kernel,
        out_shape=(jax.ShapeDtypeStruct((ROWS, COUNT), BF16), jax.ShapeDtypeStruct((2 * X, 128), F32)),
        in_specs=[SMEM] + [VMEM] * (1 + X),
        out_specs=(VMEM,) * 2,
        compiler_params=params(16),
        name="scale",
    )(place, parts, *blocks)


def transport_kernel(pieces, place, w_ref, got_ref, data_ref, *out_refs):
    lhs = jnp.concatenate([w_ref[...], got_ref[...]], axis=1)
    for s, out_ref in zip(pieces, out_refs):
        rhs = []
        for core in (place[3], 1 - place[3]):
            for n in range(X):
                rhs.append(jnp.concatenate([data_ref[n, s - 1, core, from_x(n, k)] for k in range(X)], axis=1))
        total = jnp.dot(lhs, jnp.concatenate(rhs, axis=0), preferred_element_type=F32)
        out_ref[...] = total.astype(out_ref.dtype)


def transport(place, w, got, data, pieces, hand_on):
    kinds = [jax.ShapeDtypeStruct((ROWS, SHARE), BF16) for _ in pieces]
    if hand_on:
        kinds.append(jax.ShapeDtypeStruct(data.shape, data.dtype))
    return pl.pallas_call(
        functools.partial(transport_kernel, pieces),
        out_shape=kinds,
        in_specs=[SMEM] + [VMEM] * 3,
        out_specs=[VMEM] * len(kinds),
        input_output_aliases={3: len(pieces)} if hand_on else {},
        compiler_params=params(24),
        cost_estimate=pl.CostEstimate(
            flops=2 * ROWS * COUNT * C * SHARE * len(pieces), bytes_accessed=2 * 2**20 * len(pieces), transcendentals=0
        ),
        name="transport",
    )(place, w, got, data)


def near_scale_kernel(place, part_ref, *refs):
    blocks, out_ref = refs[:X], refs[X]
    parts = jnp.stack([part_ref[k * X + place[1]] for k in range(Z)])
    top = jnp.max(parts, axis=0)
    total = top + jnp.log2(jnp.sum(jnp.exp2(parts - top[None]), axis=0))
    column = to_column(jnp.exp2(part_ref[place[0] * X + place[1]] - total))
    for by in range(X):
        for h in range(2):
            out_ref[by, :, chunk(h)] = (blocks[by][:, chunk(h)].astype(F32) * column).astype(BF16)


def near_scale(place, parts, blocks):
    return pl.pallas_call(
        near_scale_kernel,
        out_shape=jax.ShapeDtypeStruct((X, QUARTER, ROWS), BF16),
        in_specs=[SMEM] + [VMEM] * (1 + X),
        out_specs=VMEM,
        compiler_params=params(16),
        name="near_scale",
    )(place, parts, *blocks)


def near_kernel(place, w_ref, got_ref, data_ref, own_ref, *out_refs):
    rhs = [
        jnp.concatenate([data_ref[core, from_x(place[1], k)] for k in range(X)], axis=1)
        for core in (place[3], 1 - place[3])
    ]
    rhs = jnp.concatenate(rhs, axis=0)
    for by in range(X):
        lhs = jnp.concatenate([w_ref[by], got_ref[by]], axis=0)
        total = lax.dot_general(lhs, rhs, (((0,), (0,)), ((), ())), preferred_element_type=F32)
        if by:
            out_refs[by - 1][...] = total.astype(BF16)
        else:
            own_ref[...] = total


def near_transport(place, w, got, data):
    return pl.pallas_call(
        near_kernel,
        out_shape=(jax.ShapeDtypeStruct((ROWS, SHARE), F32),)
        + (jax.ShapeDtypeStruct((ROWS, SHARE), BF16),) * (X - 1),
        in_specs=[SMEM] + [VMEM] * 3,
        out_specs=(VMEM,) * X,
        compiler_params=params(16),
        name="near",
    )(place, w, got, data)


def body(noise, data):
    z, x, y, c = (lax.axis_index(a) for a in ("z", "x", "y", "core"))
    place = jnp.stack([z, x, y, c]).astype(jnp.int32)
    dealt = deal(place, data)
    swapped = jnp.stack([dealt[0]] + [shift(dealt[by], "x", by) for by in range(1, X)])
    noise_after, swapped = lax.optimization_barrier((noise, swapped))
    samples = lax.all_gather(swapped, ("z", "core")).reshape(Y, C, C, X, QUARTER, SLICE)
    samples, noise_all, sqn_mine = lax.optimization_barrier((samples, *collect(gather_noise(noise_after))))
    far, near = pick(place, samples)
    data_all = lax.all_gather(far, "x")
    got = shift(theirs(place, far, near, noise_all, sqn_mine), "core", 1)
    mine, sq_mine = ours(place, far, near, noise_all)
    q, rows, sq, sq_noise = score(mine, sq_mine, sqn_mine, got)
    for step in range(ITERS):
        if step:
            rows = noise_lse(q, columns)
        parts = lax.all_to_all(rows, ("x", "y", "core"), 0, 0)
        if step < ITERS - 1:
            columns, f = data_lse(q, parts)
            columns = lax.all_to_all(columns, "z", 0, 0)
    columns, f, *blocks = last_lse(place, q, parts, sq)
    given, blocks = blocks, [blocks[0]] + [shift(blocks[by], "x", by) for by in range(1, X)]
    columns = lax.all_to_all(columns, ("z", "x"), 0, 0)
    w, pot_g = scale(place, columns, blocks)
    data_all, pot_g = lax.optimization_barrier((data_all, pot_g))
    got = shift(w, "core", 1)
    opposite, data_all = transport(place, w, got, data_all, (2,), True)
    up, down = transport(place, w, got, data_all, (1, 3), False)
    near_w = near_scale(place, columns, given)
    near_w, opposite = lax.optimization_barrier((near_w, opposite))
    target, *rest = near_transport(place, near_w, shift(near_w, "core", 1), near)
    for by, part in zip((2, 1, 3), (opposite, up, down)):
        target = target + shift(part, "y", by).astype(F32)
    for by, part in zip((2, 1, 3), (rest[1], rest[0], rest[2])):
        target = target + shift(part, "x", by).astype(F32)
    velocity = (target - noise.astype(F32)).astype(BF16)
    own = lax.dynamic_index_in_dim(f.reshape(2, X, 128), x, 1, False)
    pot_f = (own * (EPS / LOG2E) + sq_noise / WIDTH).reshape(ROWS)
    return pot_f, pot_g.reshape(COUNT), velocity


def solution(mesh):
    fine = Mesh(mesh.devices.reshape(Z, X, Y, C), ("z", "x", "y", "core"))
    row, col = ("z", "x"), ("y", "core")
    return jax.shard_map(
        body,
        mesh=fine,
        in_specs=(P(row, col), P(col, row)),
        out_specs=(P(row), P(col), P(row, col)),
        check_vma=False,
    )
```

```python
import functools
import math

import jax
import jax.numpy as jnp
from jax import lax
from jax.experimental import pallas as pl
from jax.experimental.pallas import tpu as pltpu
from jax.sharding import Mesh, PartitionSpec as P

ITERS = 3
EPS = 0.01
LOG2E = math.log2(math.e)
Z, X, Y, C = 8, 4, 4, 2
ROWS, SHARE = 256, 512
COUNT, SLICE = 1024, 128
WIDTH = 4096
QUARTER = COUNT // X
TALL = ROWS * X
CHUNKS = TALL // 128
GROUP = X * Y * C
CUT = ROWS // 2
AROUND = (0, -1, 1, 2)
TOTAL = 8192
UNIT = LOG2E / (WIDTH * EPS)
LOG2N = math.log2(TOTAL)
F32, BF16 = jnp.float32, jnp.bfloat16
VMEM = pl.BlockSpec(memory_space=pltpu.VMEM)
SMEM = pl.BlockSpec(memory_space=pltpu.SMEM)


def shift(x, axis, by):
    n = {"z": Z, "x": X, "y": Y, "core": C}[axis]
    return lax.ppermute(x, axis, [(j, (j + by) % n) for j in range(n)])


def params(mib):
    return pltpu.CompilerParams(vmem_limit_bytes=mib * 2**20)


def both_ways(forward, backward, axis):
    return shift(forward, axis, 1), shift(backward, axis, -1)


def halves(forward, backward, axis):
    cut = forward.shape[0] // 2
    return both_ways(forward[:cut], backward[cut:], axis)


def around(block, axis):
    far = shift(block, axis, 2)
    return [block, shift(block, axis, 1), shift(block, axis, -1), far]


def gather_noise(noise):
    hold = lax.optimization_barrier
    across, along = hold((around(noise[:CUT], "x"), around(noise[CUT:], "y")))
    across, along = jnp.stack(across), jnp.stack(along)
    y1, x1 = hold((both_ways(across, across, "y"), both_ways(along, along, "x")))
    return [across, *y1, *halves(*y1, "y"), along, *x1, *halves(*x1, "x")]


def squares(ref, pieces):
    total = None
    for view in pieces:
        part = ref[view].astype(F32)
        total = part * part if total is None else total + part * part
    return total


def lse(t, axis):
    top = jnp.max(t, axis=axis, keepdims=True)
    return top + jnp.log2(jnp.sum(jnp.exp2(t - top), axis=axis, keepdims=True))


def merged(ref):
    parts = ref[...]
    top = jnp.max(parts, axis=0)
    return top + jnp.log2(jnp.sum(jnp.exp2(parts - top[None]), axis=0))


def chunk(r):
    return pl.ds(r * 128, 128)


def at(place, which, rel, size):
    return lax.rem(place[which] + rel + size, size)


def from_x(x, n):
    return lax.rem(x - n + X, X) if not isinstance(x, int) else (x - n) % X


def blocks_of(parts):
    first, second = parts[:5], parts[5:]

    def of(five, far, near):
        if far < 3:
            return five[far].at[near]
        return five[3 + near // 2].at[near % 2]

    return (
        [[of(first, k, j) for k in range(Y)] for j in range(X)],
        [[of(second, j, k) for k in range(Y)] for j in range(X)],
    )


def collect_kernel(*refs):
    parts, (noise_ref, sqn_ref) = refs[:10], refs[10:]
    rows = []
    for h, blocks in enumerate(blocks_of(parts)):
        for j, row in enumerate(blocks):
            for k, ref in enumerate(row):
                noise_ref[pl.ds((h * X + j) * CUT, CUT), pl.ds(k * SHARE, SHARE)] = ref[...]
        t = [squares(ref, [(slice(None), pl.ds(lane, 128)) for lane in range(0, SHARE, 128)]) for ref in blocks[0]]
        total = (t[0] + t[3]) + (t[1] + t[2])
        rows.append(jnp.sum(jnp.transpose(total), axis=0, keepdims=True))
    sqn_ref[...] = jnp.concatenate(rows, axis=0)


def collect(parts):
    return pl.pallas_call(
        collect_kernel,
        out_shape=(jax.ShapeDtypeStruct((TALL, WIDTH // C), BF16), jax.ShapeDtypeStruct((2, 128), F32)),
        in_specs=[VMEM] * 10,
        out_specs=(VMEM,) * 2,
        compiler_params=params(16),
        name="collect",
    )(*parts)


def pick_kernel(place, all_ref, out_ref, buffer_ref, sems):
    ins = [pltpu.make_async_copy(all_ref.at[y, place[3]], buffer_ref.at[y], sems.at[0, y]) for y in range(Y)]
    outs = [pltpu.make_async_copy(buffer_ref.at[y], out_ref.at[y], sems.at[1, y]) for y in range(Y)]
    for copy in ins:
        copy.start()
    for y in range(Y):
        ins[y].wait()
        outs[y].start()
    for copy in outs:
        copy.wait()


def pick(place, samples):
    half = (Y, C, X, QUARTER, SLICE)
    return pl.pallas_call(
        pick_kernel,
        out_shape=jax.ShapeDtypeStruct(half, BF16),
        in_specs=[SMEM, pl.BlockSpec(memory_space=pl.ANY)],
        out_specs=pl.BlockSpec(memory_space=pl.ANY),
        scratch_shapes=[pltpu.VMEM(half, BF16), pltpu.SemaphoreType.DMA((2, Y))],
        compiler_params=params(53),
        name="pick",
    )(place, samples)


def deal_kernel(place, data_ref, *out_refs):
    for by, ref in enumerate(out_refs):
        ref[...] = data_ref[at(place, 1, by, X)]


def deal(place, data):
    return pl.pallas_call(
        deal_kernel,
        out_shape=(jax.ShapeDtypeStruct((QUARTER, SLICE), BF16),) * X,
        in_specs=[SMEM, VMEM],
        out_specs=(VMEM,) * X,
        compiler_params=params(16),
        name="deal",
    )(place, data.reshape(X, QUARTER, SLICE))


def partial_scores(place, data_ref, core, noise_ref, q_ref, sq_ref):
    pieces = [at(place, 2, rel, Y) for rel in AROUND]
    lhs = jnp.concatenate([data_ref[p, core, from_x(place[1], n)] for p in pieces for n in range(X)], axis=1)
    for h in range(2):
        rhs = noise_ref[pl.ds(h * X * CUT, X * CUT), :]
        gram = lax.dot_general(lhs, rhs, (((1,), (1,)), ((), ())), preferred_element_type=F32) * (2.0 * UNIT)
        for j, rel in enumerate(AROUND):
            lanes = pl.ds(pl.multiple_of((h * X + at(place, 1, rel, X)) * 128, 128), 128)
            q_ref[:QUARTER, lanes] = gram[:, j * 128 : (j + 1) * 128]
    sq_ref[...] = squares(data_ref, [(p, core, n) for p in range(Y) for n in range(X)])


def theirs_kernel(place, data_ref, noise_ref, sqn_ref, out_ref, sq_ref):
    partial_scores(place, data_ref, 1 - place[3], noise_ref, out_ref, sq_ref)
    out_ref[:QUARTER, TALL:] = sq_ref[...]
    out_ref[QUARTER:, :] = jnp.zeros((8, TALL + 128), F32)
    out_ref[QUARTER : QUARTER + 2, :128] = sqn_ref[...]


def theirs(place, data, noise, sqn):
    return pl.pallas_call(
        theirs_kernel,
        out_shape=jax.ShapeDtypeStruct((QUARTER + 8, TALL + 128), F32),
        in_specs=[SMEM] + [VMEM] * 3,
        out_specs=VMEM,
        scratch_shapes=[pltpu.VMEM((QUARTER, 128), F32)],
        compiler_params=params(24),
        name="theirs",
    )(place, data, noise, sqn)


def ours_kernel(place, data_ref, noise_ref, q_ref, sq_ref):
    partial_scores(place, data_ref, place[3], noise_ref, q_ref, sq_ref)


def ours(place, data, noise):
    return pl.pallas_call(
        ours_kernel,
        out_shape=(jax.ShapeDtypeStruct((QUARTER, TALL), F32), jax.ShapeDtypeStruct((QUARTER, 128), F32)),
        in_specs=[SMEM] + [VMEM] * 2,
        out_specs=(VMEM,) * 2,
        compiler_params=params(24),
        cost_estimate=pl.CostEstimate(flops=QUARTER * TALL * WIDTH, bytes_accessed=6 * 2**20, transcendentals=0),
        name="ours",
    )(place, data, noise)


def score_kernel(mine_ref, sq_mine_ref, sqn_mine_ref, got_ref, q_ref, out_ref, sq_ref, sqn_ref, lse_ref):
    sq = jnp.sum(sq_mine_ref[...] + got_ref[:QUARTER, TALL:], axis=1, keepdims=True)
    sq_ref[...] = jnp.broadcast_to(sq, (QUARTER, 128))
    sqn_ref[...] = sqn_mine_ref[...] + got_ref[QUARTER : QUARTER + 2, :128]
    for r in range(CHUNKS):
        q = mine_ref[:, chunk(r)] + got_ref[:QUARTER, chunk(r)]
        q_ref[:, chunk(r)] = q
        lse_ref[pl.ds(r, 1), :] = lse(q - UNIT * sq_ref[...], 0)
    out_ref[...] = jnp.broadcast_to(lse_ref[...][None], (GROUP, CHUNKS, 128))


def score(mine, sq_mine, sqn_mine, got):
    return pl.pallas_call(
        score_kernel,
        out_shape=(
            jax.ShapeDtypeStruct((QUARTER, TALL), F32),
            jax.ShapeDtypeStruct((GROUP, CHUNKS, 128), F32),
            jax.ShapeDtypeStruct((QUARTER, 128), F32),
            jax.ShapeDtypeStruct((2, 128), F32),
        ),
        in_specs=[VMEM] * 4,
        out_specs=(VMEM,) * 4,
        scratch_shapes=[pltpu.VMEM((CHUNKS, 128), F32)],
        compiler_params=params(16),
        name="score",
    )(mine, sq_mine, sqn_mine, got)


def to_column(g):
    return jnp.concatenate([jnp.transpose(jnp.broadcast_to(g[r : r + 1], (128, 128))) for r in range(2)], axis=0)


def noise_kernel(q_ref, part_ref, out_ref, lse_ref, g_ref):
    g_ref[...] = to_column(-LOG2N - merged(part_ref))
    for r in range(CHUNKS):
        lse_ref[pl.ds(r, 1), :] = lse(q_ref[:, chunk(r)] + g_ref[...], 0)
    out_ref[...] = jnp.broadcast_to(lse_ref[...][None], (GROUP, CHUNKS, 128))


def noise_lse(q, parts):
    return pl.pallas_call(
        noise_kernel,
        out_shape=jax.ShapeDtypeStruct((GROUP, CHUNKS, 128), F32),
        in_specs=[VMEM] * 2,
        out_specs=VMEM,
        scratch_shapes=[pltpu.VMEM((CHUNKS, 128), F32), pltpu.VMEM((QUARTER, 128), F32)],
        compiler_params=params(16),
        name="noise_lse",
    )(q, parts)


def data_kernel(q_ref, part_ref, out_ref, f_ref, lane_ref):
    f_ref[...] = -LOG2N - merged(part_ref)
    row = data_row(q_ref, f_ref, lane_ref)
    out_ref[...] = jnp.broadcast_to(two_rows(row)[None], (Z, 8, 128))


def data_row(q_ref, f_ref, lane_ref):
    step = 32
    for start in range(0, QUARTER, step):
        rows = pl.ds(start, step)
        t = [q_ref[rows, chunk(r)] + f_ref[pl.ds(r, 1), :] for r in range(CHUNKS)]
        top = functools.reduce(jnp.maximum, t)
        lane_ref[rows, :] = top + jnp.log2(sum(jnp.exp2(part - top) for part in t))
    return lse(jnp.transpose(lane_ref[...]), 0)


def two_rows(*rows):
    halves = [half for row in rows for half in (row[:, :128], row[:, 128:])]
    return jnp.concatenate(halves + [jnp.zeros((8 - len(halves), 128), F32)], axis=0)


def data_lse(q, parts):
    return pl.pallas_call(
        data_kernel,
        out_shape=(jax.ShapeDtypeStruct((Z, 8, 128), F32), jax.ShapeDtypeStruct((CHUNKS, 128), F32)),
        in_specs=[VMEM] * 2,
        out_specs=(VMEM, VMEM),
        scratch_shapes=[pltpu.VMEM((QUARTER, 128), F32)],
        compiler_params=params(16),
        name="data_lse",
    )(q, parts)


def last_kernel(place, q_ref, part_ref, sq_ref, out_ref, f_ref, *refs):
    w_refs, lane_ref = refs[:X], refs[X]
    f_ref[...] = -LOG2N - merged(part_ref)
    tile = two_rows(data_row(q_ref, f_ref, lane_ref), jnp.transpose(sq_ref[...])[0:1, :])
    out_ref[...] = jnp.broadcast_to(tile[None], (Z * X, 8, 128))
    column = to_column(tile)
    for by in range(X):
        block = lax.rem(place[1] + by, X)
        for h in range(2):
            lanes = pl.ds(pl.multiple_of((h * X + block) * 128, 128), 128)
            w = jnp.exp2((q_ref[:, lanes] + f_ref[pl.ds(h * X + block, 1), :]) - column)
            w_refs[by][:, pl.ds(h * 128, 128)] = w.astype(BF16)


def last_lse(place, q, parts, sq):
    return pl.pallas_call(
        last_kernel,
        out_shape=(jax.ShapeDtypeStruct((Z * X, 8, 128), F32), jax.ShapeDtypeStruct((CHUNKS, 128), F32))
        + (jax.ShapeDtypeStruct((QUARTER, ROWS), BF16),) * X,
        in_specs=[SMEM] + [VMEM] * 3,
        out_specs=(VMEM,) * (2 + X),
        scratch_shapes=[pltpu.VMEM((QUARTER, 128), F32)],
        compiler_params=params(16),
        name="last_lse",
    )(place, q, parts, sq)


def scale_kernel(place, part_ref, *refs):
    w_refs, (w_ref, pot_ref) = refs[:X], refs[X:]
    z, x = place[0], place[1]
    for n in range(X):
        parts = jnp.stack([part_ref[k * X + n, 0:4, :] for k in range(Z)])
        top = jnp.max(parts, axis=0)
        total = top + jnp.log2(jnp.sum(jnp.exp2(parts - top[None]), axis=0))
        pot_ref[pl.ds(2 * n, 2), :] = (-LOG2N - total[0:2]) * (EPS / LOG2E) + parts[0, 2:4] * (1.0 / WIDTH)
    for w_ref_by, by in zip(w_refs, (0, 2, 1, 3)):
        n = lax.rem(x - by + X, X)
        parts = jnp.stack([part_ref[k * X + n] for k in range(Z)])
        top = jnp.max(parts, axis=0)
        total = top + jnp.log2(jnp.sum(jnp.exp2(parts - top[None]), axis=0))
        factor = jnp.exp2(part_ref[z * X + n] - total)
        factor = jnp.concatenate([factor[0:1], factor[1:2]], axis=1)
        lanes = pl.ds(pl.multiple_of(n * QUARTER, QUARTER), QUARTER)
        for h in range(2):
            w = jnp.transpose(w_ref_by[:, pl.ds(h * 128, 128)].astype(F32)) * factor
            w_ref[pl.ds(h * 128, 128), lanes] = w.astype(BF16)


def scale(place, parts, blocks):
    return pl.pallas_call(
        scale_kernel,
        out_shape=(jax.ShapeDtypeStruct((ROWS, COUNT), BF16), jax.ShapeDtypeStruct((2 * X, 128), F32)),
        in_specs=[SMEM] + [VMEM] * (1 + X),
        out_specs=(VMEM,) * 2,
        compiler_params=params(16),
        name="scale",
    )(place, parts, *blocks)


def transport_kernel(pieces, place, w_ref, got_ref, data_ref, *out_refs):
    lhs = jnp.concatenate([w_ref[...], got_ref[...]], axis=1)
    for s, out_ref in zip(pieces, out_refs):
        y = at(place, 2, s, Y)
        rhs = []
        for core in (place[3], 1 - place[3]):
            for n in range(X):
                rhs.append(jnp.concatenate([data_ref[n, y, core, from_x(n, k)] for k in range(X)], axis=1))
        total = jnp.dot(lhs, jnp.concatenate(rhs, axis=0), preferred_element_type=F32)
        out_ref[...] = total.astype(out_ref.dtype)


def transport(place, w, got, data, pieces, hand_on):
    kinds = [jax.ShapeDtypeStruct((ROWS, SHARE), BF16 if s else F32) for s in pieces]
    if hand_on:
        kinds.append(jax.ShapeDtypeStruct(data.shape, data.dtype))
    return pl.pallas_call(
        functools.partial(transport_kernel, pieces),
        out_shape=kinds,
        in_specs=[SMEM] + [VMEM] * 3,
        out_specs=[VMEM] * len(kinds),
        input_output_aliases={3: len(pieces)} if hand_on else {},
        compiler_params=params(24),
        cost_estimate=pl.CostEstimate(
            flops=2 * ROWS * COUNT * C * SHARE * len(pieces), bytes_accessed=2 * 2**20 * len(pieces), transcendentals=0
        ),
        name="transport",
    )(place, w, got, data)


def body(noise, data):
    z, x, y, c = (lax.axis_index(a) for a in ("z", "x", "y", "core"))
    place = jnp.stack([z, x, y, c]).astype(jnp.int32)
    dealt = deal(place, data)
    swapped = jnp.stack([dealt[0]] + [shift(dealt[by], "x", by) for by in range(1, X)])
    noise_after, swapped = lax.optimization_barrier((noise, swapped))
    samples = lax.all_gather(swapped, ("z", "core")).reshape(Y, C, C, X, QUARTER, SLICE)
    samples, noise_all, sqn_mine = lax.optimization_barrier((samples, *collect(gather_noise(noise_after))))
    samples = pick(place, samples)
    data_all = lax.all_gather(samples, "x")
    got = shift(theirs(place, samples, noise_all, sqn_mine), "core", 1)
    mine, sq_mine = ours(place, samples, noise_all)
    q, rows, sq, sq_noise = score(mine, sq_mine, sqn_mine, got)
    for step in range(ITERS):
        if step:
            rows = noise_lse(q, columns)
        parts = lax.all_to_all(rows, ("x", "y", "core"), 0, 0)
        if step < ITERS - 1:
            columns, f = data_lse(q, parts)
            columns = lax.all_to_all(columns, "z", 0, 0)
    columns, f, *blocks = last_lse(place, q, parts, sq)
    blocks = [blocks[0]] + [shift(blocks[by], "x", by) for by in (2, 1, 3)]
    columns = lax.all_to_all(columns, ("z", "x"), 0, 0)
    w, pot_g = scale(place, columns, blocks)
    data_all, pot_g = lax.optimization_barrier((data_all, pot_g))
    got = shift(w, "core", 1)
    opposite, data_all = transport(place, w, got, data_all, (2,), True)
    up, down, data_all = transport(place, w, got, data_all, (1, 3), True)
    (target,) = transport(place, w, got, data_all, (0,), False)
    for by, part in zip((2, 1, 3), (opposite, up, down)):
        target = target + shift(part, "y", by).astype(F32)
    velocity = (target - noise.astype(F32)).astype(BF16)
    own = lax.dynamic_index_in_dim(f.reshape(2, X, 128), x, 1, False)
    pot_f = (own * (EPS / LOG2E) + sq_noise / WIDTH).reshape(ROWS)
    return pot_f, pot_g.reshape(COUNT), velocity


def solution(mesh):
    fine = Mesh(mesh.devices.reshape(Z, X, Y, C), ("z", "x", "y", "core"))
    row, col = ("z", "x"), ("y", "core")
    return jax.shard_map(
        body,
        mesh=fine,
        in_specs=(P(row, col), P(col, row)),
        out_specs=(P(row), P(col), P(row, col)),
        check_vma=False,
    )
```

```python
import functools
import math

import jax
import jax.numpy as jnp
from jax import lax
from jax.experimental import pallas as pl
from jax.experimental.pallas import tpu as pltpu
from jax.sharding import Mesh, PartitionSpec as P

ITERS = 3
EPS = 0.01
LOG2E = math.log2(math.e)
Z, X, Y, C = 8, 4, 4, 2
ROWS, SHARE = 256, 512
COUNT, SLICE = 1024, 128
WIDTH = 4096
QUARTER = COUNT // X
TALL = ROWS * X
CHUNKS = TALL // 128
GROUP = X * Y * C
CUT = ROWS // 2
AROUND = (0, -1, 1, 2)
TOTAL = 8192
UNIT = LOG2E / (WIDTH * EPS)
LOG2N = math.log2(TOTAL)
F32, BF16 = jnp.float32, jnp.bfloat16
VMEM = pl.BlockSpec(memory_space=pltpu.VMEM)
SMEM = pl.BlockSpec(memory_space=pltpu.SMEM)


def shift(x, axis, by):
    n = {"z": Z, "x": X, "y": Y, "core": C}[axis]
    return lax.ppermute(x, axis, [(j, (j + by) % n) for j in range(n)])


def params(mib):
    return pltpu.CompilerParams(vmem_limit_bytes=mib * 2**20)


def both_ways(forward, backward, axis):
    return shift(forward, axis, 1), shift(backward, axis, -1)


def halves(forward, backward, axis):
    cut = forward.shape[0] // 2
    return both_ways(forward[:cut], backward[cut:], axis)


def around(block, axis):
    return [block, shift(block, axis, 1), shift(block, axis, -1), shift(block, axis, 2)]


def gather_noise(noise):
    hold = lax.optimization_barrier
    across, along = hold((around(noise[:CUT], "x"), around(noise[CUT:], "y")))
    across, along = jnp.stack(across), jnp.stack(along)
    y1, x1 = hold((both_ways(across, across, "y"), both_ways(along, along, "x")))
    return [across, *y1, *halves(*y1, "y"), along, *x1, *halves(*x1, "x")]


def squares(ref, pieces):
    total = None
    for view in pieces:
        part = ref[view].astype(F32)
        total = part * part if total is None else total + part * part
    return total


def lse(t, axis):
    top = jnp.max(t, axis=axis, keepdims=True)
    return top + jnp.log2(jnp.sum(jnp.exp2(t - top), axis=axis, keepdims=True))


def merged(ref):
    parts = ref[...]
    top = jnp.max(parts, axis=0)
    return top + jnp.log2(jnp.sum(jnp.exp2(parts - top[None]), axis=0))


def chunk(r):
    return pl.ds(r * 128, 128)


def at(place, which, rel, size):
    return lax.rem(place[which] + rel + size, size)


def from_x(x, n):
    return lax.rem(x - n + X, X) if not isinstance(x, int) else (x - n) % X


def blocks_of(parts):
    first, second = parts[:5], parts[5:]

    def of(five, far, near):
        if far < 3:
            return five[far].at[near]
        return five[3 + near // 2].at[near % 2]

    return (
        [[of(first, k, j) for k in range(Y)] for j in range(X)],
        [[of(second, j, k) for k in range(Y)] for j in range(X)],
    )


def collect_kernel(*refs):
    parts, (noise_ref, sqn_ref) = refs[:10], refs[10:]
    rows = []
    for h, blocks in enumerate(blocks_of(parts)):
        for j, row in enumerate(blocks):
            for k, ref in enumerate(row):
                noise_ref[pl.ds((h * X + j) * CUT, CUT), pl.ds(k * SHARE, SHARE)] = ref[...]
        t = [squares(ref, [(slice(None), pl.ds(lane, 128)) for lane in range(0, SHARE, 128)]) for ref in blocks[0]]
        total = (t[0] + t[3]) + (t[1] + t[2])
        rows.append(jnp.sum(jnp.transpose(total), axis=0, keepdims=True))
    sqn_ref[...] = jnp.concatenate(rows, axis=0)


def collect(parts):
    return pl.pallas_call(
        collect_kernel,
        out_shape=(jax.ShapeDtypeStruct((TALL, WIDTH // C), BF16), jax.ShapeDtypeStruct((2, 128), F32)),
        in_specs=[VMEM] * 10,
        out_specs=(VMEM,) * 2,
        compiler_params=params(16),
        name="collect",
    )(*parts)


def pick_kernel(place, all_ref, out_ref, buffer_ref, sems):
    ins = [pltpu.make_async_copy(all_ref.at[y, place[3]], buffer_ref.at[y], sems.at[0, y]) for y in range(Y)]
    outs = [pltpu.make_async_copy(buffer_ref.at[y], out_ref.at[y], sems.at[1, y]) for y in range(Y)]
    for copy in ins:
        copy.start()
    for y in range(Y):
        ins[y].wait()
        outs[y].start()
    for copy in outs:
        copy.wait()


def pick(place, samples):
    half = (Y, C, X, QUARTER, SLICE)
    return pl.pallas_call(
        pick_kernel,
        out_shape=jax.ShapeDtypeStruct(half, BF16),
        in_specs=[SMEM, pl.BlockSpec(memory_space=pl.ANY)],
        out_specs=pl.BlockSpec(memory_space=pl.ANY),
        scratch_shapes=[pltpu.VMEM(half, BF16), pltpu.SemaphoreType.DMA((2, Y))],
        compiler_params=params(53),
        name="pick",
    )(place, samples)


def deal_kernel(place, data_ref, *out_refs):
    for by, ref in enumerate(out_refs):
        ref[...] = data_ref[at(place, 1, by, X)]


def deal(place, data):
    return pl.pallas_call(
        deal_kernel,
        out_shape=(jax.ShapeDtypeStruct((QUARTER, SLICE), BF16),) * X,
        in_specs=[SMEM, VMEM],
        out_specs=(VMEM,) * X,
        compiler_params=params(16),
        name="deal",
    )(place, data.reshape(X, QUARTER, SLICE))


def partial_scores(place, data_ref, core, noise_ref, q_ref, sq_ref):
    pieces = [at(place, 2, rel, Y) for rel in AROUND]
    lhs = jnp.concatenate([data_ref[p, core, from_x(place[1], n)] for p in pieces for n in range(X)], axis=1)
    for h in range(2):
        rhs = noise_ref[pl.ds(h * X * CUT, X * CUT), :]
        gram = lax.dot_general(lhs, rhs, (((1,), (1,)), ((), ())), preferred_element_type=F32) * (2.0 * UNIT)
        for j, rel in enumerate(AROUND):
            lanes = pl.ds(pl.multiple_of((h * X + at(place, 1, rel, X)) * 128, 128), 128)
            q_ref[:QUARTER, lanes] = gram[:, j * 128 : (j + 1) * 128]
    sq_ref[...] = squares(data_ref, [(p, core, n) for p in range(Y) for n in range(X)])


def theirs_kernel(place, data_ref, noise_ref, sqn_ref, out_ref, sq_ref):
    partial_scores(place, data_ref, 1 - place[3], noise_ref, out_ref, sq_ref)
    out_ref[:QUARTER, TALL:] = sq_ref[...]
    out_ref[QUARTER:, :] = jnp.zeros((8, TALL + 128), F32)
    out_ref[QUARTER : QUARTER + 2, :128] = sqn_ref[...]


def theirs(place, data, noise, sqn):
    return pl.pallas_call(
        theirs_kernel,
        out_shape=jax.ShapeDtypeStruct((QUARTER + 8, TALL + 128), F32),
        in_specs=[SMEM] + [VMEM] * 3,
        out_specs=VMEM,
        scratch_shapes=[pltpu.VMEM((QUARTER, 128), F32)],
        compiler_params=params(24),
        name="theirs",
    )(place, data, noise, sqn)


def ours_kernel(place, data_ref, noise_ref, q_ref, sq_ref):
    partial_scores(place, data_ref, place[3], noise_ref, q_ref, sq_ref)


def ours(place, data, noise):
    return pl.pallas_call(
        ours_kernel,
        out_shape=(jax.ShapeDtypeStruct((QUARTER, TALL), F32), jax.ShapeDtypeStruct((QUARTER, 128), F32)),
        in_specs=[SMEM] + [VMEM] * 2,
        out_specs=(VMEM,) * 2,
        compiler_params=params(24),
        cost_estimate=pl.CostEstimate(flops=QUARTER * TALL * WIDTH, bytes_accessed=6 * 2**20, transcendentals=0),
        name="ours",
    )(place, data, noise)


def score_kernel(mine_ref, sq_mine_ref, sqn_mine_ref, got_ref, q_ref, out_ref, sq_ref, sqn_ref, lse_ref):
    sq = jnp.sum(sq_mine_ref[...] + got_ref[:QUARTER, TALL:], axis=1, keepdims=True)
    sq_ref[...] = jnp.broadcast_to(sq, (QUARTER, 128))
    sqn_ref[...] = sqn_mine_ref[...] + got_ref[QUARTER : QUARTER + 2, :128]
    for r in range(CHUNKS):
        q = mine_ref[:, chunk(r)] + got_ref[:QUARTER, chunk(r)]
        q_ref[:, chunk(r)] = q
        lse_ref[pl.ds(r, 1), :] = lse(q - UNIT * sq_ref[...], 0)
    out_ref[...] = jnp.broadcast_to(lse_ref[...][None], (GROUP, CHUNKS, 128))


def score(mine, sq_mine, sqn_mine, got):
    return pl.pallas_call(
        score_kernel,
        out_shape=(
            jax.ShapeDtypeStruct((QUARTER, TALL), F32),
            jax.ShapeDtypeStruct((GROUP, CHUNKS, 128), F32),
            jax.ShapeDtypeStruct((QUARTER, 128), F32),
            jax.ShapeDtypeStruct((2, 128), F32),
        ),
        in_specs=[VMEM] * 4,
        out_specs=(VMEM,) * 4,
        scratch_shapes=[pltpu.VMEM((CHUNKS, 128), F32)],
        compiler_params=params(16),
        name="score",
    )(mine, sq_mine, sqn_mine, got)


def to_column(g):
    return jnp.concatenate([jnp.transpose(jnp.broadcast_to(g[r : r + 1], (128, 128))) for r in range(2)], axis=0)


def noise_kernel(q_ref, part_ref, out_ref, lse_ref, g_ref):
    g_ref[...] = to_column(-LOG2N - merged(part_ref))
    for r in range(CHUNKS):
        lse_ref[pl.ds(r, 1), :] = lse(q_ref[:, chunk(r)] + g_ref[...], 0)
    out_ref[...] = jnp.broadcast_to(lse_ref[...][None], (GROUP, CHUNKS, 128))


def noise_lse(q, parts):
    return pl.pallas_call(
        noise_kernel,
        out_shape=jax.ShapeDtypeStruct((GROUP, CHUNKS, 128), F32),
        in_specs=[VMEM] * 2,
        out_specs=VMEM,
        scratch_shapes=[pltpu.VMEM((CHUNKS, 128), F32), pltpu.VMEM((QUARTER, 128), F32)],
        compiler_params=params(16),
        name="noise_lse",
    )(q, parts)


def data_kernel(q_ref, part_ref, out_ref, f_ref, lane_ref):
    f_ref[...] = -LOG2N - merged(part_ref)
    row = data_row(q_ref, f_ref, lane_ref)
    out_ref[...] = jnp.broadcast_to(two_rows(row)[None], (Z, 8, 128))


def data_row(q_ref, f_ref, lane_ref):
    step = 32
    for start in range(0, QUARTER, step):
        rows = pl.ds(start, step)
        t = [q_ref[rows, chunk(r)] + f_ref[pl.ds(r, 1), :] for r in range(CHUNKS)]
        top = functools.reduce(jnp.maximum, t)
        lane_ref[rows, :] = top + jnp.log2(sum(jnp.exp2(part - top) for part in t))
    return lse(jnp.transpose(lane_ref[...]), 0)


def two_rows(*rows):
    halves = [half for row in rows for half in (row[:, :128], row[:, 128:])]
    return jnp.concatenate(halves + [jnp.zeros((8 - len(halves), 128), F32)], axis=0)


def data_lse(q, parts):
    return pl.pallas_call(
        data_kernel,
        out_shape=(jax.ShapeDtypeStruct((Z, 8, 128), F32), jax.ShapeDtypeStruct((CHUNKS, 128), F32)),
        in_specs=[VMEM] * 2,
        out_specs=(VMEM, VMEM),
        scratch_shapes=[pltpu.VMEM((QUARTER, 128), F32)],
        compiler_params=params(16),
        name="data_lse",
    )(q, parts)


def last_kernel(place, q_ref, part_ref, sq_ref, out_ref, f_ref, *refs):
    w_refs, lane_ref = refs[:X], refs[X]
    f_ref[...] = -LOG2N - merged(part_ref)
    tile = two_rows(data_row(q_ref, f_ref, lane_ref), jnp.transpose(sq_ref[...])[0:1, :])
    out_ref[...] = jnp.broadcast_to(tile[None], (Z * X, 8, 128))
    column = to_column(tile)
    for by in range(X):
        block = lax.rem(place[1] + by, X)
        for h in range(2):
            lanes = pl.ds(pl.multiple_of((h * X + block) * 128, 128), 128)
            w = jnp.exp2((q_ref[:, lanes] + f_ref[pl.ds(h * X + block, 1), :]) - column)
            w_refs[by][:, pl.ds(h * 128, 128)] = w.astype(BF16)


def last_lse(place, q, parts, sq):
    return pl.pallas_call(
        last_kernel,
        out_shape=(jax.ShapeDtypeStruct((Z * X, 8, 128), F32), jax.ShapeDtypeStruct((CHUNKS, 128), F32))
        + (jax.ShapeDtypeStruct((QUARTER, ROWS), BF16),) * X,
        in_specs=[SMEM] + [VMEM] * 3,
        out_specs=(VMEM,) * (2 + X),
        scratch_shapes=[pltpu.VMEM((QUARTER, 128), F32)],
        compiler_params=params(16),
        name="last_lse",
    )(place, q, parts, sq)


def scale_kernel(place, part_ref, *refs):
    w_refs, (w_ref, pot_ref) = refs[:X], refs[X:]
    z, x = place[0], place[1]
    for n in range(X):
        parts = jnp.stack([part_ref[k * X + n, 0:4, :] for k in range(Z)])
        top = jnp.max(parts, axis=0)
        total = top + jnp.log2(jnp.sum(jnp.exp2(parts - top[None]), axis=0))
        pot_ref[pl.ds(2 * n, 2), :] = (-LOG2N - total[0:2]) * (EPS / LOG2E) + parts[0, 2:4] * (1.0 / WIDTH)
    for by in range(X):
        n = lax.rem(x - by + X, X)
        parts = jnp.stack([part_ref[k * X + n] for k in range(Z)])
        top = jnp.max(parts, axis=0)
        total = top + jnp.log2(jnp.sum(jnp.exp2(parts - top[None]), axis=0))
        factor = jnp.exp2(part_ref[z * X + n] - total)
        factor = jnp.concatenate([factor[0:1], factor[1:2]], axis=1)
        lanes = pl.ds(pl.multiple_of(n * QUARTER, QUARTER), QUARTER)
        for h in range(2):
            w = jnp.transpose(w_refs[by][:, pl.ds(h * 128, 128)].astype(F32)) * factor
            w_ref[pl.ds(h * 128, 128), lanes] = w.astype(BF16)


def scale(place, parts, blocks):
    return pl.pallas_call(
        scale_kernel,
        out_shape=(jax.ShapeDtypeStruct((ROWS, COUNT), BF16), jax.ShapeDtypeStruct((2 * X, 128), F32)),
        in_specs=[SMEM] + [VMEM] * (1 + X),
        out_specs=(VMEM,) * 2,
        compiler_params=params(16),
        name="scale",
    )(place, parts, *blocks)


def transport_kernel(pieces, place, w_ref, got_ref, data_ref, *out_refs):
    lhs = jnp.concatenate([w_ref[...], got_ref[...]], axis=1)
    for s, out_ref in zip(pieces, out_refs):
        y = at(place, 2, s, Y)
        rhs = []
        for core in (place[3], 1 - place[3]):
            for n in range(X):
                rhs.append(jnp.concatenate([data_ref[n, y, core, from_x(n, k)] for k in range(X)], axis=1))
        total = jnp.dot(lhs, jnp.concatenate(rhs, axis=0), preferred_element_type=F32)
        out_ref[...] = total.astype(out_ref.dtype)


def transport(place, w, got, data, pieces, hand_on):
    kinds = [jax.ShapeDtypeStruct((ROWS, SHARE), BF16 if s else F32) for s in pieces]
    if hand_on:
        kinds.append(jax.ShapeDtypeStruct(data.shape, data.dtype))
    return pl.pallas_call(
        functools.partial(transport_kernel, pieces),
        out_shape=kinds,
        in_specs=[SMEM] + [VMEM] * 3,
        out_specs=[VMEM] * len(kinds),
        input_output_aliases={3: len(pieces)} if hand_on else {},
        compiler_params=params(24),
        cost_estimate=pl.CostEstimate(
            flops=2 * ROWS * COUNT * C * SHARE * len(pieces), bytes_accessed=2 * 2**20 * len(pieces), transcendentals=0
        ),
        name="transport",
    )(place, w, got, data)


def body(noise, data):
    z, x, y, c = (lax.axis_index(a) for a in ("z", "x", "y", "core"))
    place = jnp.stack([z, x, y, c]).astype(jnp.int32)
    dealt = deal(place, data)
    swapped = jnp.stack([dealt[0]] + [shift(dealt[by], "x", by) for by in range(1, X)])
    noise_after, swapped = lax.optimization_barrier((noise, swapped))
    samples = lax.all_gather(swapped, ("z", "core")).reshape(Y, C, C, X, QUARTER, SLICE)
    samples, noise_all, sqn_mine = lax.optimization_barrier((samples, *collect(gather_noise(noise_after))))
    samples = pick(place, samples)
    data_all = lax.all_gather(samples, "x")
    got = shift(theirs(place, samples, noise_all, sqn_mine), "core", 1)
    mine, sq_mine = ours(place, samples, noise_all)
    q, rows, sq, sq_noise = score(mine, sq_mine, sqn_mine, got)
    for step in range(ITERS):
        if step:
            rows = noise_lse(q, columns)
        parts = lax.all_to_all(rows, ("x", "y", "core"), 0, 0)
        if step < ITERS - 1:
            columns, f = data_lse(q, parts)
            columns = lax.all_to_all(columns, "z", 0, 0)
    columns, f, *blocks = last_lse(place, q, parts, sq)
    blocks = [blocks[0]] + [shift(blocks[by], "x", by) for by in range(1, X)]
    columns = lax.all_to_all(columns, ("z", "x"), 0, 0)
    w, pot_g = scale(place, columns, blocks)
    data_all, pot_g = lax.optimization_barrier((data_all, pot_g))
    got = shift(w, "core", 1)
    up, data_all = transport(place, w, got, data_all, (1,), True)
    opposite, down, data_all = transport(place, w, got, data_all, (2, 3), True)
    (target,) = transport(place, w, got, data_all, (0,), False)
    for by, part in zip((1, 2, 3), (up, opposite, down)):
        target = target + shift(part, "y", by).astype(F32)
    velocity = (target - noise.astype(F32)).astype(BF16)
    own = lax.dynamic_index_in_dim(f.reshape(2, X, 128), x, 1, False)
    pot_f = (own * (EPS / LOG2E) + sq_noise / WIDTH).reshape(ROWS)
    return pot_f, pot_g.reshape(COUNT), velocity


def solution(mesh):
    fine = Mesh(mesh.devices.reshape(Z, X, Y, C), ("z", "x", "y", "core"))
    row, col = ("z", "x"), ("y", "core")
    return jax.shard_map(
        body,
        mesh=fine,
        in_specs=(P(row, col), P(col, row)),
        out_specs=(P(row), P(col), P(row, col)),
        check_vma=False,
    )
```

```python
import functools
import math

import jax
import jax.numpy as jnp
from jax import lax
from jax.experimental import pallas as pl
from jax.experimental.pallas import tpu as pltpu
from jax.sharding import Mesh, PartitionSpec as P

ITERS = 3
EPS = 0.01
LOG2E = math.log2(math.e)
Z, X, Y, C = 8, 4, 4, 2
ROWS, SHARE = 256, 512
COUNT, SLICE = 1024, 128
WIDTH = 4096
QUARTER = COUNT // X
TALL = ROWS * X
CHUNKS = TALL // 128
GROUP = X * Y * C
CUT = ROWS // 2
AROUND = (0, -1, 1, 2)
TOTAL = 8192
UNIT = LOG2E / (WIDTH * EPS)
LOG2N = math.log2(TOTAL)
F32, BF16 = jnp.float32, jnp.bfloat16
VMEM = pl.BlockSpec(memory_space=pltpu.VMEM)
SMEM = pl.BlockSpec(memory_space=pltpu.SMEM)


def shift(x, axis, by):
    n = {"z": Z, "x": X, "y": Y, "core": C}[axis]
    return lax.ppermute(x, axis, [(j, (j + by) % n) for j in range(n)])


def params(mib):
    return pltpu.CompilerParams(vmem_limit_bytes=mib * 2**20)


def both_ways(forward, backward, axis):
    return shift(forward, axis, 1), shift(backward, axis, -1)


def halves(forward, backward, axis):
    cut = forward.shape[0] // 2
    return both_ways(forward[:cut], backward[cut:], axis)


def around(block, axis):
    return [block, shift(block, axis, 1), shift(block, axis, -1), shift(block, axis, 2)]


def gather_noise(noise):
    hold = lax.optimization_barrier
    across, along = hold((around(noise[:CUT], "x"), around(noise[CUT:], "y")))
    across, along = jnp.stack(across), jnp.stack(along)
    y1, x1 = hold((both_ways(across, across, "y"), both_ways(along, along, "x")))
    return [across, *y1, *halves(*y1, "y"), along, *x1, *halves(*x1, "x")]


def squares(ref, pieces):
    total = None
    for view in pieces:
        part = ref[view].astype(F32)
        total = part * part if total is None else total + part * part
    return total


def lse(t, axis):
    top = jnp.max(t, axis=axis, keepdims=True)
    return top + jnp.log2(jnp.sum(jnp.exp2(t - top), axis=axis, keepdims=True))


def merged(ref):
    parts = ref[...]
    top = jnp.max(parts, axis=0)
    return top + jnp.log2(jnp.sum(jnp.exp2(parts - top[None]), axis=0))


def chunk(r):
    return pl.ds(r * 128, 128)


def at(place, which, rel, size):
    return lax.rem(place[which] + rel + size, size)


def from_x(x, n):
    return lax.rem(x - n + X, X) if not isinstance(x, int) else (x - n) % X


def blocks_of(parts):
    first, second = parts[:5], parts[5:]

    def of(five, far, near):
        if far < 3:
            return five[far].at[near]
        return five[3 + near // 2].at[near % 2]

    return (
        [[of(first, k, j) for k in range(Y)] for j in range(X)],
        [[of(second, j, k) for k in range(Y)] for j in range(X)],
    )


def collect_kernel(*refs):
    parts, (noise_ref, sqn_ref) = refs[:10], refs[10:]
    rows = []
    for h, blocks in enumerate(blocks_of(parts)):
        for j, row in enumerate(blocks):
            for k, ref in enumerate(row):
                noise_ref[pl.ds((h * X + j) * CUT, CUT), pl.ds(k * SHARE, SHARE)] = ref[...]
        t = [squares(ref, [(slice(None), pl.ds(lane, 128)) for lane in range(0, SHARE, 128)]) for ref in blocks[0]]
        total = (t[0] + t[3]) + (t[1] + t[2])
        rows.append(jnp.sum(jnp.transpose(total), axis=0, keepdims=True))
    sqn_ref[...] = jnp.concatenate(rows, axis=0)


def collect(parts):
    return pl.pallas_call(
        collect_kernel,
        out_shape=(jax.ShapeDtypeStruct((TALL, WIDTH // C), BF16), jax.ShapeDtypeStruct((2, 128), F32)),
        in_specs=[VMEM] * 10,
        out_specs=(VMEM,) * 2,
        compiler_params=params(16),
        name="collect",
    )(*parts)


def pick_kernel(place, all_ref, out_ref, buffer_ref, sems):
    ins = [pltpu.make_async_copy(all_ref.at[y, place[3]], buffer_ref.at[y], sems.at[0, y]) for y in range(Y)]
    outs = [pltpu.make_async_copy(buffer_ref.at[y], out_ref.at[y], sems.at[1, y]) for y in range(Y)]
    for copy in ins:
        copy.start()
    for y in range(Y):
        ins[y].wait()
        outs[y].start()
    for copy in outs:
        copy.wait()


def pick(place, samples):
    half = (Y, C, X, QUARTER, SLICE)
    return pl.pallas_call(
        pick_kernel,
        out_shape=jax.ShapeDtypeStruct(half, BF16),
        in_specs=[SMEM, pl.BlockSpec(memory_space=pl.ANY)],
        out_specs=pl.BlockSpec(memory_space=pl.ANY),
        scratch_shapes=[pltpu.VMEM(half, BF16), pltpu.SemaphoreType.DMA((2, Y))],
        compiler_params=params(53),
        name="pick",
    )(place, samples)


def deal_kernel(place, data_ref, *out_refs):
    for by, ref in enumerate(out_refs):
        ref[...] = data_ref[at(place, 1, by, X)]


def deal(place, data):
    return pl.pallas_call(
        deal_kernel,
        out_shape=(jax.ShapeDtypeStruct((QUARTER, SLICE), BF16),) * X,
        in_specs=[SMEM, VMEM],
        out_specs=(VMEM,) * X,
        compiler_params=params(16),
        name="deal",
    )(place, data.reshape(X, QUARTER, SLICE))


def partial_scores(place, data_ref, core, noise_ref, q_ref, sq_ref):
    pieces = [at(place, 2, rel, Y) for rel in AROUND]
    lhs = jnp.concatenate([data_ref[p, core, from_x(place[1], n)] for p in pieces for n in range(X)], axis=1)
    for h in range(2):
        rhs = noise_ref[pl.ds(h * X * CUT, X * CUT), :]
        gram = lax.dot_general(lhs, rhs, (((1,), (1,)), ((), ())), preferred_element_type=F32) * (2.0 * UNIT)
        for j, rel in enumerate(AROUND):
            lanes = pl.ds(pl.multiple_of((h * X + at(place, 1, rel, X)) * 128, 128), 128)
            q_ref[:QUARTER, lanes] = gram[:, j * 128 : (j + 1) * 128]
    sq_ref[...] = squares(data_ref, [(p, core, n) for p in range(Y) for n in range(X)])


def theirs_kernel(place, data_ref, noise_ref, sqn_ref, out_ref, sq_ref):
    partial_scores(place, data_ref, 1 - place[3], noise_ref, out_ref, sq_ref)
    out_ref[:QUARTER, TALL:] = sq_ref[...]
    out_ref[QUARTER:, :] = jnp.zeros((8, TALL + 128), F32)
    out_ref[QUARTER : QUARTER + 2, :128] = sqn_ref[...]


def theirs(place, data, noise, sqn):
    return pl.pallas_call(
        theirs_kernel,
        out_shape=jax.ShapeDtypeStruct((QUARTER + 8, TALL + 128), F32),
        in_specs=[SMEM] + [VMEM] * 3,
        out_specs=VMEM,
        scratch_shapes=[pltpu.VMEM((QUARTER, 128), F32)],
        compiler_params=params(24),
        name="theirs",
    )(place, data, noise, sqn)


def ours_kernel(place, data_ref, noise_ref, q_ref, sq_ref):
    partial_scores(place, data_ref, place[3], noise_ref, q_ref, sq_ref)


def ours(place, data, noise):
    return pl.pallas_call(
        ours_kernel,
        out_shape=(jax.ShapeDtypeStruct((QUARTER, TALL), F32), jax.ShapeDtypeStruct((QUARTER, 128), F32)),
        in_specs=[SMEM] + [VMEM] * 2,
        out_specs=(VMEM,) * 2,
        compiler_params=params(24),
        cost_estimate=pl.CostEstimate(flops=QUARTER * TALL * WIDTH, bytes_accessed=6 * 2**20, transcendentals=0),
        name="ours",
    )(place, data, noise)


def score_kernel(mine_ref, sq_mine_ref, sqn_mine_ref, got_ref, q_ref, out_ref, sq_ref, sqn_ref, lse_ref):
    sq = jnp.sum(sq_mine_ref[...] + got_ref[:QUARTER, TALL:], axis=1, keepdims=True)
    sq_ref[...] = jnp.broadcast_to(sq, (QUARTER, 128))
    sqn_ref[...] = sqn_mine_ref[...] + got_ref[QUARTER : QUARTER + 2, :128]
    for r in range(CHUNKS):
        q = mine_ref[:, chunk(r)] + got_ref[:QUARTER, chunk(r)]
        q_ref[:, chunk(r)] = q
        lse_ref[pl.ds(r, 1), :] = lse(q - UNIT * sq_ref[...], 0)
    out_ref[...] = jnp.broadcast_to(lse_ref[...][None], (GROUP, CHUNKS, 128))


def score(mine, sq_mine, sqn_mine, got):
    return pl.pallas_call(
        score_kernel,
        out_shape=(
            jax.ShapeDtypeStruct((QUARTER, TALL), F32),
            jax.ShapeDtypeStruct((GROUP, CHUNKS, 128), F32),
            jax.ShapeDtypeStruct((QUARTER, 128), F32),
            jax.ShapeDtypeStruct((2, 128), F32),
        ),
        in_specs=[VMEM] * 4,
        out_specs=(VMEM,) * 4,
        scratch_shapes=[pltpu.VMEM((CHUNKS, 128), F32)],
        compiler_params=params(16),
        name="score",
    )(mine, sq_mine, sqn_mine, got)


def to_column(g):
    return jnp.concatenate([jnp.transpose(jnp.broadcast_to(g[r : r + 1], (128, 128))) for r in range(2)], axis=0)


def noise_kernel(q_ref, part_ref, out_ref, lse_ref, g_ref):
    g_ref[...] = to_column(-LOG2N - merged(part_ref))
    for r in range(CHUNKS):
        lse_ref[pl.ds(r, 1), :] = lse(q_ref[:, chunk(r)] + g_ref[...], 0)
    out_ref[...] = jnp.broadcast_to(lse_ref[...][None], (GROUP, CHUNKS, 128))


def noise_lse(q, parts):
    return pl.pallas_call(
        noise_kernel,
        out_shape=jax.ShapeDtypeStruct((GROUP, CHUNKS, 128), F32),
        in_specs=[VMEM] * 2,
        out_specs=VMEM,
        scratch_shapes=[pltpu.VMEM((CHUNKS, 128), F32), pltpu.VMEM((QUARTER, 128), F32)],
        compiler_params=params(16),
        name="noise_lse",
    )(q, parts)


def data_kernel(q_ref, part_ref, out_ref, f_ref, lane_ref):
    f_ref[...] = -LOG2N - merged(part_ref)
    row = data_row(q_ref, f_ref, lane_ref)
    out_ref[...] = jnp.broadcast_to(two_rows(row)[None, 0:2], (Z, 2, 128))


def data_row(q_ref, f_ref, lane_ref):
    step = 32
    for start in range(0, QUARTER, step):
        rows = pl.ds(start, step)
        t = [q_ref[rows, chunk(r)] + f_ref[pl.ds(r, 1), :] for r in range(CHUNKS)]
        top = functools.reduce(jnp.maximum, t)
        lane_ref[rows, :] = top + jnp.log2(sum(jnp.exp2(part - top) for part in t))
    return lse(jnp.transpose(lane_ref[...]), 0)


def two_rows(*rows):
    halves = [half for row in rows for half in (row[:, :128], row[:, 128:])]
    return jnp.concatenate(halves + [jnp.zeros((8 - len(halves), 128), F32)], axis=0)


def data_lse(q, parts):
    return pl.pallas_call(
        data_kernel,
        out_shape=(jax.ShapeDtypeStruct((Z, 2, 128), F32), jax.ShapeDtypeStruct((CHUNKS, 128), F32)),
        in_specs=[VMEM] * 2,
        out_specs=(VMEM, VMEM),
        scratch_shapes=[pltpu.VMEM((QUARTER, 128), F32)],
        compiler_params=params(16),
        name="data_lse",
    )(q, parts)


def last_kernel(place, q_ref, part_ref, sq_ref, out_ref, f_ref, *refs):
    w_refs, lane_ref = refs[:X], refs[X]
    f_ref[...] = -LOG2N - merged(part_ref)
    tile = two_rows(data_row(q_ref, f_ref, lane_ref), jnp.transpose(sq_ref[...])[0:1, :])
    out_ref[...] = jnp.broadcast_to(tile[None], (Z * X, 8, 128))
    column = to_column(tile)
    for by in range(X):
        block = lax.rem(place[1] + by, X)
        for h in range(2):
            lanes = pl.ds(pl.multiple_of((h * X + block) * 128, 128), 128)
            w = jnp.exp2((q_ref[:, lanes] + f_ref[pl.ds(h * X + block, 1), :]) - column)
            w_refs[by][:, pl.ds(h * 128, 128)] = w.astype(BF16)


def last_lse(place, q, parts, sq):
    return pl.pallas_call(
        last_kernel,
        out_shape=(jax.ShapeDtypeStruct((Z * X, 8, 128), F32), jax.ShapeDtypeStruct((CHUNKS, 128), F32))
        + (jax.ShapeDtypeStruct((QUARTER, ROWS), BF16),) * X,
        in_specs=[SMEM] + [VMEM] * 3,
        out_specs=(VMEM,) * (2 + X),
        scratch_shapes=[pltpu.VMEM((QUARTER, 128), F32)],
        compiler_params=params(16),
        name="last_lse",
    )(place, q, parts, sq)


def scale_kernel(place, part_ref, *refs):
    w_refs, (w_ref, pot_ref) = refs[:X], refs[X:]
    z, x = place[0], place[1]
    for n in range(X):
        parts = jnp.stack([part_ref[k * X + n, 0:4, :] for k in range(Z)])
        top = jnp.max(parts, axis=0)
        total = top + jnp.log2(jnp.sum(jnp.exp2(parts - top[None]), axis=0))
        pot_ref[pl.ds(2 * n, 2), :] = (-LOG2N - total[0:2]) * (EPS / LOG2E) + parts[0, 2:4] * (1.0 / WIDTH)
    for by in range(X):
        n = lax.rem(x - by + X, X)
        parts = jnp.stack([part_ref[k * X + n] for k in range(Z)])
        top = jnp.max(parts, axis=0)
        total = top + jnp.log2(jnp.sum(jnp.exp2(parts - top[None]), axis=0))
        factor = jnp.exp2(part_ref[z * X + n] - total)
        factor = jnp.concatenate([factor[0:1], factor[1:2]], axis=1)
        lanes = pl.ds(pl.multiple_of(n * QUARTER, QUARTER), QUARTER)
        for h in range(2):
            w = jnp.transpose(w_refs[by][:, pl.ds(h * 128, 128)].astype(F32)) * factor
            w_ref[pl.ds(h * 128, 128), lanes] = w.astype(BF16)


def scale(place, parts, blocks):
    return pl.pallas_call(
        scale_kernel,
        out_shape=(jax.ShapeDtypeStruct((ROWS, COUNT), BF16), jax.ShapeDtypeStruct((2 * X, 128), F32)),
        in_specs=[SMEM] + [VMEM] * (1 + X),
        out_specs=(VMEM,) * 2,
        compiler_params=params(16),
        name="scale",
    )(place, parts, *blocks)


def transport_kernel(pieces, place, w_ref, got_ref, data_ref, *out_refs):
    lhs = jnp.concatenate([w_ref[...], got_ref[...]], axis=1)
    for s, out_ref in zip(pieces, out_refs):
        y = at(place, 2, s, Y)
        rhs = []
        for core in (place[3], 1 - place[3]):
            for n in range(X):
                rhs.append(jnp.concatenate([data_ref[n, y, core, from_x(n, k)] for k in range(X)], axis=1))
        total = jnp.dot(lhs, jnp.concatenate(rhs, axis=0), preferred_element_type=F32)
        out_ref[...] = total.astype(out_ref.dtype)


def transport(place, w, got, data, pieces, hand_on):
    kinds = [jax.ShapeDtypeStruct((ROWS, SHARE), BF16 if s else F32) for s in pieces]
    if hand_on:
        kinds.append(jax.ShapeDtypeStruct(data.shape, data.dtype))
    return pl.pallas_call(
        functools.partial(transport_kernel, pieces),
        out_shape=kinds,
        in_specs=[SMEM] + [VMEM] * 3,
        out_specs=[VMEM] * len(kinds),
        input_output_aliases={3: len(pieces)} if hand_on else {},
        compiler_params=params(24),
        cost_estimate=pl.CostEstimate(
            flops=2 * ROWS * COUNT * C * SHARE * len(pieces), bytes_accessed=2 * 2**20 * len(pieces), transcendentals=0
        ),
        name="transport",
    )(place, w, got, data)


def body(noise, data):
    z, x, y, c = (lax.axis_index(a) for a in ("z", "x", "y", "core"))
    place = jnp.stack([z, x, y, c]).astype(jnp.int32)
    dealt = deal(place, data)
    swapped = jnp.stack([dealt[0]] + [shift(dealt[by], "x", by) for by in range(1, X)])
    noise_after, swapped = lax.optimization_barrier((noise, swapped))
    samples = lax.all_gather(swapped, ("z", "core")).reshape(Y, C, C, X, QUARTER, SLICE)
    samples, noise_all, sqn_mine = lax.optimization_barrier((samples, *collect(gather_noise(noise_after))))
    samples = pick(place, samples)
    data_all = lax.all_gather(samples, "x")
    got = shift(theirs(place, samples, noise_all, sqn_mine), "core", 1)
    mine, sq_mine = ours(place, samples, noise_all)
    q, rows, sq, sq_noise = score(mine, sq_mine, sqn_mine, got)
    for step in range(ITERS):
        if step:
            rows = noise_lse(q, columns)
        parts = lax.all_to_all(rows, ("x", "y", "core"), 0, 0)
        if step < ITERS - 1:
            columns, f = data_lse(q, parts)
            columns = lax.all_to_all(columns, "z", 0, 0)
    columns, f, *blocks = last_lse(place, q, parts, sq)
    blocks = [blocks[0]] + [shift(blocks[by], "x", by) for by in range(1, X)]
    columns = lax.all_to_all(columns, ("z", "x"), 0, 0)
    w, pot_g = scale(place, columns, blocks)
    data_all, pot_g = lax.optimization_barrier((data_all, pot_g))
    got = shift(w, "core", 1)
    opposite, data_all = transport(place, w, got, data_all, (2,), True)
    up, down, data_all = transport(place, w, got, data_all, (1, 3), True)
    (target,) = transport(place, w, got, data_all, (0,), False)
    for by, part in zip((2, 1, 3), (opposite, up, down)):
        target = target + shift(part, "y", by).astype(F32)
    velocity = (target - noise.astype(F32)).astype(BF16)
    own = lax.dynamic_index_in_dim(f.reshape(2, X, 128), x, 1, False)
    pot_f = (own * (EPS / LOG2E) + sq_noise / WIDTH).reshape(ROWS)
    return pot_f, pot_g.reshape(COUNT), velocity


def solution(mesh):
    fine = Mesh(mesh.devices.reshape(Z, X, Y, C), ("z", "x", "y", "core"))
    row, col = ("z", "x"), ("y", "core")
    return jax.shard_map(
        body,
        mesh=fine,
        in_specs=(P(row, col), P(col, row)),
        out_specs=(P(row), P(col), P(row, col)),
        check_vma=False,
    )
```
